256 devices in a mesh: seq: 8 (over z), chan: 8 (over x, core), dp: 4 (over y).
Axes of the slice: x: 4, y: 4, z: 8, core: 2. Of those that a mesh axis runs over, the one named last changes fastest.
Arguments:
- grad_out: bfloat16 [4, 64, 131072], P('dp', 'chan', 'seq'), may hold values from -6 to 6
- input_spectrum: float32 [4, 2, 64, 512, 512], P('dp', None, 'chan', 'seq'), may hold values from -6 to 6
- filter_spectrum: float32 [2, 64, 512, 512], P(None, 'chan', 'seq'), may hold values from -6 to 6
Outputs:
- input_grad: bfloat16 [4, 64, 131072], P('dp', 'chan', 'seq')
- filter_grad: float32 [64, 131072], P('chan', ('seq', 'dp'))
The draws below stay inside these ranges and needn't reach their ends.
All inputs are finite; a program needn't handle non-finite values.
Results may differ from the reference program's by a relative error of at most 0.001.
Values may be sent and summed in bfloat16 or wider, within the bound.
A program may use at most 128 MiB of HBM per device.

```python
import jax
import jax.numpy as jnp
from jax import lax

FCOLS = 512
SEQ = 131072
FROWS = 512
CHAN = 64
BATCH = 4


def shard_levels(key, shape, shards, smallest, top_value):
    def one(position, blocks):
        draws = jax.random.uniform(jax.random.fold_in(jax.random.fold_in(key, 6), position), (blocks,), jnp.float32, smallest / len(shards), top_value / len(shards))
        return jnp.repeat(jnp.exp(draws), shape[position] // blocks).reshape((-1,) + (1,) * (len(shape) - position - 1))

    level = one(*shards[0])
    for cut in shards[1:]:
        level = level * one(*cut)
    return level


def bell_draw(rng, shape, scale, reach, split=(), kind=jnp.bfloat16):
    drawn = scale * jax.random.normal(rng, shape, jnp.float32)
    if split:
        drawn = drawn * shard_levels(rng, shape, split, -0.22, 0.18)
    return jnp.clip(drawn, -reach, reach).astype(kind)


def setup_inputs(seed: int = 0) -> dict:
    splits = jax.random.split(jax.random.key(seed), 4)
    grad_out = bell_draw(splits[0], (BATCH, CHAN, SEQ), 1.0, 6.0, ((0, 4), (1, 8), (2, 8)))
    input_spectrum = bell_draw(splits[1], (BATCH, 2, CHAN, FROWS, FCOLS), 1.0, 6.0, ((0, 4), (2, 8), (3, 8)), jnp.float32)
    filter_spectrum = bell_draw(splits[2], (2, CHAN, FROWS, FCOLS), 1.0, 6.0, ((1, 8), (2, 8)), jnp.float32)
    return {"grad_out": grad_out, "input_spectrum": input_spectrum, "filter_spectrum": filter_spectrum}


def back_to_time(bin_table):
    flattened = jnp.swapaxes(bin_table, -1, -2).reshape(bin_table.shape[:-2] + (2 * SEQ,))
    return jnp.real(jnp.fft.ifft(flattened, axis=-1))[..., :SEQ]


def one_channel(operands):
    gradients, inputs, filters = operands
    spectrum = jnp.fft.fft(gradients.astype(jnp.float32), n=2 * SEQ, axis=-1)
    bin_table = jnp.swapaxes(spectrum.reshape(BATCH, FCOLS, FROWS), 1, 2)
    filter_bins = lax.complex(filters[0], filters[1])
    input_bins = lax.complex(inputs[:, 0], inputs[:, 1])
    input_part = bin_table * jnp.conj(filter_bins)[None]
    filter_part = jnp.sum(bin_table * jnp.conj(input_bins), axis=0)
    return back_to_time(input_part), back_to_time(filter_part)


def reference(grad_out, input_spectrum, filter_spectrum):
    operands = (jnp.transpose(grad_out, (1, 0, 2)), jnp.transpose(input_spectrum, (2, 0, 1, 3, 4)), jnp.transpose(filter_spectrum, (1, 0, 2, 3)))
    input_rows, filter_rows = lax.map(one_channel, operands)
    input_grad = jnp.transpose(input_rows, (1, 0, 2)).astype(jnp.bfloat16)
    return input_grad, filter_rows.astype(jnp.float32)
```

```python
import functools

import jax
import jax.numpy as jnp
import numpy as np
from jax import lax
from jax.experimental import pallas as pl
from jax.experimental.pallas import tpu as pltpu
from jax.sharding import PartitionSpec as P

MESH = pl.DeviceIdType.MESH
F32 = jnp.float32
BF16 = jnp.bfloat16

SHARDS = 8
BATCHES = 4
CH = 8
HALF = 4
ROWS = 64
COLS = 512
BINS = 512
TIMES = 32
MODULUS = BINS * COLS


def split_table(table):
    high = table.astype(np.float32).astype(jnp.bfloat16)
    low = (table - high.astype(np.float64)).astype(np.float32).astype(jnp.bfloat16)
    return high, low


@functools.cache
def tables():
    turn = 2.0 * np.pi
    angle = turn * (np.outer(np.arange(COLS), np.arange(COLS)) % COLS) / COLS
    cos_high, cos_low = split_table(np.cos(angle))
    sin_high, sin_low = split_table(np.sin(angle))
    wide = np.concatenate(
        [
            np.concatenate([cos_high, cos_high, cos_low], axis=0),
            np.concatenate([sin_high, sin_high, sin_low], axis=0),
        ],
        axis=1,
    )
    half = BINS // 2
    time_angle = turn * (np.outer(np.arange(BINS), np.arange(half)) % BINS) / BINS
    cos_t = np.cos(time_angle).reshape(SHARDS, ROWS, half)
    sin_t = np.sin(time_angle).reshape(SHARDS, ROWS, half)
    first = np.concatenate([cos_t, -sin_t], axis=1)
    first_high, first_low = split_table(first)
    first_table = np.concatenate([first_high, first_low], axis=1)
    last = np.concatenate([cos_t, -sin_t], axis=1).transpose(0, 2, 1) / MODULUS
    last_high, last_low = split_table(last)
    last_table = np.concatenate([last_high, last_high, last_low], axis=2)
    twist = turn * np.outer(np.arange(BINS), np.arange(COLS)) / MODULUS
    twist_table = np.stack(
        [np.cos(twist).reshape(SHARDS, ROWS, COLS), np.sin(twist).reshape(SHARDS, ROWS, COLS)],
        axis=1,
    ).astype(np.float32)
    return wide, first_table, last_table, twist_table


def split(value):
    high = value.astype(BF16)
    low = (value - high.astype(F32)).astype(BF16)
    return high, low


def kernel(
    x_ref, xs_hbm, hs_hbm, wide_hbm, first_hbm, last_hbm, twist_hbm,
    in_ref, fl_ref,
    wide, first, last, twist, xs, hs, xf, xg, z3, d3, pcs, u, part, recv, dh, dh_recv,
    u_f, part_f, recv_f, back, load_sem, ag_send, ag_recv, rs_send, rs_recv, y_send, y_recv,
    f_send, f_recv, b_send, b_recv,
):
    me = lax.axis_index("seq")
    batch = lax.axis_index("dp")

    def ring(offset):
        return lax.rem(me + (offset + SHARDS), SHARDS)

    def peer(offset):
        return lax.rem(batch + offset, BATCHES)

    barrier = pltpu.get_barrier_semaphore()
    for offset in (1, -1):
        pl.semaphore_signal(barrier, inc=1, device_id={"seq": ring(offset)}, device_id_type=MESH)
    for offset in (1, 2, 3):
        pl.semaphore_signal(barrier, inc=1, device_id={"dp": peer(offset)}, device_id_type=MESH)

    loads = [
        pltpu.make_async_copy(first_hbm.at[me], first, load_sem.at[0]),
        pltpu.make_async_copy(twist_hbm.at[me], twist, load_sem.at[1]),
        pltpu.make_async_copy(wide_hbm, wide, load_sem.at[2]),
        pltpu.make_async_copy(hs_hbm, hs, load_sem.at[3]),
        pltpu.make_async_copy(xs_hbm.at[0], xs, load_sem.at[4]),
        pltpu.make_async_copy(last_hbm.at[me], last, load_sem.at[5]),
    ]
    for load in loads:
        load.start()

    def spread(j, carry):
        for n in range(4):
            lanes = pl.ds(pl.multiple_of(j * COLS + n * 128, 128), 128)
            xf[n, pl.ds(j, CH, stride=TIMES), :] = x_ref[0, :, lanes].astype(F32)
        return carry

    lax.fori_loop(0, TIMES, spread, 0)
    mine = pl.multiple_of(me * TIMES, TIMES)
    for c in range(CH):
        for n in range(4):
            value = xf[n, c * TIMES : (c + 1) * TIMES, :].astype(BF16)
            xg[c, pl.ds(mine, TIMES), n * 128 : (n + 1) * 128] = value

    pl.semaphore_wait(barrier, 5)

    long_way = (-1, -1, 1, 1)

    def gather_copy(q, k, long):
        way = long_way[q] if long else -long_way[q]
        source = pl.multiple_of(ring(-way * k) * TIMES, TIMES)
        block = xg.at[pl.ds(2 * q, 2), pl.ds(source, TIMES), :]
        slot = k if long else 4 + k
        return pltpu.make_async_remote_copy(
            src_ref=block, dst_ref=block, send_sem=ag_send.at[q, slot], recv_sem=ag_recv.at[q, slot],
            device_id={"seq": ring(way)}, device_id_type=MESH,
        )

    def gather_start(q):
        gather_copy(q, 0, True).start()
        gather_copy(q, 0, False).start()

    def gather_step(q, k):
        gather_copy(q, k, True).wait_recv()
        if k < 3:
            gather_copy(q, k + 1, True).start()
            gather_copy(q, k, False).wait_recv()
            if k < 2:
                gather_copy(q, k + 1, False).start()

    def stage_a(h):
        def body(c, carry):
            t = jnp.dot(first[...], xg[HALF * h + c], preferred_element_type=F32)
            real = t[0:64] + t[128:192]
            imag = t[64:128] + t[192:256]
            tc, ts = twist[0], twist[1]
            for index, value in enumerate((real * tc + imag * ts, imag * tc - real * ts)):
                high, low = split(value)
                rows = pl.ds(pl.multiple_of(index * HALF * ROWS + c * ROWS, ROWS), ROWS)
                z3[rows, 0:512] = high
                z3[rows, 512:1024] = low
                z3[rows, 1024:1536] = high
            return carry

        lax.fori_loop(0, HALF, body, 0)

    def columns(operand, rows, tiles):
        def body(n, carry):
            lanes = pl.ds(pl.multiple_of(n * 256, 256), 256)
            pcs[0:rows, lanes] = jnp.dot(
                operand[0:rows, :], wide[:, lanes], preferred_element_type=F32
            )
            return carry

        lax.fori_loop(tiles[0], tiles[1], body, 0)

    def products(h):
        def body(c, carry):
            rr = pl.ds(pl.multiple_of(c * ROWS, ROWS), ROWS)
            ri = pl.ds(pl.multiple_of(HALF * ROWS + c * ROWS, ROWS), ROWS)
            gr = pcs[rr, 0:512] + pcs[ri, 512:1024]
            gi = pcs[ri, 0:512] - pcs[rr, 512:1024]
            hr, hi = hs[0, HALF * h + c], hs[1, HALF * h + c]
            for rows, value in ((rr, gr * hr + gi * hi), (ri, gi * hr - gr * hi)):
                high, low = split(value)
                d3[rows, 0:512] = high
                d3[rows, 512:1024] = low
                d3[rows, 1024:1536] = high
            xr, xi = xs[0, HALF * h + c], xs[1, HALF * h + c]
            dh[h, c, 0] = gr * xr + gi * xi
            dh[h, c, 1] = gi * xr - gr * xi
            return carry

        lax.fori_loop(0, HALF, body, 0)

    def untwist(count, dest):
        def body(c, carry):
            rr = pl.ds(pl.multiple_of(c * ROWS, ROWS), ROWS)
            ri = pl.ds(pl.multiple_of(count * ROWS + c * ROWS, ROWS), ROWS)
            vr = pcs[rr, 0:512] - pcs[ri, 512:1024]
            vi = pcs[ri, 0:512] + pcs[rr, 512:1024]
            tc, ts = twist[0], twist[1]
            for index, value in enumerate((vr * tc - vi * ts, vi * tc + vr * ts)):
                high, low = split(value)
                dest[c, 64 * index : 64 * index + 64, :] = high
                dest[c, 128 + 64 * index : 192 + 64 * index, :] = low
                dest[c, 256 + 64 * index : 320 + 64 * index, :] = high
            return carry

        lax.fori_loop(0, count, body, 0)

    def stage_e(count, source, dest, base):
        def body(c, carry):
            y = jnp.dot(last[...], source[c], preferred_element_type=F32)
            dest[:, base + c] = y.reshape(SHARDS, TIMES, COLS)
            return carry

        lax.fori_loop(0, count, body, 0)

    def reduce_copy(bufs, piece, way, k, long):
        part_ref, recv_ref, send, received = bufs
        q, first_c, n_c = piece
        direction = way if long else -way
        hops = 4 if long else 3
        slot = k if long else 4 + k
        return pltpu.make_async_remote_copy(
            src_ref=part_ref.at[ring(direction * (hops - k)), pl.ds(first_c, n_c)],
            dst_ref=recv_ref.at[slot, pl.ds(first_c, n_c)],
            send_sem=send.at[q, slot], recv_sem=received.at[q, slot],
            device_id={"seq": ring(direction)}, device_id_type=MESH,
        )

    def reduce_start(bufs, piece, way):
        reduce_copy(bufs, piece, way, 0, True).start()
        reduce_copy(bufs, piece, way, 0, False).start()

    def reduce_half(bufs, piece, way, k, long):
        part_ref, recv_ref, _, _ = bufs
        _, first_c, n_c = piece
        hops = 4 if long else 3
        direction = way if long else -way
        slot = k if long else 4 + k
        reduce_copy(bufs, piece, way, k, long).wait_recv()
        if k < hops - 1:
            dest = ring(direction * (hops - 1 - k))
            for c in range(first_c, first_c + n_c):
                part_ref[dest, c] += recv_ref[slot, c]
            reduce_copy(bufs, piece, way, k + 1, long).start()

    def reduce_step(bufs, piece, way, k):
        reduce_half(bufs, piece, way, k, True)
        if k < 3:
            reduce_half(bufs, piece, way, k, False)

    big = (part, recv, rs_send, rs_recv)
    small = (part_f, recv_f, f_send, f_recv)

    def batch_copy(h, o):
        return pltpu.make_async_remote_copy(
            src_ref=dh.at[h, peer(o)], dst_ref=dh_recv.at[h, o - 1],
            send_sem=y_send.at[h, o - 1], recv_sem=y_recv.at[h, o - 1],
            device_id={"dp": peer(o)}, device_id_type=MESH,
        )

    for q in (0, 1):
        gather_start(q)
    for k in range(3):
        for q in (0, 1):
            gather_step(q, k)
    for q in (2, 3):
        gather_start(q)
    for q in (0, 1):
        gather_step(q, 3)

    loads[0].wait()
    loads[1].wait()
    stage_a(0)
    for q in (2, 3):
        gather_step(q, 0)
    loads[2].wait()
    columns(z3, 512, (0, 4))
    for q in (2, 3):
        gather_step(q, 1)
    loads[3].wait()
    loads[4].wait()
    products(0)
    for o in (1, 2, 3):
        batch_copy(0, o).start()
    for q in (2, 3):
        gather_step(q, 2)
    columns(d3, 512, (0, 4))
    for q in (2, 3):
        gather_step(q, 3)
    untwist(HALF, u)
    loads[5].wait()
    stage_e(HALF, u, part, 0)
    pieces = [(q, 2 * q, 2) for q in range(4)]
    for q in (0, 1):
        reduce_start(big, pieces[q], long_way[q])
    stage_a(1)
    columns(z3, 512, (0, 4))
    for q in (0, 1):
        reduce_step(big, pieces[q], long_way[q], 0)
    products(1)
    for o in (1, 2, 3):
        batch_copy(1, o).start()
    columns(d3, 512, (0, 4))
    for q in (0, 1):
        reduce_step(big, pieces[q], long_way[q], 1)
    untwist(HALF, u)
    stage_e(HALF, u, part, HALF)
    for q in (2, 3):
        reduce_start(big, pieces[q], long_way[q])
    for q in (0, 1):
        reduce_step(big, pieces[q], long_way[q], 2)
    for q in (0, 1):
        reduce_step(big, pieces[q], long_way[q], 3)
    for q in (2, 3):
        reduce_step(big, pieces[q], long_way[q], 0)

    for h in range(2):
        for o in (1, 2, 3):
            batch_copy(h, o).wait_recv()
        for index in range(2):
            value = (dh[h, batch, index] + dh_recv[h, 0, index]) + (
                dh_recv[h, 1, index] + dh_recv[h, 2, index]
            )
            high, low = split(value)
            rows = slice(index * 128 + h * 64, index * 128 + h * 64 + 64)
            z3[rows, 0:512] = high
            z3[rows, 512:1024] = low
            z3[rows, 1024:1536] = high
    for q in (2, 3):
        reduce_step(big, pieces[q], long_way[q], 1)
    columns(z3, 256, (0, 4))
    untwist(2, u_f)
    stage_e(2, u_f, part_f, 0)
    small_pieces = [(0, 0, 1), (1, 1, 1)]
    small_way = (-1, 1)
    for q in (0, 1):
        reduce_start(small, small_pieces[q], small_way[q])
    for k in range(4):
        if k < 2:
            for q in (2, 3):
                reduce_step(big, pieces[q], long_way[q], 2 + k)
        for q in (0, 1):
            reduce_step(small, small_pieces[q], small_way[q], k)

    def back_copy(h, o):
        there = pl.multiple_of(peer(o) * 8, 8)
        return pltpu.make_async_remote_copy(
            src_ref=part_f.at[me, h, pl.ds(there, 8), :],
            dst_ref=back.at[pl.ds(pl.multiple_of((HALF * h + batch) * 8, 8), 8), :],
            send_sem=b_send.at[h, o - 1], recv_sem=b_recv.at[h, o - 1],
            device_id={"dp": peer(o)}, device_id_type=MESH,
        )

    for h in range(2):
        part_f[me, h] += recv_f[3, h] + recv_f[6, h]
        for o in (1, 2, 3):
            back_copy(h, o).start()
        here = pl.multiple_of(batch * 8, 8)
        back[pl.ds(pl.multiple_of((HALF * h + batch) * 8, 8), 8), :] = part_f[
            me, h, pl.ds(here, 8), :
        ]

    for c in range(CH):
        value = part[me, c] + (recv[3, c] + recv[6, c])
        for n in range(4):
            xf[n, c * TIMES : (c + 1) * TIMES, :] = value[:, n * 128 : (n + 1) * 128]

    def collect(j, carry):
        for n in range(4):
            lanes = pl.ds(pl.multiple_of(j * COLS + n * 128, 128), 128)
            in_ref[0, :, lanes] = xf[n, pl.ds(j, CH, stride=TIMES), :].astype(BF16)
        return carry

    lax.fori_loop(0, TIMES, collect, 0)

    for h in range(2):
        for o in (1, 2, 3):
            back_copy(h, o).wait_recv()
    for n in range(4):
        xf[n, 0:64, :] = back[:, n * 128 : (n + 1) * 128]
        for j in range(8):
            start = j * COLS + n * 128
            fl_ref[:, start : start + 128] = xf[n, pl.ds(j, CH, stride=8), :]

    for q in range(4):
        for k in range(4):
            gather_copy(q, k, True).wait_send()
            reduce_copy(big, pieces[q], long_way[q], k, True).wait_send()
            if k < 3:
                gather_copy(q, k, False).wait_send()
                reduce_copy(big, pieces[q], long_way[q], k, False).wait_send()
    for q in range(2):
        for k in range(4):
            reduce_copy(small, small_pieces[q], small_way[q], k, True).wait_send()
            if k < 3:
                reduce_copy(small, small_pieces[q], small_way[q], k, False).wait_send()
        for o in (1, 2, 3):
            batch_copy(q, o).wait_send()
            back_copy(q, o).wait_send()


def on_device(grad_out, input_spectrum, filter_spectrum):
    wide, first, last, twist = (jnp.asarray(t) for t in tables())
    vmem = pl.BlockSpec(memory_space=pltpu.VMEM)
    anywhere = pl.BlockSpec(memory_space=pl.ANY)
    dma = pltpu.SemaphoreType.DMA
    return pl.pallas_call(
        kernel,
        out_shape=(
            jax.ShapeDtypeStruct((1, CH, TIMES * COLS), BF16),
            jax.ShapeDtypeStruct((CH, TIMES * COLS // BATCHES), F32),
        ),
        in_specs=[vmem] + [anywhere] * 6,
        out_specs=(vmem, vmem),
        scratch_shapes=[
            pltpu.VMEM((1536, 1024), BF16),
            pltpu.VMEM((256, 256), BF16),
            pltpu.VMEM((256, 384), BF16),
            pltpu.VMEM((2, ROWS, COLS), F32),
            pltpu.VMEM((2, CH, ROWS, COLS), F32),
            pltpu.VMEM((2, CH, ROWS, COLS), F32),
            pltpu.VMEM((4, CH * TIMES, 128), F32),
            pltpu.VMEM((CH, SHARDS * TIMES, COLS), BF16),
            pltpu.VMEM((512, 1536), BF16),
            pltpu.VMEM((512, 1536), BF16),
            pltpu.VMEM((512, 1024), F32),
            pltpu.VMEM((HALF, 384, COLS), BF16),
            pltpu.VMEM((SHARDS, CH, TIMES, COLS), F32),
            pltpu.VMEM((7, CH, TIMES, COLS), F32),
            pltpu.VMEM((2, BATCHES, 2, ROWS, COLS), F32),
            pltpu.VMEM((2, 3, 2, ROWS, COLS), F32),
            pltpu.VMEM((2, 384, COLS), BF16),
            pltpu.VMEM((SHARDS, 2, TIMES, COLS), F32),
            pltpu.VMEM((7, 2, TIMES, COLS), F32),
            pltpu.VMEM((CH * 8, COLS), F32),
            dma((6,)),
            dma((4, 7)), dma((4, 7)),
            dma((4, 7)), dma((4, 7)),
            dma((2, 3)), dma((2, 3)),
            dma((2, 7)), dma((2, 7)),
            dma((2, 3)), dma((2, 3)),
        ],
        compiler_params=pltpu.CompilerParams(
            collective_id=0, has_side_effects=True, vmem_limit_bytes=56 * 1024 * 1024
        ),
    )(grad_out, input_spectrum, filter_spectrum, wide, first, last, twist)


def solution(mesh):
    in_specs = (
        P("dp", "chan", "seq"),
        P("dp", None, "chan", "seq", None),
        P(None, "chan", "seq", None),
    )
    out_specs = (P("dp", "chan", "seq"), P("chan", ("seq", "dp")))
    return jax.shard_map(
        on_device, mesh=mesh, in_specs=in_specs, out_specs=out_specs, check_vma=False
    )
```

```python
import functools

import jax
import jax.numpy as jnp
import numpy as np
from jax import lax
from jax.experimental import pallas as pl
from jax.experimental.pallas import tpu as pltpu
from jax.sharding import PartitionSpec as P

MESH = pl.DeviceIdType.MESH
F32 = jnp.float32
BF16 = jnp.bfloat16

SHARDS = 8
BATCHES = 4
CH = 8
HALF = 4
ROWS = 64
COLS = 512
BINS = 512
TIMES = 32
MODULUS = BINS * COLS


def split_table(table):
    high = table.astype(np.float32).astype(jnp.bfloat16)
    low = (table - high.astype(np.float64)).astype(np.float32).astype(jnp.bfloat16)
    return high, low


@functools.cache
def tables():
    turn = 2.0 * np.pi
    angle = turn * (np.outer(np.arange(COLS), np.arange(COLS)) % COLS) / COLS
    cos_high, cos_low = split_table(np.cos(angle))
    sin_high, sin_low = split_table(np.sin(angle))
    wide = np.concatenate(
        [
            np.concatenate([cos_high, cos_high, cos_low], axis=0),
            np.concatenate([sin_high, sin_high, sin_low], axis=0),
        ],
        axis=1,
    )
    half = BINS // 2
    time_angle = turn * (np.outer(np.arange(BINS), np.arange(half)) % BINS) / BINS
    cos_t = np.cos(time_angle).reshape(SHARDS, ROWS, half)
    sin_t = np.sin(time_angle).reshape(SHARDS, ROWS, half)
    first = np.concatenate([cos_t, -sin_t], axis=1)
    first_high, first_low = split_table(first)
    first_table = np.concatenate([first_high, first_low], axis=1)
    last = np.concatenate([cos_t, -sin_t], axis=1).transpose(0, 2, 1) / MODULUS
    last_high, last_low = split_table(last)
    last_table = np.concatenate([last_high, last_high, last_low], axis=2)
    twist = turn * np.outer(np.arange(BINS), np.arange(COLS)) / MODULUS
    twist_table = np.stack(
        [np.cos(twist).reshape(SHARDS, ROWS, COLS), np.sin(twist).reshape(SHARDS, ROWS, COLS)],
        axis=1,
    ).astype(np.float32)
    return wide, first_table, last_table, twist_table


SPAN = 124.0
GAIN = 2.0 ** (2.0 * SPAN / 32.0) - 1.0
FLOOR = 2.0 ** (-SPAN / 32.0)


def encode(values, put, put_top):
    top = jnp.abs(values[0])
    for value in values[1:]:
        top = jnp.maximum(top, jnp.abs(value))
    top = (jnp.maximum(top, 1e-30) * 1.01).astype(BF16)
    put_top(top)
    slope = (GAIN * FLOOR) / top.astype(F32)
    for index, value in enumerate(values):
        level = jnp.abs(value) * slope + FLOOR
        for _ in range(5):
            level = level * level
        put(index, jnp.where(value < 0.0, -level, level).astype(BF16))


def decode(codes, top):
    unit = top.astype(F32) * (1.0 / GAIN)
    slope = unit * (1.0 / FLOOR)
    values = []
    for code in codes:
        wide_code = code.astype(F32)
        level = jnp.exp2(jnp.log2(jnp.abs(wide_code)) * (1.0 / 32.0))
        value = level * slope - unit
        values.append(jnp.where(wide_code < 0.0, -value, value))
    return values


def split(value):
    high = value.astype(BF16)
    low = (value - high.astype(F32)).astype(BF16)
    return high, low


def kernel(
    x_ref, xs_hbm, hs_hbm, wide_hbm, first_hbm, last_hbm, twist_hbm,
    in_ref, fl_ref,
    wide, first, last, twist, xs, hs, xf, xg, z3, d3, pcs, u, part, recv, dh, dh_recv,
    u_f, part_f, recv_f, back, sent, sent_f, load_sem, ag_send, ag_recv, rs_send, rs_recv, y_send, y_recv,
    f_send, f_recv, b_send, b_recv,
):
    me = lax.axis_index("seq")
    batch = lax.axis_index("dp")

    def ring(offset):
        return lax.rem(me + (offset + SHARDS), SHARDS)

    def peer(offset):
        return lax.rem(batch + offset, BATCHES)

    barrier = pltpu.get_barrier_semaphore()
    for offset in (1, -1):
        pl.semaphore_signal(barrier, inc=1, device_id={"seq": ring(offset)}, device_id_type=MESH)
    for offset in (1, 2, 3):
        pl.semaphore_signal(barrier, inc=1, device_id={"dp": peer(offset)}, device_id_type=MESH)

    loads = [
        pltpu.make_async_copy(first_hbm.at[me], first, load_sem.at[0]),
        pltpu.make_async_copy(twist_hbm.at[me], twist, load_sem.at[1]),
        pltpu.make_async_copy(wide_hbm, wide, load_sem.at[2]),
        pltpu.make_async_copy(hs_hbm, hs, load_sem.at[3]),
        pltpu.make_async_copy(xs_hbm.at[0], xs, load_sem.at[4]),
        pltpu.make_async_copy(last_hbm.at[me], last, load_sem.at[5]),
    ]
    for load in loads:
        load.start()

    def spread(j, carry):
        for n in range(4):
            lanes = pl.ds(pl.multiple_of(j * COLS + n * 128, 128), 128)
            xf[n, pl.ds(j, CH, stride=TIMES), :] = x_ref[0, :, lanes].astype(F32)
        return carry

    lax.fori_loop(0, TIMES, spread, 0)
    mine = pl.multiple_of(me * TIMES, TIMES)
    for c in range(CH):
        for n in range(4):
            value = xf[n, c * TIMES : (c + 1) * TIMES, :].astype(BF16)
            xg[c, pl.ds(mine, TIMES), n * 128 : (n + 1) * 128] = value

    pl.semaphore_wait(barrier, 5)

    long_way = (-1, 1, -1, 1)

    def gather_copy(q, k, long):
        way = long_way[q] if long else -long_way[q]
        source = pl.multiple_of(ring(-way * k) * TIMES, TIMES)
        block = xg.at[pl.ds(2 * q, 2), pl.ds(source, TIMES), :]
        slot = k if long else 4 + k
        return pltpu.make_async_remote_copy(
            src_ref=block, dst_ref=block, send_sem=ag_send.at[q, slot], recv_sem=ag_recv.at[q, slot],
            device_id={"seq": ring(way)}, device_id_type=MESH,
        )

    def gather_start(q):
        gather_copy(q, 0, True).start()
        gather_copy(q, 0, False).start()

    def gather_step(q, k):
        gather_copy(q, k, True).wait_recv()
        if k < 3:
            gather_copy(q, k + 1, True).start()
            gather_copy(q, k, False).wait_recv()
            if k < 2:
                gather_copy(q, k + 1, False).start()

    def stage_a(h, lo, hi):
        def body(c, carry):
            t = jnp.dot(first[...], xg[HALF * h + c], preferred_element_type=F32)
            real = t[0:64] + t[128:192]
            imag = t[64:128] + t[192:256]
            tc, ts = twist[0], twist[1]
            for index, value in enumerate((real * tc + imag * ts, imag * tc - real * ts)):
                high, low = split(value)
                rows = pl.ds(pl.multiple_of(index * HALF * ROWS + c * ROWS, ROWS), ROWS)
                z3[rows, 0:512] = high
                z3[rows, 512:1024] = low
                z3[rows, 1024:1536] = high
            return carry

        lax.fori_loop(lo, hi, body, 0)

    def columns(operand, rows, lo, hi):
        def body(n, carry):
            lanes = pl.ds(pl.multiple_of(n * 256, 256), 256)
            pcs[0:rows, lanes] = jnp.dot(
                operand[0:rows, :], wide[:, lanes], preferred_element_type=F32
            )
            return carry

        lax.fori_loop(lo, hi, body, 0)

    def products(h, lo, hi):
        def body(c, carry):
            rr = pl.ds(pl.multiple_of(c * ROWS, ROWS), ROWS)
            ri = pl.ds(pl.multiple_of(HALF * ROWS + c * ROWS, ROWS), ROWS)
            gr = pcs[rr, 0:512] + pcs[ri, 512:1024]
            gi = pcs[ri, 0:512] - pcs[rr, 512:1024]
            hr, hi = hs[0, HALF * h + c], hs[1, HALF * h + c]
            for rows, value in ((rr, gr * hr + gi * hi), (ri, gi * hr - gr * hi)):
                high, low = split(value)
                d3[rows, 0:512] = high
                d3[rows, 512:1024] = low
                d3[rows, 1024:1536] = high
            xr, xi = xs[0, HALF * h + c], xs[1, HALF * h + c]
            dh[h, c, 0] = gr * xr + gi * xi
            dh[h, c, 1] = gi * xr - gr * xi
            return carry

        lax.fori_loop(lo, hi, body, 0)

    def untwist(count, dest, lo, hi):
        def body(c, carry):
            rr = pl.ds(pl.multiple_of(c * ROWS, ROWS), ROWS)
            ri = pl.ds(pl.multiple_of(count * ROWS + c * ROWS, ROWS), ROWS)
            vr = pcs[rr, 0:512] - pcs[ri, 512:1024]
            vi = pcs[ri, 0:512] + pcs[rr, 512:1024]
            tc, ts = twist[0], twist[1]
            for index, value in enumerate((vr * tc - vi * ts, vi * tc + vr * ts)):
                high, low = split(value)
                dest[c, 64 * index : 64 * index + 64, :] = high
                dest[c, 128 + 64 * index : 192 + 64 * index, :] = low
                dest[c, 256 + 64 * index : 320 + 64 * index, :] = high
            return carry

        lax.fori_loop(lo, hi, body, 0)

    def stage_e(source, dest, base, lo, hi):
        def body(c, carry):
            y = jnp.dot(last[...], source[c], preferred_element_type=F32)
            dest[:, base + c] = y.reshape(SHARDS, TIMES, COLS)
            return carry

        lax.fori_loop(lo, hi, body, 0)

    def reduce_copy(bufs, q, way, k, long):
        _, sent_ref, recv_ref, send, received, _ = bufs
        slot = k if long else 4 + k
        return pltpu.make_async_remote_copy(
            src_ref=sent_ref.at[q, slot], dst_ref=recv_ref.at[q, slot],
            send_sem=send.at[q, slot], recv_sem=received.at[q, slot],
            device_id={"seq": ring(way if long else -way)}, device_id_type=MESH,
        )

    def blocks(bufs, q):
        n_c = bufs[5]
        return [
            (n_c * q + c, pl.ds(16 * r, 16), pl.ds(128 * n, 128))
            for c in range(n_c)
            for r in range(TIMES // 16)
            for n in range(COLS // 128)
        ]

    def arrived(bufs, q, slot):
        recv_ref = bufs[2]
        count = len(blocks(bufs, q))
        return decode([recv_ref[q, slot, b] for b in range(count)], recv_ref[q, slot, count])

    def reduce_send(bufs, q, way, k, long, values):
        sent_ref = bufs[1]
        slot = k if long else 4 + k

        def put(index, code):
            sent_ref[q, slot, index] = code

        def put_top(top):
            sent_ref[q, slot, len(values)] = top

        encode(values, put, put_top)
        reduce_copy(bufs, q, way, k, long).start()

    def reduce_hop(bufs, q, way, k, long):
        part_ref = bufs[0]
        hops = 4 if long else 3
        slot = k if long else 4 + k
        dest = ring((way if long else -way) * (hops - 1 - k))
        if k >= 0:
            reduce_copy(bufs, q, way, k, long).wait_recv()
        if k == hops - 1:
            return
        values = [part_ref[dest, c, rows, lanes] for c, rows, lanes in blocks(bufs, q)]
        if k >= 0:
            values = [a + b for a, b in zip(values, arrived(bufs, q, slot))]
        reduce_send(bufs, q, way, k + 1, long, values)

    def reduce_start(bufs, q, way):
        reduce_hop(bufs, q, way, -1, True)
        reduce_hop(bufs, q, way, -1, False)

    def reduce_step(bufs, q, way, k):
        reduce_hop(bufs, q, way, k, True)
        if k < 3:
            reduce_hop(bufs, q, way, k, False)

    def reduce_end(bufs, q):
        part_ref = bufs[0]
        return [
            (c, rows, lanes, part_ref[me, c, rows, lanes] + (a + b))
            for (c, rows, lanes), a, b in zip(
                blocks(bufs, q), arrived(bufs, q, 3), arrived(bufs, q, 6)
            )
        ]

    big = (part, sent, recv, rs_send, rs_recv, 2)
    small = (part_f, sent_f, recv_f, f_send, f_recv, 1)
    small_way = (-1, 1)

    def batch_copy(h, o):
        return pltpu.make_async_remote_copy(
            src_ref=dh.at[h, peer(o)], dst_ref=dh_recv.at[h, o - 1],
            send_sem=y_send.at[h, o - 1], recv_sem=y_recv.at[h, o - 1],
            device_id={"dp": peer(o)}, device_id_type=MESH,
        )

    def half_parts(h):
        def start_pieces(q):
            reduce_start(big, q, long_way[q])

        def batch_starts():
            for o in (1, 2, 3):
                batch_copy(h, o).start()

        def wait(index):
            if h == 0:
                loads[index].wait()

        return [
            lambda: (wait(0), wait(1), stage_a(h, 0, 2)),
            lambda: stage_a(h, 2, 4),
            lambda: (wait(2), columns(z3, 512, 0, 2)),
            lambda: columns(z3, 512, 2, 4),
            lambda: (wait(3), wait(4), products(h, 0, 2)),
            lambda: (products(h, 2, 4), batch_starts()),
            lambda: columns(d3, 512, 0, 2),
            lambda: columns(d3, 512, 2, 4),
            lambda: untwist(HALF, u, 0, 2),
            lambda: untwist(HALF, u, 2, 4),
            lambda: (wait(5), stage_e(u, part, HALF * h, 0, 2), start_pieces(2 * h)),
            lambda: (stage_e(u, part, HALF * h, 2, 4), start_pieces(2 * h + 1)),
        ]

    def weave(parts, services):
        done = 0
        for index, part_of in enumerate(parts):
            part_of()
            while done * len(parts) < (index + 1) * len(services):
                services[done]()
                done += 1

    def gather_services(pieces):
        return [functools.partial(gather_step, q, k) for k in range(4) for q in pieces]

    def reduce_services(bufs, pieces, ways, first=0):
        return [
            functools.partial(reduce_step, bufs, q, ways[q], k)
            for k in range(first, 4)
            for q in pieces
        ]

    for q in (0, 1):
        gather_start(q)
    for k in range(3):
        for q in (0, 1):
            gather_step(q, k)
    for q in (2, 3):
        gather_start(q)
    for q in (0, 1):
        gather_step(q, 3)
    weave(half_parts(0), gather_services((2, 3)))
    weave(half_parts(1), reduce_services(big, (0, 1), long_way))

    def batch_sum(h):
        for o in (1, 2, 3):
            batch_copy(h, o).wait_recv()
        for index in range(2):
            value = (dh[h, batch, index] + dh_recv[h, 0, index]) + (
                dh_recv[h, 1, index] + dh_recv[h, 2, index]
            )
            high, low = split(value)
            rows = slice(index * 128 + h * 64, index * 128 + h * 64 + 64)
            z3[rows, 0:512] = high
            z3[rows, 512:1024] = low
            z3[rows, 1024:1536] = high

    filter_parts = [
        lambda: batch_sum(0),
        lambda: batch_sum(1),
        lambda: columns(z3, 256, 0, 4),
        lambda: (
            untwist(2, u_f, 0, 2),
            stage_e(u_f, part_f, 0, 0, 2),
            reduce_start(small, 0, small_way[0]),
            reduce_start(small, 1, small_way[1]),
        ),
    ]
    services = reduce_services(big, (2, 3), long_way)
    weave(filter_parts, services[:4])
    small_services = reduce_services(small, (0, 1), small_way)
    for index in range(4):
        services[4 + index]()
        small_services[index]()
    for service in small_services[4:]:
        service()

    def back_copy(h, o):
        there = pl.multiple_of(peer(o) * 8, 8)
        return pltpu.make_async_remote_copy(
            src_ref=part_f.at[me, h, pl.ds(there, 8), :],
            dst_ref=back.at[pl.ds(pl.multiple_of((HALF * h + batch) * 8, 8), 8), :],
            send_sem=b_send.at[h, o - 1], recv_sem=b_recv.at[h, o - 1],
            device_id={"dp": peer(o)}, device_id_type=MESH,
        )

    for h in range(2):
        for c, rows, lanes, value in reduce_end(small, h):
            part_f[me, c, rows, lanes] = value
        for o in (1, 2, 3):
            back_copy(h, o).start()
        here = pl.multiple_of(batch * 8, 8)
        back[pl.ds(pl.multiple_of((HALF * h + batch) * 8, 8), 8), :] = part_f[
            me, h, pl.ds(here, 8), :
        ]

    for q in range(4):
        for c, rows, lanes, value in reduce_end(big, q):
            xf[lanes.start // 128, c * TIMES + rows.start : c * TIMES + rows.start + 16, :] = value

    def collect(j, carry):
        for n in range(4):
            lanes = pl.ds(pl.multiple_of(j * COLS + n * 128, 128), 128)
            in_ref[0, :, lanes] = xf[n, pl.ds(j, CH, stride=TIMES), :].astype(BF16)
        return carry

    lax.fori_loop(0, TIMES, collect, 0)

    for h in range(2):
        for o in (1, 2, 3):
            back_copy(h, o).wait_recv()
    for n in range(4):
        xf[n, 0:64, :] = back[:, n * 128 : (n + 1) * 128]
        for j in range(8):
            start = j * COLS + n * 128
            fl_ref[:, start : start + 128] = xf[n, pl.ds(j, CH, stride=8), :]

    for q in range(4):
        for k in range(4):
            gather_copy(q, k, True).wait_send()
            reduce_copy(big, q, long_way[q], k, True).wait_send()
            if k < 3:
                gather_copy(q, k, False).wait_send()
                reduce_copy(big, q, long_way[q], k, False).wait_send()
    for q in range(2):
        for k in range(4):
            reduce_copy(small, q, small_way[q], k, True).wait_send()
            if k < 3:
                reduce_copy(small, q, small_way[q], k, False).wait_send()
        for o in (1, 2, 3):
            batch_copy(q, o).wait_send()
            back_copy(q, o).wait_send()


def on_device(grad_out, input_spectrum, filter_spectrum):
    wide, first, last, twist = (jnp.asarray(t) for t in tables())
    vmem = pl.BlockSpec(memory_space=pltpu.VMEM)
    anywhere = pl.BlockSpec(memory_space=pl.ANY)
    dma = pltpu.SemaphoreType.DMA
    return pl.pallas_call(
        kernel,
        out_shape=(
            jax.ShapeDtypeStruct((1, CH, TIMES * COLS), BF16),
            jax.ShapeDtypeStruct((CH, TIMES * COLS // BATCHES), F32),
        ),
        in_specs=[vmem] + [anywhere] * 6,
        out_specs=(vmem, vmem),
        scratch_shapes=[
            pltpu.VMEM((1536, 1024), BF16),
            pltpu.VMEM((256, 256), BF16),
            pltpu.VMEM((256, 384), BF16),
            pltpu.VMEM((2, ROWS, COLS), F32),
            pltpu.VMEM((2, CH, ROWS, COLS), F32),
            pltpu.VMEM((2, CH, ROWS, COLS), F32),
            pltpu.VMEM((4, CH * TIMES, 128), F32),
            pltpu.VMEM((CH, SHARDS * TIMES, COLS), BF16),
            pltpu.VMEM((512, 1536), BF16),
            pltpu.VMEM((512, 1536), BF16),
            pltpu.VMEM((512, 1024), F32),
            pltpu.VMEM((HALF, 384, COLS), BF16),
            pltpu.VMEM((SHARDS, CH, TIMES, COLS), F32),
            pltpu.VMEM((4, 7, 17, 16, 128), BF16),
            pltpu.VMEM((2, BATCHES, 2, ROWS, COLS), F32),
            pltpu.VMEM((2, 3, 2, ROWS, COLS), F32),
            pltpu.VMEM((2, 384, COLS), BF16),
            pltpu.VMEM((SHARDS, 2, TIMES, COLS), F32),
            pltpu.VMEM((2, 7, 9, 16, 128), BF16),
            pltpu.VMEM((CH * 8, COLS), F32),
            pltpu.VMEM((4, 7, 17, 16, 128), BF16),
            pltpu.VMEM((2, 7, 9, 16, 128), BF16),
            dma((6,)),
            dma((4, 7)), dma((4, 7)),
            dma((4, 7)), dma((4, 7)),
            dma((2, 3)), dma((2, 3)),
            dma((2, 7)), dma((2, 7)),
            dma((2, 3)), dma((2, 3)),
        ],
        compiler_params=pltpu.CompilerParams(
            collective_id=0, has_side_effects=True, vmem_limit_bytes=56 * 1024 * 1024
        ),
    )(grad_out, input_spectrum, filter_spectrum, wide, first, last, twist)


def solution(mesh):
    in_specs = (
        P("dp", "chan", "seq"),
        P("dp", None, "chan", "seq", None),
        P(None, "chan", "seq", None),
    )
    out_specs = (P("dp", "chan", "seq"), P("chan", ("seq", "dp")))
    return jax.shard_map(
        on_device, mesh=mesh, in_specs=in_specs, out_specs=out_specs, check_vma=False
    )
```

```python
import functools

import jax
import jax.numpy as jnp
import numpy as np
from jax import lax
from jax.experimental import pallas as pl
from jax.experimental.pallas import tpu as pltpu
from jax.sharding import PartitionSpec as P

MESH = pl.DeviceIdType.MESH
F32 = jnp.float32
BF16 = jnp.bfloat16

SHARDS = 8
BATCHES = 4
CH = 8
HALF = 4
ROWS = 64
COLS = 512
BINS = 512
TIMES = 32
MODULUS = BINS * COLS
LANES = 128


def split_table(table):
    high = table.astype(np.float32).astype(jnp.bfloat16)
    low = (table - high.astype(np.float64)).astype(np.float32).astype(jnp.bfloat16)
    return high, low


@functools.cache
def tables():
    turn = 2.0 * np.pi
    fold = np.arange(LANES)
    forward, inverse = [], []
    for a in range(4):
        angle = turn * (np.outer(4 * fold + a, fold) % COLS) / COLS
        c, s = np.cos(angle), np.sin(angle)
        for group, block in (
            (forward, np.block([[c, -s], [s, c]])),
            (inverse, np.block([[c.T, s.T], [-s.T, c.T]])),
        ):
            high, low = split_table(block)
            group.append(np.concatenate([high, high, low], axis=0))
    wide = np.stack(forward + inverse)
    place = np.arange(COLS)
    order = 4 * (place % LANES) + place // LANES
    shuffle = np.zeros((COLS, COLS), np.float32)
    shuffle[order, place] = 1.0
    shuffle = np.stack([shuffle, shuffle.T]).astype(jnp.bfloat16)
    half = BINS // 2
    time_angle = turn * (np.outer(np.arange(BINS), np.arange(half)) % BINS) / BINS
    cos_t = np.cos(time_angle).reshape(SHARDS, ROWS, half)
    sin_t = np.sin(time_angle).reshape(SHARDS, ROWS, half)
    first = np.concatenate([cos_t, -sin_t], axis=1)
    first_high, first_low = split_table(first)
    first_table = np.concatenate([first_high, first_low], axis=1)
    last = np.concatenate([cos_t, -sin_t], axis=1).transpose(0, 2, 1) / MODULUS
    last_high, last_low = split_table(last)
    last_table = np.concatenate([last_high, last_high, last_low], axis=2)
    twist = turn * np.outer(np.arange(BINS), np.arange(COLS)) / MODULUS
    twist_table = np.stack(
        [np.cos(twist).reshape(SHARDS, ROWS, COLS), np.sin(twist).reshape(SHARDS, ROWS, COLS)],
        axis=1,
    ).astype(np.float32)[..., order]
    return wide, first_table, last_table, twist_table, shuffle


SPAN = 124.0
GAIN = 2.0 ** (2.0 * SPAN / 32.0) - 1.0
FLOOR = 2.0 ** (-SPAN / 32.0)


def encode(values, put, put_top):
    top = jnp.abs(values[0])
    for value in values[1:]:
        top = jnp.maximum(top, jnp.abs(value))
    top = (jnp.maximum(top, 1e-30) * 1.01).astype(BF16)
    put_top(top)
    slope = (GAIN * FLOOR) / top.astype(F32)
    for index, value in enumerate(values):
        level = jnp.abs(value) * slope + FLOOR
        for _ in range(5):
            level = level * level
        put(index, jnp.where(value < 0.0, -level, level).astype(BF16))


def decode(codes, top):
    unit = top.astype(F32) * (1.0 / GAIN)
    slope = unit * (1.0 / FLOOR)
    values = []
    for code in codes:
        wide_code = code.astype(F32)
        level = jnp.exp2(jnp.log2(jnp.abs(wide_code)) * (1.0 / 32.0))
        value = level * slope - unit
        values.append(jnp.where(wide_code < 0.0, -value, value))
    return values


def split(value):
    high = value.astype(BF16)
    low = (value - high.astype(F32)).astype(BF16)
    return high, low


def kernel(
    x_ref, xs_hbm, hs_hbm, wide_hbm, first_hbm, last_hbm, twist_hbm, shuffle_hbm,
    in_ref, fl_ref,
    wide, first, last, twist, shuffle, xs, hs, xf, xg, zb, yb, u, part, recv, dh, dh_sent, dh_recv,
    zf, yf, u_f, part_f, recv_f, back, sent, sent_f, load_sem, ag_send, ag_recv, rs_send, rs_recv, y_send, y_recv,
    f_send, f_recv, b_send, b_recv,
):
    me = lax.axis_index("seq")
    batch = lax.axis_index("dp")

    def ring(offset):
        return lax.rem(me + (offset + SHARDS), SHARDS)

    def peer(offset):
        return lax.rem(batch + offset, BATCHES)

    barrier = pltpu.get_barrier_semaphore()
    for offset in (1, -1):
        pl.semaphore_signal(barrier, inc=1, device_id={"seq": ring(offset)}, device_id_type=MESH)
    for offset in (1, 2, 3):
        pl.semaphore_signal(barrier, inc=1, device_id={"dp": peer(offset)}, device_id_type=MESH)

    loads = [
        pltpu.make_async_copy(first_hbm.at[me], first, load_sem.at[0]),
        pltpu.make_async_copy(twist_hbm.at[me], twist, load_sem.at[1]),
        pltpu.make_async_copy(wide_hbm, wide, load_sem.at[2]),
        pltpu.make_async_copy(hs_hbm, hs, load_sem.at[3]),
        pltpu.make_async_copy(xs_hbm.at[0], xs, load_sem.at[4]),
        pltpu.make_async_copy(last_hbm.at[me], last, load_sem.at[5]),
        pltpu.make_async_copy(shuffle_hbm, shuffle, load_sem.at[6]),
    ]
    for index in (6, 0, 1, 2, 3, 4, 5):
        loads[index].start()

    def spread(j, carry):
        for n in range(4):
            lanes = pl.ds(pl.multiple_of(j * COLS + n * 128, 128), 128)
            xf[n, pl.ds(j, CH, stride=TIMES), :] = x_ref[0, :, lanes].astype(F32)
        return carry

    lax.fori_loop(0, TIMES, spread, 0)
    mine = pl.multiple_of(me * TIMES, TIMES)
    loads[6].wait()
    rows = jnp.concatenate([xf[n].astype(BF16) for n in range(4)], axis=1)
    rows = jnp.dot(rows, shuffle[0], preferred_element_type=F32).astype(BF16)
    for c in range(CH):
        xg[c, pl.ds(mine, TIMES), :] = rows[c * TIMES : (c + 1) * TIMES, :]

    pl.semaphore_wait(barrier, 5)

    long_way = (-1, 1, -1, 1)

    def gather_copy(q, k, long):
        way = long_way[q] if long else -long_way[q]
        source = pl.multiple_of(ring(-way * k) * TIMES, TIMES)
        block = xg.at[pl.ds(2 * q, 2), pl.ds(source, TIMES), :]
        slot = k if long else 4 + k
        return pltpu.make_async_remote_copy(
            src_ref=block, dst_ref=block, send_sem=ag_send.at[q, slot], recv_sem=ag_recv.at[q, slot],
            device_id={"seq": ring(way)}, device_id_type=MESH,
        )

    def gather_start(q):
        gather_copy(q, 0, True).start()
        gather_copy(q, 0, False).start()

    def gather_step(q, k):
        gather_copy(q, k, True).wait_recv()
        if k < 3:
            gather_copy(q, k + 1, True).start()
            gather_copy(q, k, False).wait_recv()
            if k < 2:
                gather_copy(q, k + 1, False).start()

    def put_split(dest, a, rows, real, imag):
        for index, value in enumerate((real, imag)):
            high, low = split(value)
            for place, item in ((0, high), (2, low), (4, high)):
                lane = (place + index) * LANES
                dest[a, rows, lane : lane + LANES] = item

    def stage_a(h, lo, hi):
        def body(c, carry):
            t = jnp.dot(first[...], xg[HALF * h + c], preferred_element_type=F32)
            real = t[0:64] + t[128:192]
            imag = t[64:128] + t[192:256]
            rows = pl.ds(pl.multiple_of(c * ROWS, ROWS), ROWS)
            for a in range(4):
                lanes = slice(a * LANES, (a + 1) * LANES)
                tc, ts = twist[0, :, lanes], twist[1, :, lanes]
                ar, ai = real[:, lanes], imag[:, lanes]
                put_split(zb, a, rows, ar * tc + ai * ts, ai * tc - ar * ts)
            return carry

        lax.fori_loop(lo, hi, body, 0)

    def columns(source, dest, inverse):
        def body(a, carry):
            weight = wide[a + 4] if inverse else wide[a]
            dest[a] = jnp.dot(source[a], weight, preferred_element_type=F32)
            return carry

        lax.fori_loop(0, 4, body, 0)

    def quarters(values, forward):
        (r0, i0), (r1, i1), (r2, i2), (r3, i3) = values
        sr, si, dr, di = r0 + r2, i0 + i2, r0 - r2, i0 - i2
        tr, ti, er, ei = r1 + r3, i1 + i3, r1 - r3, i1 - i3
        left = (dr + ei, di - er)
        right = (dr - ei, di + er)
        if not forward:
            left, right = right, left
        return [(sr + tr, si + ti), left, (sr - tr, si - ti), right]

    def products(h, lo, hi):
        def body(c, carry):
            rows = pl.ds(pl.multiple_of(c * ROWS, ROWS), ROWS)
            bins = quarters(
                [(yb[a, rows, 0:LANES], yb[a, rows, LANES : 2 * LANES]) for a in range(4)], True
            )
            channel = HALF * h + c
            inner = []
            for e, (gr, gi) in enumerate(bins):
                lanes = slice(e * LANES, (e + 1) * LANES)
                hr, hi_ = hs[0, channel, :, lanes], hs[1, channel, :, lanes]
                inner.append((gr * hr + gi * hi_, gi * hr - gr * hi_))
                xr, xi = xs[0, channel, :, lanes], xs[1, channel, :, lanes]
                dh[h, c, 0, :, lanes] = gr * xr + gi * xi
                dh[h, c, 1, :, lanes] = gi * xr - gr * xi
            for a, (real, imag) in enumerate(quarters(inner, False)):
                put_split(zb, a, rows, real, imag)
            return carry

        lax.fori_loop(lo, hi, body, 0)

    def untwist(source, dest, lo, hi):
        def body(c, carry):
            rows = pl.ds(pl.multiple_of(c * ROWS, ROWS), ROWS)
            for a in range(4):
                lanes = slice(a * LANES, (a + 1) * LANES)
                vr, vi = source[a, rows, 0:LANES], source[a, rows, LANES : 2 * LANES]
                tc, ts = twist[0, :, lanes], twist[1, :, lanes]
                for index, value in enumerate((vr * tc - vi * ts, vi * tc + vr * ts)):
                    high, low = split(value)
                    dest[c, 64 * index : 64 * index + 64, lanes] = high
                    dest[c, 128 + 64 * index : 192 + 64 * index, lanes] = low
                    dest[c, 256 + 64 * index : 320 + 64 * index, lanes] = high
            return carry

        lax.fori_loop(lo, hi, body, 0)

    def stage_e(source, dest, base, lo, hi):
        def body(c, carry):
            y = jnp.dot(last[...], source[c], preferred_element_type=F32)
            dest[:, base + c] = y.reshape(SHARDS, TIMES, COLS)
            return carry

        lax.fori_loop(lo, hi, body, 0)

    def reduce_copy(bufs, q, way, k, long):
        _, sent_ref, recv_ref, send, received, _ = bufs
        slot = k if long else 4 + k
        return pltpu.make_async_remote_copy(
            src_ref=sent_ref.at[q, slot], dst_ref=recv_ref.at[q, slot],
            send_sem=send.at[q, slot], recv_sem=received.at[q, slot],
            device_id={"seq": ring(way if long else -way)}, device_id_type=MESH,
        )

    def blocks(bufs, q):
        n_c = bufs[5]
        return [
            (n_c * q + c, pl.ds(16 * r, 16), pl.ds(128 * n, 128))
            for c in range(n_c)
            for r in range(TIMES // 16)
            for n in range(COLS // 128)
        ]

    def arrived(bufs, q, slot):
        recv_ref = bufs[2]
        count = len(blocks(bufs, q))
        return decode([recv_ref[q, slot, b] for b in range(count)], recv_ref[q, slot, count])

    def reduce_send(bufs, q, way, k, long, values):
        sent_ref = bufs[1]
        slot = k if long else 4 + k

        def put(index, code):
            sent_ref[q, slot, index] = code

        def put_top(top):
            sent_ref[q, slot, len(values)] = top

        encode(values, put, put_top)
        reduce_copy(bufs, q, way, k, long).start()

    def reduce_hop(bufs, q, way, k, long):
        part_ref = bufs[0]
        hops = 4 if long else 3
        slot = k if long else 4 + k
        dest = ring((way if long else -way) * (hops - 1 - k))
        if k >= 0:
            reduce_copy(bufs, q, way, k, long).wait_recv()
        if k == hops - 1:
            return
        values = [part_ref[dest, c, rows, lanes] for c, rows, lanes in blocks(bufs, q)]
        if k >= 0:
            values = [a + b for a, b in zip(values, arrived(bufs, q, slot))]
        reduce_send(bufs, q, way, k + 1, long, values)

    def reduce_start(bufs, q, way):
        reduce_hop(bufs, q, way, -1, True)
        reduce_hop(bufs, q, way, -1, False)

    def reduce_step(bufs, q, way, k):
        reduce_hop(bufs, q, way, k, True)
        if k < 3:
            reduce_hop(bufs, q, way, k, False)

    def reduce_end(bufs, q):
        part_ref = bufs[0]
        return [
            (c, rows, lanes, part_ref[me, c, rows, lanes] + (a + b))
            for (c, rows, lanes), a, b in zip(
                blocks(bufs, q), arrived(bufs, q, 3), arrived(bufs, q, 6)
            )
        ]

    big = (part, sent, recv, rs_send, rs_recv, 2)
    small = (part_f, sent_f, recv_f, f_send, f_recv, 1)
    small_way = (-1, 1)

    def batch_copy(h, o):
        return pltpu.make_async_remote_copy(
            src_ref=dh_sent.at[h, o - 1], dst_ref=dh_recv.at[h, o - 1],
            send_sem=y_send.at[h, o - 1], recv_sem=y_recv.at[h, o - 1],
            device_id={"dp": peer(o)}, device_id_type=MESH,
        )

    tiles = [(pl.ds(16 * r, 16), pl.ds(128 * n, 128)) for r in range(ROWS // 16) for n in range(4)]

    def batch_send(h):
        for o in (1, 2, 3):

            def body(index, carry):
                def put(b, code):
                    dh_sent[h, o - 1, index, b] = code

                def put_top(top):
                    dh_sent[h, o - 1, index, 16] = top

                other = peer(o)
                encode([dh[h, other, index, rows, lanes] for rows, lanes in tiles], put, put_top)
                return carry

            lax.fori_loop(0, 2, body, 0)
            batch_copy(h, o).start()

    def batch_sum(h):
        for o in (1, 2, 3):
            batch_copy(h, o).wait_recv()

        def body(index, carry):
            for o in (1, 2, 3):
                codes = [dh_recv[h, o - 1, index, b] for b in range(16)]
                for (rows, lanes), value in zip(tiles, decode(codes, dh_recv[h, o - 1, index, 16])):
                    dh[h, batch, index, rows, lanes] += value
            return carry

        lax.fori_loop(0, 2, body, 0)
        values = [
            (
                dh[h, batch, 0, :, e * LANES : (e + 1) * LANES],
                dh[h, batch, 1, :, e * LANES : (e + 1) * LANES],
            )
            for e in range(4)
        ]
        for a, (real, imag) in enumerate(quarters(values, False)):
            put_split(zf, a, slice(0, ROWS), real, imag)

    def filter_part(h):
        batch_sum(h)
        columns(zf, yf, True)
        untwist(yf, u_f, 0, 1)
        stage_e(u_f, part_f, h, 0, 1)
        reduce_start(small, h, small_way[h])

    def half_parts(h):
        def start_pieces(q):
            reduce_start(big, q, long_way[q])

        def wait(index):
            if h == 0:
                loads[index].wait()

        return [
            lambda: (wait(0), wait(1), stage_a(h, 0, 2)),
            lambda: stage_a(h, 2, 4),
            lambda: (wait(2), columns(zb, yb, False)),
            lambda: (wait(3), wait(4), products(h, 0, 2)),
            lambda: (products(h, 2, 4), batch_send(h)),
            lambda: columns(zb, yb, True),
            lambda: (wait(5), untwist(yb, u, 0, 2), stage_e(u, part, HALF * h, 0, 2)),
            lambda: start_pieces(2 * h),
            lambda: (untwist(yb, u, 2, 4), stage_e(u, part, HALF * h, 2, 4)),
            lambda: start_pieces(2 * h + 1),
        ]

    def gather(*steps):
        for q, k in steps:
            gather_step(q, k)

    def reduce(*steps):
        for q, k in steps:
            reduce_step(big, q, long_way[q], k)

    def reduce_f(k):
        for h in range(2):
            reduce_step(small, h, small_way[h], k)

    def weave(parts, services):
        for index, part_of in enumerate(parts):
            part_of()
            for service in services.get(index, ()):
                service()

    for q in (0, 1, 2):
        gather_start(q)
    gather((0, 0), (1, 0), (2, 0), (0, 1), (1, 1))
    gather_start(3)
    gather((0, 2), (1, 2), (2, 1), (3, 0), (0, 3), (1, 3))
    weave(
        half_parts(0),
        {
            0: [lambda: gather((2, 2))],
            2: [lambda: gather((3, 1))],
            5: [lambda: gather((3, 2))],
            7: [lambda: gather((2, 3))],
            9: [lambda: gather((3, 3))],
        },
    )
    weave(half_parts(1), {3: [lambda: reduce((0, 0))], 5: [lambda: reduce((1, 0))]})
    reduce((0, 1), (1, 1), (2, 0), (3, 0))
    filter_part(0)
    reduce((0, 2), (1, 2), (2, 1), (3, 1))
    filter_part(1)
    reduce((0, 3), (1, 3), (2, 2), (3, 2))
    reduce_f(0)
    reduce((2, 3), (3, 3))
    for k in (1, 2, 3):
        reduce_f(k)

    def back_copy(h, o):
        there = pl.multiple_of(peer(o) * 8, 8)
        return pltpu.make_async_remote_copy(
            src_ref=part_f.at[me, h, pl.ds(there, 8), :],
            dst_ref=back.at[pl.ds(pl.multiple_of((HALF * h + batch) * 8, 8), 8), :],
            send_sem=b_send.at[h, o - 1], recv_sem=b_recv.at[h, o - 1],
            device_id={"dp": peer(o)}, device_id_type=MESH,
        )

    for h in range(2):
        for c, rows, lanes, value in reduce_end(small, h):
            part_f[me, c, rows, lanes] = value
        for o in (1, 2, 3):
            back_copy(h, o).start()
        here = pl.multiple_of(batch * 8, 8)
        back[pl.ds(pl.multiple_of((HALF * h + batch) * 8, 8), 8), :] = part_f[
            me, h, pl.ds(here, 8), :
        ]

    for q in range(4):
        for c, rows, lanes, value in reduce_end(big, q):
            xf[lanes.start // 128, c * TIMES + rows.start : c * TIMES + rows.start + 16, :] = value

    rows = jnp.concatenate([xf[n].astype(BF16) for n in range(4)], axis=1)
    rows = jnp.dot(rows, shuffle[1], preferred_element_type=F32)
    for n in range(4):
        xf[n] = rows[:, n * 128 : (n + 1) * 128]

    def collect(j, carry):
        for n in range(4):
            lanes = pl.ds(pl.multiple_of(j * COLS + n * 128, 128), 128)
            in_ref[0, :, lanes] = xf[n, pl.ds(j, CH, stride=TIMES), :].astype(BF16)
        return carry

    lax.fori_loop(0, TIMES, collect, 0)

    for h in range(2):
        for o in (1, 2, 3):
            back_copy(h, o).wait_recv()
    high, low = split(back[...])
    rest = (back[...] - high.astype(F32) - low.astype(F32)).astype(BF16)
    lines = sum(
        jnp.dot(item, shuffle[1], preferred_element_type=F32) for item in (rest, low, high)
    )
    for n in range(4):
        xf[n, 0:64, :] = lines[:, n * 128 : (n + 1) * 128]
        for j in range(8):
            start = j * COLS + n * 128
            fl_ref[:, start : start + 128] = xf[n, pl.ds(j, CH, stride=8), :]

    for q in range(4):
        for k in range(4):
            gather_copy(q, k, True).wait_send()
            reduce_copy(big, q, long_way[q], k, True).wait_send()
            if k < 3:
                gather_copy(q, k, False).wait_send()
                reduce_copy(big, q, long_way[q], k, False).wait_send()
    for q in range(2):
        for k in range(4):
            reduce_copy(small, q, small_way[q], k, True).wait_send()
            if k < 3:
                reduce_copy(small, q, small_way[q], k, False).wait_send()
        for o in (1, 2, 3):
            batch_copy(q, o).wait_send()
            back_copy(q, o).wait_send()


def on_device(grad_out, input_spectrum, filter_spectrum):
    wide, first, last, twist, shuffle = (jnp.asarray(t) for t in tables())
    vmem = pl.BlockSpec(memory_space=pltpu.VMEM)
    anywhere = pl.BlockSpec(memory_space=pl.ANY)
    dma = pltpu.SemaphoreType.DMA
    return pl.pallas_call(
        kernel,
        out_shape=(
            jax.ShapeDtypeStruct((1, CH, TIMES * COLS), BF16),
            jax.ShapeDtypeStruct((CH, TIMES * COLS // BATCHES), F32),
        ),
        in_specs=[vmem] + [anywhere] * 7,
        out_specs=(vmem, vmem),
        scratch_shapes=[
            pltpu.VMEM((8, 768, 256), BF16),
            pltpu.VMEM((256, 256), BF16),
            pltpu.VMEM((256, 384), BF16),
            pltpu.VMEM((2, ROWS, COLS), F32),
            pltpu.VMEM((2, COLS, COLS), BF16),
            pltpu.VMEM((2, CH, ROWS, COLS), F32),
            pltpu.VMEM((2, CH, ROWS, COLS), F32),
            pltpu.VMEM((4, CH * TIMES, 128), F32),
            pltpu.VMEM((CH, SHARDS * TIMES, COLS), BF16),
            pltpu.VMEM((4, HALF * ROWS, 768), BF16),
            pltpu.VMEM((4, HALF * ROWS, 256), F32),
            pltpu.VMEM((HALF, 384, COLS), BF16),
            pltpu.VMEM((SHARDS, CH, TIMES, COLS), F32),
            pltpu.VMEM((4, 7, 17, 16, 128), BF16),
            pltpu.VMEM((2, BATCHES, 2, ROWS, COLS), F32),
            pltpu.VMEM((2, 3, 2, 17, 16, 128), BF16),
            pltpu.VMEM((2, 3, 2, 17, 16, 128), BF16),
            pltpu.VMEM((4, ROWS, 768), BF16),
            pltpu.VMEM((4, ROWS, 256), F32),
            pltpu.VMEM((1, 384, COLS), BF16),
            pltpu.VMEM((SHARDS, 2, TIMES, COLS), F32),
            pltpu.VMEM((2, 7, 9, 16, 128), BF16),
            pltpu.VMEM((CH * 8, COLS), F32),
            pltpu.VMEM((4, 7, 17, 16, 128), BF16),
            pltpu.VMEM((2, 7, 9, 16, 128), BF16),
            dma((7,)),
            dma((4, 7)), dma((4, 7)),
            dma((4, 7)), dma((4, 7)),
            dma((2, 3)), dma((2, 3)),
            dma((2, 7)), dma((2, 7)),
            dma((2, 3)), dma((2, 3)),
        ],
        compiler_params=pltpu.CompilerParams(
            collective_id=0, has_side_effects=True, vmem_limit_bytes=56 * 1024 * 1024
        ),
    )(grad_out, input_spectrum, filter_spectrum, wide, first, last, twist, shuffle)


def solution(mesh):
    in_specs = (
        P("dp", "chan", "seq"),
        P("dp", None, "chan", "seq", None),
        P(None, "chan", "seq", None),
    )
    out_specs = (P("dp", "chan", "seq"), P("chan", ("seq", "dp")))
    return jax.shard_map(
        on_device, mesh=mesh, in_specs=in_specs, out_specs=out_specs, check_vma=False
    )
```

```python
import functools

import jax
import jax.numpy as jnp
import numpy as np
from jax import lax
from jax.experimental import pallas as pl
from jax.experimental.pallas import tpu as pltpu
from jax.sharding import PartitionSpec as P

MESH = pl.DeviceIdType.MESH
F32 = jnp.float32
BF16 = jnp.bfloat16

SHARDS = 8
BATCHES = 4
CH = 8
HALF = 4
ROWS = 64
COLS = 512
BINS = 512
TIMES = 32
MODULUS = BINS * COLS
LANES = 128
NEAR = (1, -1, 2, -2, 3, -3)
LONG_WAY = (1, 1, -1, -1, -1, 1, 1, -1)
ORDER = (
    ("gs", 0), ("gs", 1), ("gs", 2), ("gs", 3), ("gl", 0, 0), ("gr", 0, 0), ("gl", 1, 0),
    ("gr", 1, 0), ("gl", 2, 0), ("gr", 2, 0), ("gl", 3, 0), ("gr", 3, 0), ("gl", 0, 1),
    ("gr", 0, 1), ("gl", 1, 1), ("gr", 1, 1), ("gl", 2, 1), ("gr", 2, 1), ("gl", 3, 1), ("gs", 4),
    ("gs", 5), ("gr", 3, 1), ("gl", 0, 2), ("gr", 0, 2), ("gl", 1, 2), ("gs", 6), ("gr", 1, 2),
    ("gl", 2, 2), ("gr", 2, 2), ("gl", 3, 2), ("gr", 4, 0), ("gl", 4, 0), ("gl", 5, 0), ("gs", 7),
    ("gr", 5, 0), ("gr", 3, 2), ("gr", 6, 0), ("gl", 0, 3), ("A", 0), ("gl", 2, 3), ("gl", 1, 3),
    ("A", 1), ("A", 2), ("gl", 3, 3), ("gl", 6, 0), ("A", 3), ("B", 0), ("gl", 4, 1), ("gr", 4, 1),
    ("gl", 7, 0), ("gl", 5, 1), ("C", 0), ("gr", 5, 1), ("gr", 7, 0), ("Y", 0), ("D", 0),
    ("gl", 6, 1), ("gr", 6, 1), ("UE", 0), ("Rl", 0, -1), ("Rr", 0, -1), ("gl", 4, 2),
    ("gr", 4, 2), ("UE", 1), ("Rl", 1, -1), ("Rr", 1, -1), ("gl", 5, 2), ("gl", 7, 1), ("UE", 2),
    ("Rl", 2, -1), ("Rr", 2, -1), ("gr", 5, 2), ("gr", 7, 1), ("UE", 3), ("Rl", 3, -1),
    ("Rr", 3, -1), ("gl", 6, 2), ("gr", 6, 2), ("Rl", 0, 0), ("Rr", 0, 0), ("Rl", 1, 0),
    ("gl", 4, 3), ("A", 4), ("gl", 5, 3), ("Rr", 1, 0), ("A", 5), ("gl", 7, 2), ("Rr", 2, 0),
    ("gr", 7, 2), ("Rl", 2, 0), ("Rr", 3, 0), ("Rl", 3, 0), ("F", 0), ("Fs", 0), ("Rr", 1, 1),
    ("gl", 6, 3), ("Rl", 0, 1), ("Rr", 0, 1), ("Rl", 1, 1), ("gl", 7, 3), ("A", 6), ("A", 7),
    ("B", 1), ("C", 1), ("Rl", 3, 1), ("Rr", 3, 1), ("Y", 1), ("Fa", 0), ("Fc", 0), ("D", 1),
    ("Fb", 0), ("UE", 4), ("Rl", 4, -1), ("Rr", 4, -1), ("Rl", 0, 2), ("UE", 5), ("Rl", 5, -1),
    ("Rr", 5, -1), ("Rl", 1, 2), ("UE", 6), ("Rl", 6, -1), ("Rr", 6, -1), ("Rl", 3, 2), ("UE", 7),
    ("Rl", 7, -1), ("Rr", 7, -1), ("Rl", 2, 1), ("Rr", 2, 1), ("Rr", 1, 2), ("Rr", 0, 2),
    ("Rr", 3, 2), ("Rr", 4, 0), ("Fend", 0), ("Rl", 0, 3), ("X", 0), ("Rl", 4, 0), ("Rl", 5, 0),
    ("Rr", 5, 0), ("Rl", 1, 3), ("X", 1), ("Rl", 6, 0), ("F", 1), ("Fs", 1), ("Rl", 7, 0),
    ("Rr", 7, 0), ("Rr", 6, 0), ("Rl", 3, 3), ("Rr", 2, 2), ("Rr", 4, 1), ("Rl", 2, 2), ("X", 3),
    ("Rl", 4, 1), ("Rl", 5, 1), ("Rl", 6, 1), ("Rr", 5, 1), ("Fa", 1), ("Fc", 1), ("Fb", 1),
    ("Rl", 7, 1), ("Rr", 7, 1), ("Rr", 6, 1), ("Rr", 4, 2), ("Rl", 5, 2), ("Rl", 2, 3), ("X", 2),
    ("Rl", 6, 2), ("Rl", 4, 2), ("Rr", 5, 2), ("Rl", 7, 2), ("Fend", 1), ("Rr", 7, 2),
    ("Rr", 6, 2), ("Rl", 4, 3), ("Rl", 5, 3), ("X", 4), ("X", 5), ("Rl", 6, 3), ("X", 6),
    ("Rl", 7, 3), ("X", 7),
)


def split_table(table):
    high = table.astype(np.float32).astype(jnp.bfloat16)
    low = (table - high.astype(np.float64)).astype(np.float32).astype(jnp.bfloat16)
    return high, low


@functools.cache
def tables():
    turn = 2.0 * np.pi
    fold = np.arange(LANES)
    forward, inverse = [], []
    for a in range(4):
        angle = turn * (np.outer(4 * fold + a, fold) % COLS) / COLS
        c, s = np.cos(angle), np.sin(angle)
        for group, block in (
            (forward, np.block([[c, -s], [s, c]])),
            (inverse, np.block([[c.T, s.T], [-s.T, c.T]])),
        ):
            high, low = split_table(block)
            group.append(np.concatenate([high, high, low], axis=0))
    wide = np.stack(forward + inverse)
    place = np.arange(COLS)
    order = 4 * (place % LANES) + place // LANES
    shuffle = np.zeros((COLS, COLS), np.float32)
    shuffle[order, place] = 1.0
    shuffle = np.stack([shuffle, shuffle.T]).astype(jnp.bfloat16)
    half = BINS // 2
    time_angle = turn * (np.outer(np.arange(BINS), np.arange(half)) % BINS) / BINS
    cos_t = np.cos(time_angle).reshape(SHARDS, ROWS, half)
    sin_t = np.sin(time_angle).reshape(SHARDS, ROWS, half)
    first = np.concatenate([cos_t, -sin_t], axis=1)
    first_high, first_low = split_table(first)
    first_table = np.concatenate([first_high, first_low], axis=1)
    last = np.concatenate([cos_t, -sin_t], axis=1).transpose(0, 2, 1) / MODULUS
    last_high, last_low = split_table(last)
    last_table = np.concatenate([last_high, last_high, last_low], axis=2)
    twist = turn * np.outer(np.arange(BINS), np.arange(COLS)) / MODULUS
    twist_table = np.stack(
        [np.cos(twist).reshape(SHARDS, ROWS, COLS), np.sin(twist).reshape(SHARDS, ROWS, COLS)],
        axis=1,
    ).astype(np.float32)[..., order]
    return wide, first_table, last_table, twist_table, shuffle


SPAN = 124.0
GAIN = 2.0 ** (2.0 * SPAN / 32.0) - 1.0
FLOOR = 2.0 ** (-SPAN / 32.0)


def encode(values, put, put_top):
    top = jnp.abs(values[0])
    for value in values[1:]:
        top = jnp.maximum(top, jnp.abs(value))
    top = (jnp.maximum(top, 1e-30) * 1.01).astype(BF16)
    put_top(top)
    slope = (GAIN * FLOOR) / top.astype(F32)
    for index, value in enumerate(values):
        level = jnp.abs(value) * slope + FLOOR
        for _ in range(5):
            level = level * level
        put(index, jnp.where(value < 0.0, -level, level).astype(BF16))


def decode(codes, top):
    unit = top.astype(F32) * (1.0 / GAIN)
    slope = unit * (1.0 / FLOOR)
    values = []
    for code in codes:
        wide_code = code.astype(F32)
        level = jnp.exp2(jnp.log2(jnp.abs(wide_code)) * (1.0 / 32.0))
        value = level * slope - unit
        values.append(jnp.where(wide_code < 0.0, -value, value))
    return values


def split(value):
    high = value.astype(BF16)
    low = (value - high.astype(F32)).astype(BF16)
    return high, low


def kernel(
    x_ref, xs_hbm, hs_hbm, wide_hbm, first_hbm, last_hbm, twist_hbm, shuffle_hbm,
    in_ref, fl_ref,
    wide, first, last, twist, shuffle, xs, hs, xf, xg, zb, yb, db, vb, u, part, recv, dh, dh_sent, dh_recv,
    zf, yf, u_f, part_f, recv_f, back, sent, sent_f, load_sem, ag_send, ag_recv, rs_send, rs_recv, y_send, y_recv,
    f_send, f_recv, b_send, b_recv,
):
    me = lax.axis_index("seq")
    batch = lax.axis_index("dp")

    def ring(offset):
        return lax.rem(me + (offset + SHARDS), SHARDS)

    def peer(offset):
        return lax.rem(batch + offset, BATCHES)

    barrier = pltpu.get_barrier_semaphore()
    for offset in NEAR:
        pl.semaphore_signal(barrier, inc=1, device_id={"seq": ring(offset)}, device_id_type=MESH)
    for offset in (1, 2, 3):
        pl.semaphore_signal(barrier, inc=1, device_id={"dp": peer(offset)}, device_id_type=MESH)

    loads = [
        pltpu.make_async_copy(first_hbm.at[me], first, load_sem.at[0]),
        pltpu.make_async_copy(twist_hbm.at[me], twist, load_sem.at[1]),
        pltpu.make_async_copy(wide_hbm, wide, load_sem.at[2]),
        pltpu.make_async_copy(hs_hbm, hs, load_sem.at[3]),
        pltpu.make_async_copy(xs_hbm.at[0], xs, load_sem.at[4]),
        pltpu.make_async_copy(last_hbm.at[me], last, load_sem.at[5]),
        pltpu.make_async_copy(shuffle_hbm, shuffle, load_sem.at[6]),
    ]
    for index in (6, 0, 1, 2, 3, 4, 5):
        loads[index].start()

    def spread(j, carry):
        for n in range(4):
            lanes = pl.ds(pl.multiple_of(j * COLS + n * 128, 128), 128)
            xf[n, pl.ds(j, CH, stride=TIMES), :] = x_ref[0, :, lanes].astype(F32)
        return carry

    lax.fori_loop(0, TIMES, spread, 0)
    mine = pl.multiple_of(me * TIMES, TIMES)
    loads[6].wait()
    rows = jnp.concatenate([xf[n].astype(BF16) for n in range(4)], axis=1)
    rows = jnp.dot(rows, shuffle[0], preferred_element_type=F32).astype(BF16)
    for c in range(CH):
        xg[c, pl.ds(mine, TIMES), :] = rows[c * TIMES : (c + 1) * TIMES, :]

    pl.semaphore_wait(barrier, len(NEAR) + 3)

    def gather_copy(q, k, long):
        way = LONG_WAY[q] if long else -LONG_WAY[q]
        source = pl.multiple_of(ring(-way * k) * TIMES, TIMES)
        block = xg.at[q, pl.ds(source, TIMES), :]
        slot = k if long else 4 + k
        return pltpu.make_async_remote_copy(
            src_ref=block, dst_ref=block, send_sem=ag_send.at[q, slot], recv_sem=ag_recv.at[q, slot],
            device_id={"seq": ring(way)}, device_id_type=MESH,
        )

    def gather_start(q):
        gather_copy(q, 0, True).start()
        gather_copy(q, 0, False).start()

    def gather_hop(q, k, long):
        gather_copy(q, k, long).wait_recv()
        if k < (3 if long else 2):
            gather_copy(q, k + 1, long).start()

    def put_split(dest, a, rows, real, imag):
        for index, value in enumerate((real, imag)):
            high, low = split(value)
            for place, item in ((0, high), (2, low), (4, high)):
                lane = (place + index) * LANES
                dest[a, rows, lane : lane + LANES] = item

    def stage_a(q):
        h, c = divmod(q, HALF)
        t = jnp.dot(first[...], xg[q], preferred_element_type=F32)
        real = t[0:64] + t[128:192]
        imag = t[64:128] + t[192:256]
        rows = slice(c * ROWS, (c + 1) * ROWS)
        for a in range(4):
            lanes = slice(a * LANES, (a + 1) * LANES)
            tc, ts = twist[0, :, lanes], twist[1, :, lanes]
            ar, ai = real[:, lanes], imag[:, lanes]
            put_split(zb.at[h], a, rows, ar * tc + ai * ts, ai * tc - ar * ts)

    def columns(source, dest, inverse):
        for a in range(4):
            weight = wide[a + 4] if inverse else wide[a]
            dest[a] = jnp.dot(source[a], weight, preferred_element_type=F32)

    def quarters(values, forward):
        (r0, i0), (r1, i1), (r2, i2), (r3, i3) = values
        sr, si, dr, di = r0 + r2, i0 + i2, r0 - r2, i0 - i2
        tr, ti, er, ei = r1 + r3, i1 + i3, r1 - r3, i1 - i3
        left = (dr + ei, di - er)
        right = (dr - ei, di + er)
        if not forward:
            left, right = right, left
        return [(sr + tr, si + ti), left, (sr - tr, si - ti), right]

    def products(h):
        def body(c, carry):
            rows = pl.ds(pl.multiple_of(c * ROWS, ROWS), ROWS)
            bins = quarters(
                [(yb[h, a, rows, 0:LANES], yb[h, a, rows, LANES : 2 * LANES]) for a in range(4)],
                True,
            )
            channel = HALF * h + c
            inner = []
            for e, (gr, gi) in enumerate(bins):
                lanes = slice(e * LANES, (e + 1) * LANES)
                hr, hi_ = hs[0, channel, :, lanes], hs[1, channel, :, lanes]
                inner.append((gr * hr + gi * hi_, gi * hr - gr * hi_))
                xr, xi = xs[0, channel, :, lanes], xs[1, channel, :, lanes]
                dh[h, c, 0, :, lanes] = gr * xr + gi * xi
                dh[h, c, 1, :, lanes] = gi * xr - gr * xi
            for a, (real, imag) in enumerate(quarters(inner, False)):
                put_split(db.at[h], a, rows, real, imag)
            return carry

        lax.fori_loop(0, HALF, body, 0)

    def finish(source, c, buffer, dest, channel):
        rows = slice(c * ROWS, (c + 1) * ROWS)
        for a in range(4):
            lanes = slice(a * LANES, (a + 1) * LANES)
            vr, vi = source[a, rows, 0:LANES], source[a, rows, LANES : 2 * LANES]
            tc, ts = twist[0, :, lanes], twist[1, :, lanes]
            for index, value in enumerate((vr * tc - vi * ts, vi * tc + vr * ts)):
                high, low = split(value)
                buffer[64 * index : 64 * index + 64, lanes] = high
                buffer[128 + 64 * index : 192 + 64 * index, lanes] = low
                buffer[256 + 64 * index : 320 + 64 * index, lanes] = high
        y = jnp.dot(last[...], buffer[...], preferred_element_type=F32)
        dest[:, channel] = y.reshape(SHARDS, TIMES, COLS)

    def share(part_ref, dest, c):
        return [part_ref[dest, c, rows, lanes] for rows, lanes in lines_of]

    lines_of = [
        (pl.ds(16 * r, 16), pl.ds(128 * n, 128)) for r in range(TIMES // 16) for n in range(4)
    ]

    def read(ref, q, slot):
        return decode([ref[q, slot, b] for b in range(8)], ref[q, slot, 8])

    def write(ref, q, slot, values):
        def put(index, code):
            ref[q, slot, index] = code

        def put_top(top):
            ref[q, slot, 8] = top

        encode(values, put, put_top)

    def add(left, right):
        return [a + b for a, b in zip(left, right)]

    def reduce_copy(q, k, long):
        slot = k if long else 4 + k
        way = LONG_WAY[q] if long else -LONG_WAY[q]
        return pltpu.make_async_remote_copy(
            src_ref=sent.at[q, slot], dst_ref=recv.at[q, slot],
            send_sem=rs_send.at[q, slot], recv_sem=rs_recv.at[q, slot],
            device_id={"seq": ring(way)}, device_id_type=MESH,
        )

    def reduce_hop(q, k, long):
        hops = 4 if long else 3
        way = LONG_WAY[q] if long else -LONG_WAY[q]
        base = 0 if long else 4
        if k >= 0:
            reduce_copy(q, k, long).wait_recv()
        if k == hops - 1:
            return
        values = share(part, ring(way * (hops - 1 - k)), q)
        if k >= 0:
            values = add(values, read(recv, q, base + k))
        write(sent, q, base + k + 1, values)
        reduce_copy(q, k + 1, long).start()

    def reduce_end(q):
        values = add(share(part, me, q), add(read(recv, q, 3), read(recv, q, 6)))
        for (rows, lanes), value in zip(lines_of, values):
            xf[lanes.start // 128, q * TIMES + rows.start : q * TIMES + rows.start + 16, :] = value

    def pair_copy(h, slot):
        way = 1 if h else -1
        return pltpu.make_async_remote_copy(
            src_ref=sent_f.at[h, slot], dst_ref=recv_f.at[h, slot],
            send_sem=f_send.at[h, slot], recv_sem=f_recv.at[h, slot],
            device_id={"seq": ring(way * (1, 1, -1, -1, 3, 1, -2)[slot])}, device_id_type=MESH,
        )

    def pair_send(h, slot, offset, arrived=None):
        values = share(part_f, ring(offset * (1 if h else -1)), h)
        if arrived is not None:
            pair_copy(h, arrived).wait_recv()
            values = add(values, read(recv_f, h, arrived))
        write(sent_f, h, slot, values)
        pair_copy(h, slot).start()

    def pair_start(h):
        for slot, offset in ((0, 4), (1, 2), (2, -3), (3, -1)):
            pair_send(h, slot, offset)

    def pair_end(h):
        values = share(part_f, me, h)
        for slot in (3, 4, 5, 6):
            pair_copy(h, slot).wait_recv()
            values = add(values, read(recv_f, h, slot))
        for (rows, lanes), value in zip(lines_of, values):
            part_f[me, h, rows, lanes] = value
        for o in (1, 2, 3):
            back_copy(h, o).start()
        here = pl.multiple_of(batch * 8, 8)
        back[pl.ds(pl.multiple_of((HALF * h + batch) * 8, 8), 8), :] = part_f[
            me, h, pl.ds(here, 8), :
        ]

    def batch_copy(h, o):
        return pltpu.make_async_remote_copy(
            src_ref=dh_sent.at[h, o - 1], dst_ref=dh_recv.at[h, o - 1],
            send_sem=y_send.at[h, o - 1], recv_sem=y_recv.at[h, o - 1],
            device_id={"dp": peer(o)}, device_id_type=MESH,
        )

    tiles = [(pl.ds(16 * r, 16), pl.ds(128 * n, 128)) for r in range(ROWS // 16) for n in range(4)]

    def batch_send(h):
        for o in (1, 2, 3):

            def body(index, carry):
                def put(b, code):
                    dh_sent[h, o - 1, index, b] = code

                def put_top(top):
                    dh_sent[h, o - 1, index, 16] = top

                other = peer(o)
                encode([dh[h, other, index, rows, lanes] for rows, lanes in tiles], put, put_top)
                return carry

            lax.fori_loop(0, 2, body, 0)
            batch_copy(h, o).start()

    def batch_sum(h):
        for o in (1, 2, 3):
            batch_copy(h, o).wait_recv()

        def body(index, carry):
            for o in (1, 2, 3):
                codes = [dh_recv[h, o - 1, index, b] for b in range(16)]
                for (rows, lanes), value in zip(tiles, decode(codes, dh_recv[h, o - 1, index, 16])):
                    dh[h, batch, index, rows, lanes] += value
            return carry

        lax.fori_loop(0, 2, body, 0)
        values = [
            (
                dh[h, batch, 0, :, e * LANES : (e + 1) * LANES],
                dh[h, batch, 1, :, e * LANES : (e + 1) * LANES],
            )
            for e in range(4)
        ]
        for a, (real, imag) in enumerate(quarters(values, False)):
            put_split(zf, a, slice(0, ROWS), real, imag)

    def filter_part(h):
        batch_sum(h)
        columns(zf, yf, True)
        finish(yf, 0, u_f, part_f, h)

    def back_copy(h, o):
        there = pl.multiple_of(peer(o) * 8, 8)
        return pltpu.make_async_remote_copy(
            src_ref=part_f.at[me, h, pl.ds(there, 8), :],
            dst_ref=back.at[pl.ds(pl.multiple_of((HALF * h + batch) * 8, 8), 8), :],
            send_sem=b_send.at[h, o - 1], recv_sem=b_recv.at[h, o - 1],
            device_id={"dp": peer(o)}, device_id_type=MESH,
        )

    waited = set()

    def need(*indices):
        for index in indices:
            if index not in waited:
                waited.add(index)
                loads[index].wait()

    def run(kind, q, k=None):
        if kind == "gs":
            gather_start(q)
        elif kind in ("gl", "gr"):
            gather_hop(q, k, kind == "gl")
        elif kind == "A":
            need(0, 1)
            stage_a(q)
        elif kind == "B":
            need(2)
            columns(zb.at[q], yb.at[q], False)
        elif kind == "C":
            need(3, 4)
            products(q)
        elif kind == "Y":
            batch_send(q)
        elif kind == "D":
            columns(db.at[q], vb.at[q], True)
        elif kind == "UE":
            need(5)
            finish(vb.at[q // HALF], q % HALF, u.at[q % HALF], part, q)
        elif kind in ("Rl", "Rr"):
            reduce_hop(q, k, kind == "Rl")
        elif kind == "X":
            reduce_end(q)
        elif kind == "F":
            filter_part(q)
        elif kind == "Fs":
            pair_start(q)
        elif kind == "Fa":
            pair_send(q, 4, 3, 0)
        elif kind == "Fb":
            pair_send(q, 5, 1, 1)
        elif kind == "Fc":
            pair_send(q, 6, -2, 2)
        elif kind == "Fend":
            pair_end(q)

    for task in ORDER:
        run(*task)

    rows = jnp.concatenate([xf[n].astype(BF16) for n in range(4)], axis=1)
    rows = jnp.dot(rows, shuffle[1], preferred_element_type=F32)
    for n in range(4):
        xf[n] = rows[:, n * 128 : (n + 1) * 128]

    def collect(j, carry):
        for n in range(4):
            lanes = pl.ds(pl.multiple_of(j * COLS + n * 128, 128), 128)
            in_ref[0, :, lanes] = xf[n, pl.ds(j, CH, stride=TIMES), :].astype(BF16)
        return carry

    lax.fori_loop(0, TIMES, collect, 0)

    for h in range(2):
        for o in (1, 2, 3):
            back_copy(h, o).wait_recv()
    high, low = split(back[...])
    rest = (back[...] - high.astype(F32) - low.astype(F32)).astype(BF16)
    lines = sum(
        jnp.dot(item, shuffle[1], preferred_element_type=F32) for item in (rest, low, high)
    )
    for n in range(4):
        xf[n, 0:64, :] = lines[:, n * 128 : (n + 1) * 128]
        for j in range(8):
            start = j * COLS + n * 128
            fl_ref[:, start : start + 128] = xf[n, pl.ds(j, CH, stride=8), :]

    for q in range(CH):
        for k in range(4):
            gather_copy(q, k, True).wait_send()
            reduce_copy(q, k, True).wait_send()
            if k < 3:
                gather_copy(q, k, False).wait_send()
                reduce_copy(q, k, False).wait_send()
    for h in range(2):
        for slot in range(7):
            pair_copy(h, slot).wait_send()
        for o in (1, 2, 3):
            batch_copy(h, o).wait_send()
            back_copy(h, o).wait_send()


def on_device(grad_out, input_spectrum, filter_spectrum):
    wide, first, last, twist, shuffle = (jnp.asarray(t) for t in tables())
    vmem = pl.BlockSpec(memory_space=pltpu.VMEM)
    anywhere = pl.BlockSpec(memory_space=pl.ANY)
    dma = pltpu.SemaphoreType.DMA
    return pl.pallas_call(
        kernel,
        out_shape=(
            jax.ShapeDtypeStruct((1, CH, TIMES * COLS), BF16),
            jax.ShapeDtypeStruct((CH, TIMES * COLS // BATCHES), F32),
        ),
        in_specs=[vmem] + [anywhere] * 7,
        out_specs=(vmem, vmem),
        scratch_shapes=[
            pltpu.VMEM((8, 768, 256), BF16),
            pltpu.VMEM((256, 256), BF16),
            pltpu.VMEM((256, 384), BF16),
            pltpu.VMEM((2, ROWS, COLS), F32),
            pltpu.VMEM((2, COLS, COLS), BF16),
            pltpu.VMEM((2, CH, ROWS, COLS), F32),
            pltpu.VMEM((2, CH, ROWS, COLS), F32),
            pltpu.VMEM((4, CH * TIMES, 128), F32),
            pltpu.VMEM((CH, SHARDS * TIMES, COLS), BF16),
            pltpu.VMEM((2, 4, HALF * ROWS, 768), BF16),
            pltpu.VMEM((2, 4, HALF * ROWS, 256), F32),
            pltpu.VMEM((2, 4, HALF * ROWS, 768), BF16),
            pltpu.VMEM((2, 4, HALF * ROWS, 256), F32),
            pltpu.VMEM((HALF, 384, COLS), BF16),
            pltpu.VMEM((SHARDS, CH, TIMES, COLS), F32),
            pltpu.VMEM((CH, 7, 9, 16, 128), BF16),
            pltpu.VMEM((2, BATCHES, 2, ROWS, COLS), F32),
            pltpu.VMEM((2, 3, 2, 17, 16, 128), BF16),
            pltpu.VMEM((2, 3, 2, 17, 16, 128), BF16),
            pltpu.VMEM((4, ROWS, 768), BF16),
            pltpu.VMEM((4, ROWS, 256), F32),
            pltpu.VMEM((384, COLS), BF16),
            pltpu.VMEM((SHARDS, 2, TIMES, COLS), F32),
            pltpu.VMEM((2, 7, 9, 16, 128), BF16),
            pltpu.VMEM((CH * 8, COLS), F32),
            pltpu.VMEM((CH, 7, 9, 16, 128), BF16),
            pltpu.VMEM((2, 7, 9, 16, 128), BF16),
            dma((7,)),
            dma((CH, 7)), dma((CH, 7)),
            dma((CH, 7)), dma((CH, 7)),
            dma((2, 3)), dma((2, 3)),
            dma((2, 7)), dma((2, 7)),
            dma((2, 3)), dma((2, 3)),
        ],
        compiler_params=pltpu.CompilerParams(
            collective_id=0, has_side_effects=True, vmem_limit_bytes=56 * 1024 * 1024
        ),
    )(grad_out, input_spectrum, filter_spectrum, wide, first, last, twist, shuffle)


def solution(mesh):
    in_specs = (
        P("dp", "chan", "seq"),
        P("dp", None, "chan", "seq", None),
        P(None, "chan", "seq", None),
    )
    out_specs = (P("dp", "chan", "seq"), P("chan", ("seq", "dp")))
    return jax.shard_map(
        on_device, mesh=mesh, in_specs=in_specs, out_specs=out_specs, check_vma=False
    )
```

```python
import functools

import jax
import jax.numpy as jnp
import numpy as np
from jax import lax
from jax.experimental import pallas as pl
from jax.experimental.pallas import tpu as pltpu
from jax.sharding import PartitionSpec as P

MESH = pl.DeviceIdType.MESH
F32 = jnp.float32
BF16 = jnp.bfloat16

SHARDS = 8
BATCHES = 4
CH = 8
HALF = 4
ROWS = 64
COLS = 512
BINS = 512
TIMES = 32
MODULUS = BINS * COLS
LANES = 128
NEAR = (1, -1, 2, -2, 3, -3)
CHAIN_WAY = -1
LONG_WAY = (1, 1, 1, 1, -1, -1, -1, -1)
ORDER = (
    ("gs", 0), ("gs", 1), ("gs", 2), ("gs", 3), ("gl", 0, 0), ("gr", 0, 0), ("gl", 1, 0),
    ("gr", 1, 0), ("gl", 2, 0), ("gr", 2, 0), ("gl", 3, 0), ("gr", 3, 0), ("gl", 0, 1),
    ("gr", 0, 1), ("gl", 1, 1), ("gr", 1, 1), ("gl", 2, 1), ("gr", 2, 1), ("gl", 3, 1), ("gs", 5),
    ("gr", 3, 1), ("gl", 0, 2), ("gr", 0, 2), ("gl", 1, 2), ("gr", 1, 2), ("gs", 4), ("gs", 7),
    ("gl", 2, 2), ("gr", 2, 2), ("gl", 3, 2), ("gs", 6), ("gl", 5, 0), ("gr", 5, 0), ("gr", 3, 2),
    ("gl", 0, 3), ("A", 0), ("gl", 4, 0), ("gl", 1, 3), ("A", 1), ("gl", 7, 0), ("gr", 4, 0),
    ("gl", 6, 0), ("gr", 7, 0), ("gl", 5, 1), ("gl", 2, 3), ("A", 2), ("gl", 4, 1), ("gl", 3, 3),
    ("A", 3), ("B", 0), ("gl", 6, 1), ("gr", 6, 0), ("gl", 7, 1), ("gr", 5, 1), ("C", 0),
    ("gl", 5, 2), ("gr", 4, 1), ("Y", 0), ("gl", 4, 2), ("D", 0), ("gr", 7, 1), ("UE", 0),
    ("gl", 6, 2), ("gr", 6, 1), ("Rl", 0, -1), ("Rr", 0, -1), ("UE", 1), ("gl", 7, 2),
    ("gr", 5, 2), ("Rl", 1, -1), ("Rr", 1, -1), ("UE", 2), ("gl", 5, 3), ("Rl", 2, -1),
    ("Rr", 2, -1), ("gr", 4, 2), ("A", 5), ("gl", 4, 3), ("A", 4), ("gr", 7, 2), ("UE", 3),
    ("gl", 6, 3), ("gr", 6, 2), ("Rl", 3, -1), ("Rr", 3, -1), ("A", 6), ("Rr", 0, 0), ("Rl", 0, 0),
    ("gl", 7, 3), ("A", 7), ("Rl", 1, 0), ("B", 1), ("Rr", 1, 0), ("Rl", 2, 0), ("C", 1),
    ("Rl", 3, 0), ("Rr", 2, 0), ("Rr", 3, 0), ("Y", 1), ("Rl", 0, 1), ("F", 0), ("Rr", 0, 1),
    ("Rl", 1, 1), ("Rr", 1, 1), ("Rl", 2, 1), ("Fs", 0), ("D", 1), ("Rl", 3, 1), ("Rr", 2, 1),
    ("Rl", 0, 2), ("Rr", 3, 1), ("UE", 4), ("Rl", 4, -1), ("Rr", 4, -1), ("UE", 5), ("Rl", 1, 2),
    ("Rl", 5, -1), ("Rr", 5, -1), ("Rr", 0, 2), ("UE", 6), ("Rl", 2, 2), ("Rl", 6, -1),
    ("Rr", 6, -1), ("UE", 7), ("Fl", 0, 0), ("Fr", 0, 0), ("Rl", 7, -1), ("Rr", 7, -1),
    ("Rr", 1, 2), ("Rl", 3, 2), ("Rr", 2, 2), ("Rr", 3, 2), ("Rl", 0, 3), ("X", 0), ("Rl", 4, 0),
    ("F", 1), ("Fs", 1), ("Rl", 6, 0), ("Rr", 4, 0), ("Rl", 5, 0), ("Rr", 5, 0), ("Rl", 1, 3),
    ("Fl", 0, 1), ("Rl", 2, 3), ("X", 1), ("X", 2), ("Rl", 7, 0), ("Rr", 6, 0), ("Rl", 4, 1),
    ("Fr", 0, 1), ("Fc", 1), ("Rr", 7, 0), ("Rl", 3, 3), ("X", 3), ("Rl", 6, 1), ("Fa", 1),
    ("Rl", 5, 1), ("Fb", 1), ("Fl", 0, 2), ("Rr", 4, 1), ("Rl", 7, 1), ("Rr", 5, 1), ("Rl", 4, 2),
    ("Rr", 6, 1), ("Fr", 0, 2), ("Rr", 7, 1), ("Rl", 6, 2), ("Rl", 5, 2), ("Fl", 0, 3),
    ("Fend", 0), ("Rl", 7, 2), ("Fend", 1), ("Rl", 4, 3), ("Rr", 4, 2), ("X", 4), ("Rl", 6, 3),
    ("Rr", 5, 2), ("Rl", 5, 3), ("Rr", 6, 2), ("X", 5), ("X", 6), ("Rl", 7, 3), ("Rr", 7, 2),
    ("X", 7),
)


def split_table(table):
    high = table.astype(np.float32).astype(jnp.bfloat16)
    low = (table - high.astype(np.float64)).astype(np.float32).astype(jnp.bfloat16)
    return high, low


@functools.cache
def tables():
    turn = 2.0 * np.pi
    fold = np.arange(LANES)
    forward, inverse = [], []
    for a in range(4):
        angle = turn * (np.outer(4 * fold + a, fold) % COLS) / COLS
        c, s = np.cos(angle), np.sin(angle)
        for group, block in (
            (forward, np.block([[c, -s], [s, c]])),
            (inverse, np.block([[c.T, s.T], [-s.T, c.T]])),
        ):
            high, low = split_table(block)
            group.append(np.concatenate([high, high, low], axis=0))
    wide = np.stack(forward + inverse)
    place = np.arange(COLS)
    order = 4 * (place % LANES) + place // LANES
    shuffle = np.zeros((COLS, COLS), np.float32)
    shuffle[order, place] = 1.0
    shuffle = np.stack([shuffle, shuffle.T]).astype(jnp.bfloat16)
    half = BINS // 2
    time_angle = turn * (np.outer(np.arange(BINS), np.arange(half)) % BINS) / BINS
    cos_t = np.cos(time_angle).reshape(SHARDS, ROWS, half)
    sin_t = np.sin(time_angle).reshape(SHARDS, ROWS, half)
    first = np.concatenate([cos_t, -sin_t], axis=1)
    first_high, first_low = split_table(first)
    first_table = np.concatenate([first_high, first_low], axis=1)
    last = np.concatenate([cos_t, -sin_t], axis=1).transpose(0, 2, 1) / MODULUS
    last_high, last_low = split_table(last)
    last_table = np.concatenate([last_high, last_high, last_low], axis=2)
    twist = turn * np.outer(np.arange(BINS), np.arange(COLS)) / MODULUS
    twist_table = np.stack(
        [np.cos(twist).reshape(SHARDS, ROWS, COLS), np.sin(twist).reshape(SHARDS, ROWS, COLS)],
        axis=1,
    ).astype(np.float32)[..., order]
    return wide, first_table, last_table, twist_table, shuffle


SPAN = 124.0
GAIN = 2.0 ** (2.0 * SPAN / 32.0) - 1.0
FLOOR = 2.0 ** (-SPAN / 32.0)


def encode(values, put, put_top):
    top = jnp.abs(values[0])
    for value in values[1:]:
        top = jnp.maximum(top, jnp.abs(value))
    top = (jnp.maximum(top, 1e-30) * 1.01).astype(BF16)
    put_top(top)
    slope = (GAIN * FLOOR) / top.astype(F32)
    for index, value in enumerate(values):
        level = jnp.abs(value) * slope + FLOOR
        for _ in range(5):
            level = level * level
        put(index, jnp.where(value < 0.0, -level, level).astype(BF16))


def decode(codes, top):
    unit = top.astype(F32) * (1.0 / GAIN)
    slope = unit * (1.0 / FLOOR)
    values = []
    for code in codes:
        wide_code = code.astype(F32)
        level = jnp.exp2(jnp.log2(jnp.abs(wide_code)) * (1.0 / 32.0))
        value = level * slope - unit
        values.append(jnp.where(wide_code < 0.0, -value, value))
    return values


def split(value):
    high = value.astype(BF16)
    low = (value - high.astype(F32)).astype(BF16)
    return high, low


def kernel(
    x_ref, xs_hbm, hs_hbm, wide_hbm, first_hbm, last_hbm, twist_hbm, shuffle_hbm,
    in_ref, fl_ref,
    wide, first, last, twist, shuffle, xs, hs, xf, xg, zb, yb, db, vb, u, part, recv, dh, dh_sent, dh_recv,
    zf, yf, u_f, part_f, recv_f, back, sent, sent_f, load_sem, ag_send, ag_recv, rs_send, rs_recv, y_send, y_recv,
    f_send, f_recv, b_send, b_recv,
):
    me = lax.axis_index("seq")
    batch = lax.axis_index("dp")

    def ring(offset):
        return lax.rem(me + (offset + SHARDS), SHARDS)

    def peer(offset):
        return lax.rem(batch + offset, BATCHES)

    barrier = pltpu.get_barrier_semaphore()
    for offset in NEAR:
        pl.semaphore_signal(barrier, inc=1, device_id={"seq": ring(offset)}, device_id_type=MESH)
    for offset in (1, 2, 3):
        pl.semaphore_signal(barrier, inc=1, device_id={"dp": peer(offset)}, device_id_type=MESH)

    loads = [
        pltpu.make_async_copy(first_hbm.at[me], first, load_sem.at[0]),
        pltpu.make_async_copy(twist_hbm.at[me], twist, load_sem.at[1]),
        pltpu.make_async_copy(wide_hbm, wide, load_sem.at[2]),
        pltpu.make_async_copy(hs_hbm, hs, load_sem.at[3]),
        pltpu.make_async_copy(xs_hbm.at[0], xs, load_sem.at[4]),
        pltpu.make_async_copy(last_hbm.at[me], last, load_sem.at[5]),
        pltpu.make_async_copy(shuffle_hbm, shuffle, load_sem.at[6]),
    ]
    for index in (6, 0, 1, 2, 3, 4, 5):
        loads[index].start()

    def spread(j, carry):
        for n in range(4):
            lanes = pl.ds(pl.multiple_of(j * COLS + n * 128, 128), 128)
            xf[n, pl.ds(j, CH, stride=TIMES), :] = x_ref[0, :, lanes].astype(F32)
        return carry

    lax.fori_loop(0, TIMES, spread, 0)
    mine = pl.multiple_of(me * TIMES, TIMES)
    loads[6].wait()
    rows = jnp.concatenate([xf[n].astype(BF16) for n in range(4)], axis=1)
    rows = jnp.dot(rows, shuffle[0], preferred_element_type=F32).astype(BF16)
    for c in range(CH):
        xg[c, pl.ds(mine, TIMES), :] = rows[c * TIMES : (c + 1) * TIMES, :]

    pl.semaphore_wait(barrier, len(NEAR) + 3)

    def gather_copy(q, k, long):
        way = LONG_WAY[q] if long else -LONG_WAY[q]
        source = pl.multiple_of(ring(-way * k) * TIMES, TIMES)
        block = xg.at[q, pl.ds(source, TIMES), :]
        slot = k if long else 4 + k
        return pltpu.make_async_remote_copy(
            src_ref=block, dst_ref=block, send_sem=ag_send.at[q, slot], recv_sem=ag_recv.at[q, slot],
            device_id={"seq": ring(way)}, device_id_type=MESH,
        )

    def gather_start(q):
        gather_copy(q, 0, True).start()
        gather_copy(q, 0, False).start()

    def gather_hop(q, k, long):
        gather_copy(q, k, long).wait_recv()
        if k < (3 if long else 2):
            gather_copy(q, k + 1, long).start()

    def put_split(dest, a, rows, real, imag):
        for index, value in enumerate((real, imag)):
            high, low = split(value)
            for place, item in ((0, high), (2, low), (4, high)):
                lane = (place + index) * LANES
                dest[a, rows, lane : lane + LANES] = item

    def stage_a(q):
        h, c = divmod(q, HALF)
        t = jnp.dot(first[...], xg[q], preferred_element_type=F32)
        real = t[0:64] + t[128:192]
        imag = t[64:128] + t[192:256]
        rows = slice(c * ROWS, (c + 1) * ROWS)
        for a in range(4):
            lanes = slice(a * LANES, (a + 1) * LANES)
            tc, ts = twist[0, :, lanes], twist[1, :, lanes]
            ar, ai = real[:, lanes], imag[:, lanes]
            put_split(zb.at[h], a, rows, ar * tc + ai * ts, ai * tc - ar * ts)

    def columns(source, dest, inverse):
        for a in range(4):
            weight = wide[a + 4] if inverse else wide[a]
            dest[a] = jnp.dot(source[a], weight, preferred_element_type=F32)

    def quarters(values, forward):
        (r0, i0), (r1, i1), (r2, i2), (r3, i3) = values
        sr, si, dr, di = r0 + r2, i0 + i2, r0 - r2, i0 - i2
        tr, ti, er, ei = r1 + r3, i1 + i3, r1 - r3, i1 - i3
        left = (dr + ei, di - er)
        right = (dr - ei, di + er)
        if not forward:
            left, right = right, left
        return [(sr + tr, si + ti), left, (sr - tr, si - ti), right]

    def products(h):
        def body(c, carry):
            rows = pl.ds(pl.multiple_of(c * ROWS, ROWS), ROWS)
            bins = quarters(
                [(yb[h, a, rows, 0:LANES], yb[h, a, rows, LANES : 2 * LANES]) for a in range(4)],
                True,
            )
            channel = HALF * h + c
            inner = []
            for e, (gr, gi) in enumerate(bins):
                lanes = slice(e * LANES, (e + 1) * LANES)
                hr, hi_ = hs[0, channel, :, lanes], hs[1, channel, :, lanes]
                inner.append((gr * hr + gi * hi_, gi * hr - gr * hi_))
                xr, xi = xs[0, channel, :, lanes], xs[1, channel, :, lanes]
                dh[h, c, 0, :, lanes] = gr * xr + gi * xi
                dh[h, c, 1, :, lanes] = gi * xr - gr * xi
            for a, (real, imag) in enumerate(quarters(inner, False)):
                put_split(db.at[h], a, rows, real, imag)
            return carry

        lax.fori_loop(0, HALF, body, 0)

    def finish(source, c, buffer, dest, channel):
        rows = slice(c * ROWS, (c + 1) * ROWS)
        for a in range(4):
            lanes = slice(a * LANES, (a + 1) * LANES)
            vr, vi = source[a, rows, 0:LANES], source[a, rows, LANES : 2 * LANES]
            tc, ts = twist[0, :, lanes], twist[1, :, lanes]
            for index, value in enumerate((vr * tc - vi * ts, vi * tc + vr * ts)):
                high, low = split(value)
                buffer[64 * index : 64 * index + 64, lanes] = high
                buffer[128 + 64 * index : 192 + 64 * index, lanes] = low
                buffer[256 + 64 * index : 320 + 64 * index, lanes] = high
        y = jnp.dot(last[...], buffer[...], preferred_element_type=F32)
        dest[:, channel] = y.reshape(SHARDS, TIMES, COLS)

    def share(part_ref, dest, c):
        return [part_ref[dest, c, rows, lanes] for rows, lanes in lines_of]

    lines_of = [
        (pl.ds(16 * r, 16), pl.ds(128 * n, 128)) for r in range(TIMES // 16) for n in range(4)
    ]

    def read(ref, q, slot):
        return decode([ref[q, slot, b] for b in range(8)], ref[q, slot, 8])

    def write(ref, q, slot, values):
        def put(index, code):
            ref[q, slot, index] = code

        def put_top(top):
            ref[q, slot, 8] = top

        encode(values, put, put_top)

    def add(left, right):
        return [a + b for a, b in zip(left, right)]

    def reduce_copy(q, k, long):
        slot = k if long else 4 + k
        way = LONG_WAY[q] if long else -LONG_WAY[q]
        return pltpu.make_async_remote_copy(
            src_ref=sent.at[q, slot], dst_ref=recv.at[q, slot],
            send_sem=rs_send.at[q, slot], recv_sem=rs_recv.at[q, slot],
            device_id={"seq": ring(way)}, device_id_type=MESH,
        )

    def reduce_hop(q, k, long):
        hops = 4 if long else 3
        way = LONG_WAY[q] if long else -LONG_WAY[q]
        base = 0 if long else 4
        if k >= 0:
            reduce_copy(q, k, long).wait_recv()
        if k == hops - 1:
            return
        values = share(part, ring(way * (hops - 1 - k)), q)
        if k >= 0:
            values = add(values, read(recv, q, base + k))
        write(sent, q, base + k + 1, values)
        reduce_copy(q, k + 1, long).start()

    def reduce_end(q):
        values = add(share(part, me, q), add(read(recv, q, 3), read(recv, q, 6)))
        for (rows, lanes), value in zip(lines_of, values):
            xf[lanes.start // 128, q * TIMES + rows.start : q * TIMES + rows.start + 16, :] = value

    def pair_copy(h, slot):
        way = 1 if h else -1
        return pltpu.make_async_remote_copy(
            src_ref=sent_f.at[h, slot], dst_ref=recv_f.at[h, slot],
            send_sem=f_send.at[h, slot], recv_sem=f_recv.at[h, slot],
            device_id={"seq": ring(way * (1, 1, -1, -1, 3, 1, -2)[slot])}, device_id_type=MESH,
        )

    def pair_send(h, slot, offset, arrived=None):
        values = share(part_f, ring(offset * (1 if h else -1)), h)
        if arrived is not None:
            pair_copy(h, arrived).wait_recv()
            values = add(values, read(recv_f, h, arrived))
        write(sent_f, h, slot, values)
        pair_copy(h, slot).start()

    def chain_copy(h, k, long):
        slot = k if long else 4 + k
        return pltpu.make_async_remote_copy(
            src_ref=sent_f.at[h, slot], dst_ref=recv_f.at[h, slot],
            send_sem=f_send.at[h, slot], recv_sem=f_recv.at[h, slot],
            device_id={"seq": ring(CHAIN_WAY if long else -CHAIN_WAY)}, device_id_type=MESH,
        )

    def chain_hop(h, k, long):
        hops = 4 if long else 3
        base = 0 if long else 4
        if k >= 0:
            chain_copy(h, k, long).wait_recv()
        if k == hops - 1:
            return
        way = CHAIN_WAY if long else -CHAIN_WAY
        values = share(part_f, ring(way * (hops - 1 - k)), h)
        if k >= 0:
            values = add(values, read(recv_f, h, base + k))
        write(sent_f, h, base + k + 1, values)
        chain_copy(h, k + 1, long).start()

    def pair_start(h):
        for slot, offset in ((0, 4), (1, 2), (2, -3), (3, -1)):
            pair_send(h, slot, offset)

    def pair_end(h):
        values = share(part_f, me, h)
        for slot in (3, 6) if h == 0 else (3, 4, 5, 6):
            if h:
                pair_copy(h, slot).wait_recv()
            values = add(values, read(recv_f, h, slot))
        for (rows, lanes), value in zip(lines_of, values):
            part_f[me, h, rows, lanes] = value
        for o in (1, 2, 3):
            back_copy(h, o).start()
        here = pl.multiple_of(batch * 8, 8)
        back[pl.ds(pl.multiple_of((HALF * h + batch) * 8, 8), 8), :] = part_f[
            me, h, pl.ds(here, 8), :
        ]

    def batch_copy(h, o):
        return pltpu.make_async_remote_copy(
            src_ref=dh_sent.at[h, o - 1], dst_ref=dh_recv.at[h, o - 1],
            send_sem=y_send.at[h, o - 1], recv_sem=y_recv.at[h, o - 1],
            device_id={"dp": peer(o)}, device_id_type=MESH,
        )

    tiles = [(pl.ds(16 * r, 16), pl.ds(128 * n, 128)) for r in range(ROWS // 16) for n in range(4)]

    def batch_send(h):
        for o in (1, 2, 3):

            def body(index, carry):
                def put(b, code):
                    dh_sent[h, o - 1, index, b] = code

                def put_top(top):
                    dh_sent[h, o - 1, index, 16] = top

                other = peer(o)
                encode([dh[h, other, index, rows, lanes] for rows, lanes in tiles], put, put_top)
                return carry

            lax.fori_loop(0, 2, body, 0)
            batch_copy(h, o).start()

    def batch_sum(h):
        for o in (1, 2, 3):
            batch_copy(h, o).wait_recv()

        def body(index, carry):
            for o in (1, 2, 3):
                codes = [dh_recv[h, o - 1, index, b] for b in range(16)]
                for (rows, lanes), value in zip(tiles, decode(codes, dh_recv[h, o - 1, index, 16])):
                    dh[h, batch, index, rows, lanes] += value
            return carry

        lax.fori_loop(0, 2, body, 0)
        values = [
            (
                dh[h, batch, 0, :, e * LANES : (e + 1) * LANES],
                dh[h, batch, 1, :, e * LANES : (e + 1) * LANES],
            )
            for e in range(4)
        ]
        for a, (real, imag) in enumerate(quarters(values, False)):
            put_split(zf, a, slice(0, ROWS), real, imag)

    def filter_part(h):
        batch_sum(h)
        columns(zf, yf, True)
        finish(yf, 0, u_f, part_f, h)

    def back_copy(h, o):
        there = pl.multiple_of(peer(o) * 8, 8)
        return pltpu.make_async_remote_copy(
            src_ref=part_f.at[me, h, pl.ds(there, 8), :],
            dst_ref=back.at[pl.ds(pl.multiple_of((HALF * h + batch) * 8, 8), 8), :],
            send_sem=b_send.at[h, o - 1], recv_sem=b_recv.at[h, o - 1],
            device_id={"dp": peer(o)}, device_id_type=MESH,
        )

    waited = set()

    def need(*indices):
        for index in indices:
            if index not in waited:
                waited.add(index)
                loads[index].wait()

    def run(kind, q, k=None):
        if kind == "gs":
            gather_start(q)
        elif kind in ("gl", "gr"):
            gather_hop(q, k, kind == "gl")
        elif kind == "A":
            need(0, 1)
            stage_a(q)
        elif kind == "B":
            need(2)
            columns(zb.at[q], yb.at[q], False)
        elif kind == "C":
            need(3, 4)
            products(q)
        elif kind == "Y":
            batch_send(q)
        elif kind == "D":
            columns(db.at[q], vb.at[q], True)
        elif kind == "UE":
            need(5)
            finish(vb.at[q // HALF], q % HALF, u.at[q % HALF], part, q)
        elif kind in ("Rl", "Rr"):
            reduce_hop(q, k, kind == "Rl")
        elif kind == "X":
            reduce_end(q)
        elif kind == "F":
            filter_part(q)
        elif kind == "Fs" and q == 0:
            chain_hop(q, -1, True)
            chain_hop(q, -1, False)
        elif kind in ("Fl", "Fr"):
            chain_hop(q, k, kind == "Fl")
        elif kind == "Fs":
            pair_start(q)
        elif kind == "Fa":
            pair_send(q, 4, 3, 0)
        elif kind == "Fb":
            pair_send(q, 5, 1, 1)
        elif kind == "Fc":
            pair_send(q, 6, -2, 2)
        elif kind == "Fend":
            pair_end(q)

    for task in ORDER:
        run(*task)

    rows = jnp.concatenate([xf[n].astype(BF16) for n in range(4)], axis=1)
    rows = jnp.dot(rows, shuffle[1], preferred_element_type=F32)
    for n in range(4):
        xf[n] = rows[:, n * 128 : (n + 1) * 128]

    def collect(j, carry):
        for n in range(4):
            lanes = pl.ds(pl.multiple_of(j * COLS + n * 128, 128), 128)
            in_ref[0, :, lanes] = xf[n, pl.ds(j, CH, stride=TIMES), :].astype(BF16)
        return carry

    lax.fori_loop(0, TIMES, collect, 0)

    for h in range(2):
        for o in (1, 2, 3):
            back_copy(h, o).wait_recv()
    high, low = split(back[...])
    rest = (back[...] - high.astype(F32) - low.astype(F32)).astype(BF16)
    lines = sum(
        jnp.dot(item, shuffle[1], preferred_element_type=F32) for item in (rest, low, high)
    )
    for n in range(4):
        xf[n, 0:64, :] = lines[:, n * 128 : (n + 1) * 128]
        for j in range(8):
            start = j * COLS + n * 128
            fl_ref[:, start : start + 128] = xf[n, pl.ds(j, CH, stride=8), :]

    for q in range(CH):
        for k in range(4):
            gather_copy(q, k, True).wait_send()
            reduce_copy(q, k, True).wait_send()
            if k < 3:
                gather_copy(q, k, False).wait_send()
                reduce_copy(q, k, False).wait_send()
    for h in range(2):
        for slot in range(7):
            if h:
                pair_copy(h, slot).wait_send()
            else:
                chain_copy(h, slot % 4, slot < 4).wait_send()
        for o in (1, 2, 3):
            batch_copy(h, o).wait_send()
            back_copy(h, o).wait_send()


def hand_on(in_a, in_b, out_a, out_b):
    out_a[...] = in_a[...]
    out_b[...] = in_b[...]


def on_device(grad_out, input_spectrum, filter_spectrum):
    wide, first, last, twist, shuffle = (jnp.asarray(t) for t in tables())
    vmem = pl.BlockSpec(memory_space=pltpu.VMEM)
    anywhere = pl.BlockSpec(memory_space=pl.ANY)
    dma = pltpu.SemaphoreType.DMA
    out_shape = (
        jax.ShapeDtypeStruct((1, CH, TIMES * COLS), BF16),
        jax.ShapeDtypeStruct((CH, TIMES * COLS // BATCHES), F32),
    )
    results = pl.pallas_call(
        kernel,
        out_shape=out_shape,
        in_specs=[vmem] + [anywhere] * 7,
        out_specs=(vmem, vmem),
        scratch_shapes=[
            pltpu.VMEM((8, 768, 256), BF16),
            pltpu.VMEM((256, 256), BF16),
            pltpu.VMEM((256, 384), BF16),
            pltpu.VMEM((2, ROWS, COLS), F32),
            pltpu.VMEM((2, COLS, COLS), BF16),
            pltpu.VMEM((2, CH, ROWS, COLS), F32),
            pltpu.VMEM((2, CH, ROWS, COLS), F32),
            pltpu.VMEM((4, CH * TIMES, 128), F32),
            pltpu.VMEM((CH, SHARDS * TIMES, COLS), BF16),
            pltpu.VMEM((2, 4, HALF * ROWS, 768), BF16),
            pltpu.VMEM((2, 4, HALF * ROWS, 256), F32),
            pltpu.VMEM((2, 4, HALF * ROWS, 768), BF16),
            pltpu.VMEM((2, 4, HALF * ROWS, 256), F32),
            pltpu.VMEM((HALF, 384, COLS), BF16),
            pltpu.VMEM((SHARDS, CH, TIMES, COLS), F32),
            pltpu.VMEM((CH, 7, 9, 16, 128), BF16),
            pltpu.VMEM((2, BATCHES, 2, ROWS, COLS), F32),
            pltpu.VMEM((2, 3, 2, 17, 16, 128), BF16),
            pltpu.VMEM((2, 3, 2, 17, 16, 128), BF16),
            pltpu.VMEM((4, ROWS, 768), BF16),
            pltpu.VMEM((4, ROWS, 256), F32),
            pltpu.VMEM((384, COLS), BF16),
            pltpu.VMEM((SHARDS, 2, TIMES, COLS), F32),
            pltpu.VMEM((2, 7, 9, 16, 128), BF16),
            pltpu.VMEM((CH * 8, COLS), F32),
            pltpu.VMEM((CH, 7, 9, 16, 128), BF16),
            pltpu.VMEM((2, 7, 9, 16, 128), BF16),
            dma((7,)),
            dma((CH, 7)), dma((CH, 7)),
            dma((CH, 7)), dma((CH, 7)),
            dma((2, 3)), dma((2, 3)),
            dma((2, 7)), dma((2, 7)),
            dma((2, 3)), dma((2, 3)),
        ],
        compiler_params=pltpu.CompilerParams(
            collective_id=0, has_side_effects=True, vmem_limit_bytes=56 * 1024 * 1024
        ),
    )(grad_out, input_spectrum, filter_spectrum, wide, first, last, twist, shuffle)
    return pl.pallas_call(
        hand_on,
        out_shape=out_shape,
        in_specs=[vmem] * 2,
        out_specs=(vmem,) * 2,
    )(*results)


def solution(mesh):
    in_specs = (
        P("dp", "chan", "seq"),
        P("dp", None, "chan", "seq", None),
        P(None, "chan", "seq", None),
    )
    out_specs = (P("dp", "chan", "seq"), P("chan", ("seq", "dp")))
    return jax.shard_map(
        on_device, mesh=mesh, in_specs=in_specs, out_specs=out_specs, check_vma=False
    )
```

```python
import functools

import jax
import jax.numpy as jnp
import numpy as np
from jax import lax
from jax.experimental import pallas as pl
from jax.experimental.pallas import tpu as pltpu
from jax.sharding import PartitionSpec as P

MESH = pl.DeviceIdType.MESH
F32 = jnp.float32
BF16 = jnp.bfloat16

SHARDS = 8
BATCHES = 4
CH = 8
HALF = 4
ROWS = 64
COLS = 512
BINS = 512
TIMES = 32
MODULUS = BINS * COLS
LANES = 128
NEAR = (1, -1, 2, -2, 3, -3)
CHAIN_WAY = -1
LONG_WAY = (1, 1, 1, 1, -1, -1, -1, -1)
ORDER = (
    ("gs", 0), ("gs", 1), ("gs", 2), ("gs", 3), ("gl", 0, 0), ("gr", 0, 0), ("gl", 1, 0),
    ("gr", 1, 0), ("gl", 2, 0), ("gr", 2, 0), ("gl", 3, 0), ("gr", 3, 0), ("gl", 0, 1),
    ("gr", 0, 1), ("gl", 1, 1), ("gr", 1, 1), ("gl", 2, 1), ("gr", 2, 1), ("gl", 3, 1), ("gs", 5),
    ("gr", 3, 1), ("gl", 0, 2), ("gr", 0, 2), ("gl", 1, 2), ("gr", 1, 2), ("gs", 4), ("gs", 7),
    ("gl", 2, 2), ("gr", 2, 2), ("gl", 3, 2), ("gs", 6), ("gl", 5, 0), ("gr", 5, 0), ("gr", 3, 2),
    ("gl", 0, 3), ("A", 0), ("gl", 4, 0), ("gl", 1, 3), ("A", 1), ("gl", 7, 0), ("gr", 4, 0),
    ("gl", 6, 0), ("gr", 7, 0), ("gl", 5, 1), ("gl", 2, 3), ("A", 2), ("gl", 4, 1), ("gl", 3, 3),
    ("A", 3), ("B", 0), ("gl", 6, 1), ("gr", 6, 0), ("gl", 7, 1), ("gr", 5, 1), ("C", 0),
    ("gl", 5, 2), ("gr", 4, 1), ("Y", 0), ("gl", 4, 2), ("D", 0), ("gr", 7, 1), ("UE", 0),
    ("gl", 6, 2), ("gr", 6, 1), ("Rl", 0, -1), ("Rr", 0, -1), ("UE", 1), ("gl", 7, 2),
    ("gr", 5, 2), ("Rl", 1, -1), ("Rr", 1, -1), ("UE", 2), ("gl", 5, 3), ("Rl", 2, -1),
    ("Rr", 2, -1), ("gr", 4, 2), ("A", 5), ("gl", 4, 3), ("A", 4), ("gr", 7, 2), ("UE", 3),
    ("gl", 6, 3), ("gr", 6, 2), ("Rl", 3, -1), ("Rr", 3, -1), ("A", 6), ("Rr", 0, 0), ("Rl", 0, 0),
    ("gl", 7, 3), ("A", 7), ("Rl", 1, 0), ("B", 1), ("Rr", 1, 0), ("Rl", 2, 0), ("C", 1),
    ("Rl", 3, 0), ("Rr", 2, 0), ("Rr", 3, 0), ("Y", 1), ("Rl", 0, 1), ("F", 0), ("Rr", 0, 1),
    ("Rl", 1, 1), ("Rr", 1, 1), ("Rl", 2, 1), ("Fs", 0), ("D", 1), ("Rl", 3, 1), ("Rr", 2, 1),
    ("Rl", 0, 2), ("Rr", 3, 1), ("UE", 4), ("Rl", 4, -1), ("Rr", 4, -1), ("UE", 5), ("Rl", 1, 2),
    ("Rl", 5, -1), ("Rr", 5, -1), ("Rr", 0, 2), ("UE", 6), ("Rl", 2, 2), ("Rl", 6, -1),
    ("Rr", 6, -1), ("UE", 7), ("Fl", 0, 0), ("Fr", 0, 0), ("Rl", 7, -1), ("Rr", 7, -1),
    ("Rr", 1, 2), ("Rl", 3, 2), ("Rr", 2, 2), ("Rr", 3, 2), ("Rl", 0, 3), ("X", 0), ("Rl", 4, 0),
    ("F", 1), ("Fs", 1), ("Rl", 6, 0), ("Rr", 4, 0), ("Rl", 5, 0), ("Rr", 5, 0), ("Rl", 1, 3),
    ("Fl", 0, 1), ("Rl", 2, 3), ("X", 1), ("X", 2), ("Rl", 7, 0), ("Rr", 6, 0), ("Rl", 4, 1),
    ("Fr", 0, 1), ("Fc", 1), ("Rr", 7, 0), ("Rl", 3, 3), ("X", 3), ("Rl", 6, 1), ("Fa", 1),
    ("Rl", 5, 1), ("Fb", 1), ("Fl", 0, 2), ("Rr", 4, 1), ("Rl", 7, 1), ("Rr", 5, 1), ("Rl", 4, 2),
    ("Rr", 6, 1), ("Fr", 0, 2), ("Rr", 7, 1), ("Rl", 6, 2), ("Rl", 5, 2), ("Fl", 0, 3),
    ("Fend", 0), ("Rl", 7, 2), ("Fend", 1), ("Rl", 4, 3), ("Rr", 4, 2), ("X", 4), ("Rl", 6, 3),
    ("Rr", 5, 2), ("Rl", 5, 3), ("Rr", 6, 2), ("X", 5), ("X", 6), ("Rl", 7, 3), ("Rr", 7, 2),
    ("X", 7),
)


def split_table(table):
    high = table.astype(np.float32).astype(jnp.bfloat16)
    low = (table - high.astype(np.float64)).astype(np.float32).astype(jnp.bfloat16)
    return high, low


@functools.cache
def tables():
    turn = 2.0 * np.pi
    fold = np.arange(LANES)
    forward, inverse = [], []
    for a in range(4):
        angle = turn * (np.outer(4 * fold + a, fold) % COLS) / COLS
        c, s = np.cos(angle), np.sin(angle)
        for group, block in (
            (forward, np.block([[c, -s], [s, c]])),
            (inverse, np.block([[c.T, s.T], [-s.T, c.T]])),
        ):
            high, low = split_table(block)
            group.append(np.concatenate([high, high, low], axis=0))
    wide = np.stack(forward + inverse)
    place = np.arange(COLS)
    order = 4 * (place % LANES) + place // LANES
    shuffle = np.zeros((COLS, COLS), np.float32)
    shuffle[order, place] = 1.0
    shuffle = np.stack([shuffle, shuffle.T]).astype(jnp.bfloat16)
    half = BINS // 2
    time_angle = turn * (np.outer(np.arange(BINS), np.arange(half)) % BINS) / BINS
    cos_t = np.cos(time_angle).reshape(SHARDS, ROWS, half)
    sin_t = np.sin(time_angle).reshape(SHARDS, ROWS, half)
    first = np.concatenate([cos_t, -sin_t], axis=1)
    first_high, first_low = split_table(first)
    first_table = np.concatenate([first_high, first_low], axis=1)
    last = np.concatenate([cos_t, -sin_t], axis=1).transpose(0, 2, 1) / MODULUS
    last_high, last_low = split_table(last)
    last_table = np.concatenate([last_high, last_high, last_low], axis=2)
    twist = turn * np.outer(np.arange(BINS), np.arange(COLS)) / MODULUS
    twist_table = np.stack(
        [np.cos(twist).reshape(SHARDS, ROWS, COLS), np.sin(twist).reshape(SHARDS, ROWS, COLS)],
        axis=1,
    ).astype(np.float32)[..., order]
    return wide, first_table, last_table, twist_table, shuffle


SPAN = 124.0
GAIN = 2.0 ** (2.0 * SPAN / 32.0) - 1.0
FLOOR = 2.0 ** (-SPAN / 32.0)


def encode(values, put, put_top):
    top = jnp.abs(values[0])
    for value in values[1:]:
        top = jnp.maximum(top, jnp.abs(value))
    top = (jnp.maximum(top, 1e-30) * 1.01).astype(BF16)
    put_top(top)
    slope = (GAIN * FLOOR) / top.astype(F32)
    for index, value in enumerate(values):
        level = jnp.abs(value) * slope + FLOOR
        for _ in range(5):
            level = level * level
        put(index, jnp.where(value < 0.0, -level, level).astype(BF16))


def decode(codes, top):
    unit = top.astype(F32) * (1.0 / GAIN)
    slope = unit * (1.0 / FLOOR)
    values = []
    for code in codes:
        wide_code = code.astype(F32)
        level = jnp.exp2(jnp.log2(jnp.abs(wide_code)) * (1.0 / 32.0))
        value = level * slope - unit
        values.append(jnp.where(wide_code < 0.0, -value, value))
    return values


def split(value):
    high = value.astype(BF16)
    low = (value - high.astype(F32)).astype(BF16)
    return high, low


def kernel(
    x_hbm, xs_hbm, hs_hbm, wide_hbm, first_hbm, last_hbm, twist_hbm, shuffle_hbm,
    in_ref, fl_ref,
    x_ref, wide, first, last, twist, shuffle, xs, hs, xf, xg, zb, yb, db, vb, u, part, recv, dh, dh_sent, dh_recv,
    zf, yf, u_f, part_f, recv_f, back, sent, sent_f, load_sem, ag_send, ag_recv, rs_send, rs_recv, y_send, y_recv,
    f_send, f_recv, b_send, b_recv,
):
    me = lax.axis_index("seq")
    batch = lax.axis_index("dp")

    def ring(offset):
        return lax.rem(me + (offset + SHARDS), SHARDS)

    def peer(offset):
        return lax.rem(batch + offset, BATCHES)

    barrier = pltpu.get_barrier_semaphore()
    for offset in NEAR:
        pl.semaphore_signal(barrier, inc=1, device_id={"seq": ring(offset)}, device_id_type=MESH)
    for offset in (1, 2, 3):
        pl.semaphore_signal(barrier, inc=1, device_id={"dp": peer(offset)}, device_id_type=MESH)

    loads = [
        pltpu.make_async_copy(first_hbm.at[me], first, load_sem.at[0]),
        pltpu.make_async_copy(twist_hbm.at[me], twist, load_sem.at[1]),
        pltpu.make_async_copy(wide_hbm, wide, load_sem.at[2]),
        pltpu.make_async_copy(hs_hbm, hs, load_sem.at[3]),
        pltpu.make_async_copy(xs_hbm.at[0], xs, load_sem.at[4]),
        pltpu.make_async_copy(last_hbm.at[me], last, load_sem.at[5]),
        pltpu.make_async_copy(shuffle_hbm, shuffle, load_sem.at[6]),
        pltpu.make_async_copy(x_hbm, x_ref, load_sem.at[7]),
    ]
    for index in (7, 6, 0, 1, 2, 3, 4, 5):
        loads[index].start()
    loads[7].wait()

    def spread(j, carry):
        for n in range(4):
            lanes = pl.ds(pl.multiple_of(j * COLS + n * 128, 128), 128)
            xf[n, pl.ds(j, CH, stride=TIMES), :] = x_ref[0, :, lanes].astype(F32)
        return carry

    lax.fori_loop(0, TIMES, spread, 0)
    mine = pl.multiple_of(me * TIMES, TIMES)
    loads[6].wait()
    rows = jnp.concatenate([xf[n].astype(BF16) for n in range(4)], axis=1)
    rows = jnp.dot(rows, shuffle[0], preferred_element_type=F32).astype(BF16)
    for c in range(CH):
        xg[c, pl.ds(mine, TIMES), :] = rows[c * TIMES : (c + 1) * TIMES, :]

    pl.semaphore_wait(barrier, len(NEAR) + 3)

    def gather_copy(q, k, long):
        way = LONG_WAY[q] if long else -LONG_WAY[q]
        source = pl.multiple_of(ring(-way * k) * TIMES, TIMES)
        block = xg.at[q, pl.ds(source, TIMES), :]
        slot = k if long else 4 + k
        return pltpu.make_async_remote_copy(
            src_ref=block, dst_ref=block, send_sem=ag_send.at[q, slot], recv_sem=ag_recv.at[q, slot],
            device_id={"seq": ring(way)}, device_id_type=MESH,
        )

    def gather_start(q):
        gather_copy(q, 0, True).start()
        gather_copy(q, 0, False).start()

    def gather_hop(q, k, long):
        gather_copy(q, k, long).wait_recv()
        if k < (3 if long else 2):
            gather_copy(q, k + 1, long).start()

    def put_split(dest, a, rows, real, imag):
        for index, value in enumerate((real, imag)):
            high, low = split(value)
            for place, item in ((0, high), (2, low), (4, high)):
                lane = (place + index) * LANES
                dest[a, rows, lane : lane + LANES] = item

    def stage_a(q):
        h, c = divmod(q, HALF)
        t = jnp.dot(first[...], xg[q], preferred_element_type=F32)
        real = t[0:64] + t[128:192]
        imag = t[64:128] + t[192:256]
        rows = slice(c * ROWS, (c + 1) * ROWS)
        for a in range(4):
            lanes = slice(a * LANES, (a + 1) * LANES)
            tc, ts = twist[0, :, lanes], twist[1, :, lanes]
            ar, ai = real[:, lanes], imag[:, lanes]
            put_split(zb.at[h], a, rows, ar * tc + ai * ts, ai * tc - ar * ts)

    def columns(source, dest, inverse):
        for a in range(4):
            weight = wide[a + 4] if inverse else wide[a]
            dest[a] = jnp.dot(source[a], weight, preferred_element_type=F32)

    def quarters(values, forward):
        (r0, i0), (r1, i1), (r2, i2), (r3, i3) = values
        sr, si, dr, di = r0 + r2, i0 + i2, r0 - r2, i0 - i2
        tr, ti, er, ei = r1 + r3, i1 + i3, r1 - r3, i1 - i3
        left = (dr + ei, di - er)
        right = (dr - ei, di + er)
        if not forward:
            left, right = right, left
        return [(sr + tr, si + ti), left, (sr - tr, si - ti), right]

    def products(h):
        def body(c, carry):
            rows = pl.ds(pl.multiple_of(c * ROWS, ROWS), ROWS)
            bins = quarters(
                [(yb[h, a, rows, 0:LANES], yb[h, a, rows, LANES : 2 * LANES]) for a in range(4)],
                True,
            )
            channel = HALF * h + c
            inner = []
            for e, (gr, gi) in enumerate(bins):
                lanes = slice(e * LANES, (e + 1) * LANES)
                hr, hi_ = hs[0, channel, :, lanes], hs[1, channel, :, lanes]
                inner.append((gr * hr + gi * hi_, gi * hr - gr * hi_))
                xr, xi = xs[0, channel, :, lanes], xs[1, channel, :, lanes]
                dh[h, c, 0, :, lanes] = gr * xr + gi * xi
                dh[h, c, 1, :, lanes] = gi * xr - gr * xi
            for a, (real, imag) in enumerate(quarters(inner, False)):
                put_split(db.at[h], a, rows, real, imag)
            return carry

        lax.fori_loop(0, HALF, body, 0)

    def finish(source, c, buffer, dest, channel):
        rows = slice(c * ROWS, (c + 1) * ROWS)
        for a in range(4):
            lanes = slice(a * LANES, (a + 1) * LANES)
            vr, vi = source[a, rows, 0:LANES], source[a, rows, LANES : 2 * LANES]
            tc, ts = twist[0, :, lanes], twist[1, :, lanes]
            for index, value in enumerate((vr * tc - vi * ts, vi * tc + vr * ts)):
                high, low = split(value)
                buffer[64 * index : 64 * index + 64, lanes] = high
                buffer[128 + 64 * index : 192 + 64 * index, lanes] = low
                buffer[256 + 64 * index : 320 + 64 * index, lanes] = high
        y = jnp.dot(last[...], buffer[...], preferred_element_type=F32)
        dest[:, channel] = y.reshape(SHARDS, TIMES, COLS)

    def share(part_ref, dest, c):
        return [part_ref[dest, c, rows, lanes] for rows, lanes in lines_of]

    lines_of = [
        (pl.ds(16 * r, 16), pl.ds(128 * n, 128)) for r in range(TIMES // 16) for n in range(4)
    ]

    def read(ref, q, slot):
        return decode([ref[q, slot, b] for b in range(8)], ref[q, slot, 8])

    def write(ref, q, slot, values):
        def put(index, code):
            ref[q, slot, index] = code

        def put_top(top):
            ref[q, slot, 8] = top

        encode(values, put, put_top)

    def add(left, right):
        return [a + b for a, b in zip(left, right)]

    def reduce_copy(q, k, long):
        slot = k if long else 4 + k
        way = LONG_WAY[q] if long else -LONG_WAY[q]
        return pltpu.make_async_remote_copy(
            src_ref=sent.at[q, slot], dst_ref=recv.at[q, slot],
            send_sem=rs_send.at[q, slot], recv_sem=rs_recv.at[q, slot],
            device_id={"seq": ring(way)}, device_id_type=MESH,
        )

    def reduce_hop(q, k, long):
        hops = 4 if long else 3
        way = LONG_WAY[q] if long else -LONG_WAY[q]
        base = 0 if long else 4
        if k >= 0:
            reduce_copy(q, k, long).wait_recv()
        if k == hops - 1:
            return
        values = share(part, ring(way * (hops - 1 - k)), q)
        if k >= 0:
            values = add(values, read(recv, q, base + k))
        write(sent, q, base + k + 1, values)
        reduce_copy(q, k + 1, long).start()

    def gather_sent(q):
        for k in range(7):
            gather_copy(q, k % 4, k < 4).wait_send()

    def reduce_end(q):
        for k in range(7):
            reduce_copy(q, k % 4, k < 4).wait_send()
        values = add(share(part, me, q), add(read(recv, q, 3), read(recv, q, 6)))
        for (rows, lanes), value in zip(lines_of, values):
            xf[lanes.start // 128, q * TIMES + rows.start : q * TIMES + rows.start + 16, :] = value

    def pair_copy(h, slot):
        way = 1 if h else -1
        return pltpu.make_async_remote_copy(
            src_ref=sent_f.at[h, slot], dst_ref=recv_f.at[h, slot],
            send_sem=f_send.at[h, slot], recv_sem=f_recv.at[h, slot],
            device_id={"seq": ring(way * (1, 1, -1, -1, 3, 1, -2)[slot])}, device_id_type=MESH,
        )

    def pair_send(h, slot, offset, arrived=None):
        values = share(part_f, ring(offset * (1 if h else -1)), h)
        if arrived is not None:
            pair_copy(h, arrived).wait_recv()
            values = add(values, read(recv_f, h, arrived))
        write(sent_f, h, slot, values)
        pair_copy(h, slot).start()

    def chain_copy(h, k, long):
        slot = k if long else 4 + k
        return pltpu.make_async_remote_copy(
            src_ref=sent_f.at[h, slot], dst_ref=recv_f.at[h, slot],
            send_sem=f_send.at[h, slot], recv_sem=f_recv.at[h, slot],
            device_id={"seq": ring(CHAIN_WAY if long else -CHAIN_WAY)}, device_id_type=MESH,
        )

    def chain_hop(h, k, long):
        hops = 4 if long else 3
        base = 0 if long else 4
        if k >= 0:
            chain_copy(h, k, long).wait_recv()
        if k == hops - 1:
            return
        way = CHAIN_WAY if long else -CHAIN_WAY
        values = share(part_f, ring(way * (hops - 1 - k)), h)
        if k >= 0:
            values = add(values, read(recv_f, h, base + k))
        write(sent_f, h, base + k + 1, values)
        chain_copy(h, k + 1, long).start()

    def pair_start(h):
        for slot, offset in ((0, 4), (1, 2), (2, -3), (3, -1)):
            pair_send(h, slot, offset)

    def pair_end(h):
        values = share(part_f, me, h)
        for slot in (3, 6) if h == 0 else (3, 4, 5, 6):
            if h:
                pair_copy(h, slot).wait_recv()
            values = add(values, read(recv_f, h, slot))
        for (rows, lanes), value in zip(lines_of, values):
            part_f[me, h, rows, lanes] = value
        for o in (1, 2, 3):
            back_copy(h, o).start()
        for o in (1, 2, 3):
            batch_copy(h, o).wait_send()
        for slot in range(7):
            if h:
                pair_copy(h, slot).wait_send()
            else:
                chain_copy(h, slot % 4, slot < 4).wait_send()
        here = pl.multiple_of(batch * 8, 8)
        back[pl.ds(pl.multiple_of((HALF * h + batch) * 8, 8), 8), :] = part_f[
            me, h, pl.ds(here, 8), :
        ]

    def batch_copy(h, o):
        return pltpu.make_async_remote_copy(
            src_ref=dh_sent.at[h, o - 1], dst_ref=dh_recv.at[h, o - 1],
            send_sem=y_send.at[h, o - 1], recv_sem=y_recv.at[h, o - 1],
            device_id={"dp": peer(o)}, device_id_type=MESH,
        )

    tiles = [(pl.ds(16 * r, 16), pl.ds(128 * n, 128)) for r in range(ROWS // 16) for n in range(4)]

    def batch_send(h):
        for o in (1, 2, 3):

            def body(index, carry):
                def put(b, code):
                    dh_sent[h, o - 1, index, b] = code

                def put_top(top):
                    dh_sent[h, o - 1, index, 16] = top

                other = peer(o)
                encode([dh[h, other, index, rows, lanes] for rows, lanes in tiles], put, put_top)
                return carry

            lax.fori_loop(0, 2, body, 0)
            batch_copy(h, o).start()

    def batch_sum(h):
        for o in (1, 2, 3):
            batch_copy(h, o).wait_recv()

        def body(index, carry):
            for o in (1, 2, 3):
                codes = [dh_recv[h, o - 1, index, b] for b in range(16)]
                for (rows, lanes), value in zip(tiles, decode(codes, dh_recv[h, o - 1, index, 16])):
                    dh[h, batch, index, rows, lanes] += value
            return carry

        lax.fori_loop(0, 2, body, 0)
        values = [
            (
                dh[h, batch, 0, :, e * LANES : (e + 1) * LANES],
                dh[h, batch, 1, :, e * LANES : (e + 1) * LANES],
            )
            for e in range(4)
        ]
        for a, (real, imag) in enumerate(quarters(values, False)):
            put_split(zf, a, slice(0, ROWS), real, imag)

    def filter_part(h):
        batch_sum(h)
        columns(zf, yf, True)
        finish(yf, 0, u_f, part_f, h)

    def back_copy(h, o):
        there = pl.multiple_of(peer(o) * 8, 8)
        return pltpu.make_async_remote_copy(
            src_ref=part_f.at[me, h, pl.ds(there, 8), :],
            dst_ref=back.at[pl.ds(pl.multiple_of((HALF * h + batch) * 8, 8), 8), :],
            send_sem=b_send.at[h, o - 1], recv_sem=b_recv.at[h, o - 1],
            device_id={"dp": peer(o)}, device_id_type=MESH,
        )

    waited = set()

    def need(*indices):
        for index in indices:
            if index not in waited:
                waited.add(index)
                loads[index].wait()

    def run(kind, q, k=None):
        if kind == "gs":
            gather_start(q)
        elif kind in ("gl", "gr"):
            gather_hop(q, k, kind == "gl")
        elif kind == "A":
            need(0, 1)
            stage_a(q)
        elif kind == "B":
            need(2)
            columns(zb.at[q], yb.at[q], False)
        elif kind == "C":
            need(3, 4)
            products(q)
        elif kind == "Y":
            batch_send(q)
        elif kind == "D":
            columns(db.at[q], vb.at[q], True)
        elif kind == "UE":
            need(5)
            finish(vb.at[q // HALF], q % HALF, u.at[q % HALF], part, q)
            gather_sent(q)
        elif kind in ("Rl", "Rr"):
            reduce_hop(q, k, kind == "Rl")
        elif kind == "X":
            reduce_end(q)
        elif kind == "F":
            filter_part(q)
        elif kind == "Fs" and q == 0:
            chain_hop(q, -1, True)
            chain_hop(q, -1, False)
        elif kind in ("Fl", "Fr"):
            chain_hop(q, k, kind == "Fl")
        elif kind == "Fs":
            pair_start(q)
        elif kind == "Fa":
            pair_send(q, 4, 3, 0)
        elif kind == "Fb":
            pair_send(q, 5, 1, 1)
        elif kind == "Fc":
            pair_send(q, 6, -2, 2)
        elif kind == "Fend":
            pair_end(q)

    for task in ORDER:
        run(*task)

    rows = jnp.concatenate([xf[n].astype(BF16) for n in range(4)], axis=1)
    rows = jnp.dot(rows, shuffle[1], preferred_element_type=F32)
    for n in range(4):
        xf[n] = rows[:, n * 128 : (n + 1) * 128]

    def collect(j, carry):
        for n in range(4):
            lanes = pl.ds(pl.multiple_of(j * COLS + n * 128, 128), 128)
            in_ref[0, :, lanes] = xf[n, pl.ds(j, CH, stride=TIMES), :].astype(BF16)
        return carry

    lax.fori_loop(0, TIMES, collect, 0)

    for h in range(2):
        for o in (1, 2, 3):
            back_copy(h, o).wait()
    high, low = split(back[...])
    rest = (back[...] - high.astype(F32) - low.astype(F32)).astype(BF16)
    lines = sum(
        jnp.dot(item, shuffle[1], preferred_element_type=F32) for item in (rest, low, high)
    )
    for n in range(4):
        xf[n, 0:64, :] = lines[:, n * 128 : (n + 1) * 128]
        for j in range(8):
            start = j * COLS + n * 128
            fl_ref[:, start : start + 128] = xf[n, pl.ds(j, CH, stride=8), :]


def hand_on(in_a, in_b, out_a, out_b):
    out_a[...] = in_a[...]
    out_b[...] = in_b[...]


def on_device(grad_out, input_spectrum, filter_spectrum):
    wide, first, last, twist, shuffle = (jnp.asarray(t) for t in tables())
    vmem = pl.BlockSpec(memory_space=pltpu.VMEM)
    anywhere = pl.BlockSpec(memory_space=pl.ANY)
    dma = pltpu.SemaphoreType.DMA
    out_shape = (
        jax.ShapeDtypeStruct((1, CH, TIMES * COLS), BF16),
        jax.ShapeDtypeStruct((CH, TIMES * COLS // BATCHES), F32),
    )
    results = pl.pallas_call(
        kernel,
        out_shape=out_shape,
        in_specs=[anywhere] * 8,
        out_specs=(vmem, vmem),
        scratch_shapes=[
            pltpu.VMEM((1, CH, TIMES * COLS), BF16),
            pltpu.VMEM((8, 768, 256), BF16),
            pltpu.VMEM((256, 256), BF16),
            pltpu.VMEM((256, 384), BF16),
            pltpu.VMEM((2, ROWS, COLS), F32),
            pltpu.VMEM((2, COLS, COLS), BF16),
            pltpu.VMEM((2, CH, ROWS, COLS), F32),
            pltpu.VMEM((2, CH, ROWS, COLS), F32),
            pltpu.VMEM((4, CH * TIMES, 128), F32),
            pltpu.VMEM((CH, SHARDS * TIMES, COLS), BF16),
            pltpu.VMEM((2, 4, HALF * ROWS, 768), BF16),
            pltpu.VMEM((2, 4, HALF * ROWS, 256), F32),
            pltpu.VMEM((2, 4, HALF * ROWS, 768), BF16),
            pltpu.VMEM((2, 4, HALF * ROWS, 256), F32),
            pltpu.VMEM((HALF, 384, COLS), BF16),
            pltpu.VMEM((SHARDS, CH, TIMES, COLS), F32),
            pltpu.VMEM((CH, 7, 9, 16, 128), BF16),
            pltpu.VMEM((2, BATCHES, 2, ROWS, COLS), F32),
            pltpu.VMEM((2, 3, 2, 17, 16, 128), BF16),
            pltpu.VMEM((2, 3, 2, 17, 16, 128), BF16),
            pltpu.VMEM((4, ROWS, 768), BF16),
            pltpu.VMEM((4, ROWS, 256), F32),
            pltpu.VMEM((384, COLS), BF16),
            pltpu.VMEM((SHARDS, 2, TIMES, COLS), F32),
            pltpu.VMEM((2, 7, 9, 16, 128), BF16),
            pltpu.VMEM((CH * 8, COLS), F32),
            pltpu.VMEM((CH, 7, 9, 16, 128), BF16),
            pltpu.VMEM((2, 7, 9, 16, 128), BF16),
            dma((8,)),
            dma((CH, 7)), dma((CH, 7)),
            dma((CH, 7)), dma((CH, 7)),
            dma((2, 3)), dma((2, 3)),
            dma((2, 7)), dma((2, 7)),
            dma((2, 3)), dma((2, 3)),
        ],
        compiler_params=pltpu.CompilerParams(
            collective_id=0, has_side_effects=True, vmem_limit_bytes=56 * 1024 * 1024
        ),
    )(grad_out, input_spectrum, filter_spectrum, wide, first, last, twist, shuffle)
    return pl.pallas_call(
        hand_on,
        out_shape=out_shape,
        in_specs=[vmem] * 2,
        out_specs=(vmem,) * 2,
    )(*results)


def solution(mesh):
    in_specs = (
        P("dp", "chan", "seq"),
        P("dp", None, "chan", "seq", None),
        P(None, "chan", "seq", None),
    )
    out_specs = (P("dp", "chan", "seq"), P("chan", ("seq", "dp")))
    return jax.shard_map(
        on_device, mesh=mesh, in_specs=in_specs, out_specs=out_specs, check_vma=False
    )
```

```python
import functools

import jax
import jax.numpy as jnp
import numpy as np
from jax import lax
from jax.experimental import pallas as pl
from jax.experimental.pallas import tpu as pltpu
from jax.sharding import PartitionSpec as P

MESH = pl.DeviceIdType.MESH
F32 = jnp.float32
BF16 = jnp.bfloat16

SHARDS = 8
BATCHES = 4
CH = 8
HALF = 4
ROWS = 64
COLS = 512
BINS = 512
TIMES = 32
MODULUS = BINS * COLS
LANES = 128
NEAR = (1, -1, 2, -2, 3, -3)
CHAIN_WAY = -1
LONG_WAY = (1, 1, 1, -1, 1, -1, -1, -1)
ORDER = (
    ("gs", 0), ("gs", 1), ("gs", 2), ("gs", 3), ("gl", 0, 0), ("gr", 0, 0), ("gl", 1, 0),
    ("gr", 1, 0), ("gl", 2, 0), ("gr", 2, 0), ("gl", 3, 0), ("gs", 4), ("gr", 3, 0), ("gl", 0, 1),
    ("gr", 0, 1), ("gl", 1, 1), ("gr", 1, 1), ("gl", 2, 1), ("gr", 2, 1), ("gl", 4, 0),
    ("gl", 3, 1), ("gs", 7), ("gr", 4, 0), ("gr", 3, 1), ("gr", 0, 2), ("gl", 0, 2), ("gr", 1, 2),
    ("gl", 1, 2), ("gs", 6), ("gr", 2, 2), ("gl", 2, 2), ("gs", 5), ("gl", 4, 1), ("gl", 3, 2),
    ("gl", 7, 0), ("gr", 7, 0), ("gr", 4, 1), ("gr", 3, 2), ("gl", 6, 0), ("gl", 0, 3), ("A", 0),
    ("gl", 1, 3), ("gl", 5, 0), ("A", 1), ("gr", 6, 0), ("gl", 3, 3), ("A", 3), ("gl", 7, 1),
    ("gl", 2, 3), ("A", 2), ("B", 0), ("gr", 4, 2), ("gr", 5, 0), ("gl", 6, 1), ("gl", 4, 2),
    ("C", 0), ("gr", 7, 1), ("gl", 5, 1), ("Y", 0), ("D", 0), ("gr", 6, 1), ("gl", 7, 2),
    ("UE", 0), ("Rl", 0, -1), ("gr", 5, 1), ("gl", 6, 2), ("Rr", 0, -1), ("UE", 1), ("gl", 4, 3),
    ("Rl", 1, -1), ("gl", 5, 2), ("Rr", 1, -1), ("A", 4), ("UE", 2), ("gr", 7, 2), ("Rl", 2, -1),
    ("Rr", 2, -1), ("UE", 3), ("gr", 6, 2), ("gl", 7, 3), ("Rl", 3, -1), ("Rr", 3, -1), ("A", 7),
    ("Rl", 0, 0), ("gl", 6, 3), ("A", 6), ("gr", 5, 2), ("Rr", 0, 0), ("Rl", 1, 0), ("gl", 5, 3),
    ("A", 5), ("B", 1), ("Rr", 1, 0), ("Rl", 2, 0), ("C", 1), ("Rr", 3, 0), ("Rr", 2, 0),
    ("Rl", 0, 1), ("Rl", 3, 0), ("F", 0), ("Rr", 0, 1), ("Fs", 0), ("Rl", 1, 1), ("Rr", 1, 1),
    ("Rl", 2, 1), ("Y", 1), ("D", 1), ("Rr", 3, 1), ("Rr", 2, 1), ("Rl", 0, 2), ("Rl", 3, 1),
    ("UE", 4), ("Rl", 4, -1), ("Rr", 4, -1), ("UE", 5), ("Fr", 0, 0), ("Rl", 5, -1), ("Rr", 5, -1),
    ("Fl", 0, 0), ("Rl", 1, 2), ("UE", 6), ("Rl", 6, -1), ("Rr", 6, -1), ("Rl", 2, 2), ("UE", 7),
    ("Rl", 7, -1), ("Rr", 7, -1), ("Rr", 0, 2), ("Rr", 3, 2), ("Rr", 1, 2), ("Rr", 2, 2),
    ("Rl", 3, 2), ("Rl", 0, 3), ("X", 0), ("Rr", 4, 0), ("Rl", 4, 0), ("Rl", 5, 0), ("Fr", 0, 1),
    ("Fl", 0, 1), ("Rr", 5, 0), ("Rl", 6, 0), ("F", 1), ("Fs", 1), ("Rr", 6, 0), ("Rl", 7, 0),
    ("Rl", 3, 3), ("Rl", 1, 3), ("Rr", 4, 1), ("Rl", 2, 3), ("Rr", 7, 0), ("X", 1), ("X", 2),
    ("X", 3), ("Rl", 5, 1), ("Rl", 4, 1), ("Fl", 0, 2), ("Fr", 0, 2), ("Rl", 6, 1), ("Rr", 5, 1),
    ("Fc", 1), ("Fa", 1), ("Fb", 1), ("Rl", 7, 1), ("Rr", 6, 1), ("Rr", 4, 2), ("Rr", 7, 1),
    ("Rl", 5, 2), ("Rl", 4, 2), ("Fl", 0, 3), ("Fend", 0), ("Rr", 5, 2), ("Rl", 6, 2),
    ("Rl", 7, 2), ("Fend", 1), ("Rl", 5, 3), ("X", 5), ("Rr", 6, 2), ("Rl", 6, 3), ("X", 6),
    ("Rr", 7, 2), ("Rl", 4, 3), ("X", 4), ("Rl", 7, 3), ("X", 7),
)


def split_table(table):
    high = table.astype(np.float32).astype(jnp.bfloat16)
    low = (table - high.astype(np.float64)).astype(np.float32).astype(jnp.bfloat16)
    return high, low


@functools.cache
def tables():
    turn = 2.0 * np.pi
    fold = np.arange(LANES)
    forward, inverse = [], []
    for a in range(4):
        angle = turn * (np.outer(4 * fold + a, fold) % COLS) / COLS
        c, s = np.cos(angle), np.sin(angle)
        for group, block in (
            (forward, np.block([[c, -s], [s, c]])),
            (inverse, np.block([[c.T, s.T], [-s.T, c.T]])),
        ):
            high, low = split_table(block)
            group.append(np.concatenate([high, high, low], axis=0))
    wide = np.stack(forward + inverse)
    place = np.arange(COLS)
    order = 4 * (place % LANES) + place // LANES
    shuffle = np.zeros((COLS, COLS), np.float32)
    shuffle[order, place] = 1.0
    shuffle = np.stack([shuffle, shuffle.T]).astype(jnp.bfloat16)
    half = BINS // 2
    time_angle = turn * (np.outer(np.arange(BINS), np.arange(half)) % BINS) / BINS
    cos_t = np.cos(time_angle).reshape(SHARDS, ROWS, half)
    sin_t = np.sin(time_angle).reshape(SHARDS, ROWS, half)
    first = np.concatenate([cos_t, -sin_t], axis=1)
    first_high, first_low = split_table(first)
    first_table = np.concatenate([first_high, first_low], axis=1)
    last = np.concatenate([cos_t, -sin_t], axis=1).transpose(0, 2, 1) / MODULUS
    last_high, last_low = split_table(last)
    last_table = np.concatenate([last_high, last_high, last_low], axis=2)
    twist = turn * np.outer(np.arange(BINS), np.arange(COLS)) / MODULUS
    twist_table = np.stack(
        [np.cos(twist).reshape(SHARDS, ROWS, COLS), np.sin(twist).reshape(SHARDS, ROWS, COLS)],
        axis=1,
    ).astype(np.float32)[..., order]
    return wide, first_table, last_table, twist_table, shuffle


SPAN = 124.0
GAIN = 2.0 ** (2.0 * SPAN / 32.0) - 1.0
FLOOR = 2.0 ** (-SPAN / 32.0)


def encode(values, put, put_top):
    top = jnp.abs(values[0])
    for value in values[1:]:
        top = jnp.maximum(top, jnp.abs(value))
    top = (jnp.maximum(top, 1e-30) * 1.01).astype(BF16)
    put_top(top)
    slope = (GAIN * FLOOR) / top.astype(F32)
    for index, value in enumerate(values):
        level = jnp.abs(value) * slope + FLOOR
        for _ in range(5):
            level = level * level
        put(index, jnp.where(value < 0.0, -level, level).astype(BF16))


def decode(codes, top):
    unit = top.astype(F32) * (1.0 / GAIN)
    slope = unit * (1.0 / FLOOR)
    values = []
    for code in codes:
        wide_code = code.astype(F32)
        level = jnp.exp2(jnp.log2(jnp.abs(wide_code)) * (1.0 / 32.0))
        value = level * slope - unit
        values.append(jnp.where(wide_code < 0.0, -value, value))
    return values


def split(value):
    high = value.astype(BF16)
    low = (value - high.astype(F32)).astype(BF16)
    return high, low


def kernel(
    x_hbm, xs_hbm, hs_hbm, wide_hbm, first_hbm, last_hbm, twist_hbm, shuffle_hbm,
    in_ref, fl_ref,
    x_ref, wide, first, last, twist, shuffle, xs, hs, xf, xg, zb, yb, db, vb, u, part, recv, dh, dh_sent, dh_recv,
    zf, yf, u_f, part_f, recv_f, back, sent, sent_f, load_sem, ag_send, ag_recv, rs_send, rs_recv, y_send, y_recv,
    f_send, f_recv, b_send, b_recv,
):
    me = lax.axis_index("seq")
    batch = lax.axis_index("dp")

    def ring(offset):
        return lax.rem(me + (offset + SHARDS), SHARDS)

    def peer(offset):
        return lax.rem(batch + offset, BATCHES)

    barrier = pltpu.get_barrier_semaphore()
    for offset in NEAR:
        pl.semaphore_signal(barrier, inc=1, device_id={"seq": ring(offset)}, device_id_type=MESH)
    for offset in (1, 2, 3):
        pl.semaphore_signal(barrier, inc=1, device_id={"dp": peer(offset)}, device_id_type=MESH)

    loads = [
        pltpu.make_async_copy(first_hbm.at[me], first, load_sem.at[0]),
        pltpu.make_async_copy(twist_hbm.at[me], twist, load_sem.at[1]),
        pltpu.make_async_copy(wide_hbm, wide, load_sem.at[2]),
        pltpu.make_async_copy(hs_hbm, hs, load_sem.at[3]),
        pltpu.make_async_copy(xs_hbm.at[0], xs, load_sem.at[4]),
        pltpu.make_async_copy(last_hbm.at[me], last, load_sem.at[5]),
        pltpu.make_async_copy(shuffle_hbm.at[0], shuffle.at[0], load_sem.at[6]),
        pltpu.make_async_copy(x_hbm, x_ref, load_sem.at[7]),
        pltpu.make_async_copy(shuffle_hbm.at[1], shuffle.at[1], load_sem.at[8]),
    ]
    loads[7].start()
    loads[6].start()
    loads[7].wait()

    def spread(j, carry):
        for n in range(4):
            lanes = pl.ds(pl.multiple_of(j * COLS + n * 128, 128), 128)
            xf[n, pl.ds(j, CH, stride=TIMES), :] = x_ref[0, :, lanes].astype(F32)
        return carry

    lax.fori_loop(0, TIMES, spread, 0, unroll=8)
    mine = pl.multiple_of(me * TIMES, TIMES)
    loads[6].wait()
    rows = jnp.concatenate([xf[n].astype(BF16) for n in range(4)], axis=1)
    rows = jnp.dot(rows, shuffle[0], preferred_element_type=F32).astype(BF16)
    for c in range(CH):
        xg[c, pl.ds(mine, TIMES), :] = rows[c * TIMES : (c + 1) * TIMES, :]

    pl.semaphore_wait(barrier, len(NEAR) + 3)

    def gather_copy(q, k, long):
        way = LONG_WAY[q] if long else -LONG_WAY[q]
        source = pl.multiple_of(ring(-way * k) * TIMES, TIMES)
        block = xg.at[q, pl.ds(source, TIMES), :]
        slot = k if long else 4 + k
        return pltpu.make_async_remote_copy(
            src_ref=block, dst_ref=block, send_sem=ag_send.at[q, slot], recv_sem=ag_recv.at[q, slot],
            device_id={"seq": ring(way)}, device_id_type=MESH,
        )

    def gather_start(q):
        gather_copy(q, 0, True).start()
        gather_copy(q, 0, False).start()

    def gather_hop(q, k, long):
        gather_copy(q, k, long).wait_recv()
        if k < (3 if long else 2):
            gather_copy(q, k + 1, long).start()

    def put_split(dest, a, rows, real, imag):
        for index, value in enumerate((real, imag)):
            high, low = split(value)
            for place, item in ((0, high), (2, low), (4, high)):
                lane = (place + index) * LANES
                dest[a, rows, lane : lane + LANES] = item

    def stage_a(q):
        h, c = divmod(q, HALF)
        t = jnp.dot(first[...], xg[q], preferred_element_type=F32)
        real = t[0:64] + t[128:192]
        imag = t[64:128] + t[192:256]
        rows = slice(c * ROWS, (c + 1) * ROWS)
        for a in range(4):
            lanes = slice(a * LANES, (a + 1) * LANES)
            tc, ts = twist[0, :, lanes], twist[1, :, lanes]
            ar, ai = real[:, lanes], imag[:, lanes]
            put_split(zb.at[h], a, rows, ar * tc + ai * ts, ai * tc - ar * ts)

    def columns(source, dest, inverse):
        for a in range(4):
            weight = wide[a + 4] if inverse else wide[a]
            dest[a] = jnp.dot(source[a], weight, preferred_element_type=F32)

    def quarters(values, forward):
        (r0, i0), (r1, i1), (r2, i2), (r3, i3) = values
        sr, si, dr, di = r0 + r2, i0 + i2, r0 - r2, i0 - i2
        tr, ti, er, ei = r1 + r3, i1 + i3, r1 - r3, i1 - i3
        left = (dr + ei, di - er)
        right = (dr - ei, di + er)
        if not forward:
            left, right = right, left
        return [(sr + tr, si + ti), left, (sr - tr, si - ti), right]

    def products(h):
        def body(c, carry):
            rows = pl.ds(pl.multiple_of(c * ROWS, ROWS), ROWS)
            bins = quarters(
                [(yb[h, a, rows, 0:LANES], yb[h, a, rows, LANES : 2 * LANES]) for a in range(4)],
                True,
            )
            channel = HALF * h + c
            inner = []
            for e, (gr, gi) in enumerate(bins):
                lanes = slice(e * LANES, (e + 1) * LANES)
                hr, hi_ = hs[0, channel, :, lanes], hs[1, channel, :, lanes]
                inner.append((gr * hr + gi * hi_, gi * hr - gr * hi_))
                xr, xi = xs[0, channel, :, lanes], xs[1, channel, :, lanes]
                dh[h, c, 0, :, lanes] = gr * xr + gi * xi
                dh[h, c, 1, :, lanes] = gi * xr - gr * xi
            for a, (real, imag) in enumerate(quarters(inner, False)):
                put_split(db.at[h], a, rows, real, imag)
            return carry

        lax.fori_loop(0, HALF, body, 0)

    def finish(source, c, buffer, dest, channel):
        rows = slice(c * ROWS, (c + 1) * ROWS)
        for a in range(4):
            lanes = slice(a * LANES, (a + 1) * LANES)
            vr, vi = source[a, rows, 0:LANES], source[a, rows, LANES : 2 * LANES]
            tc, ts = twist[0, :, lanes], twist[1, :, lanes]
            for index, value in enumerate((vr * tc - vi * ts, vi * tc + vr * ts)):
                high, low = split(value)
                buffer[64 * index : 64 * index + 64, lanes] = high
                buffer[128 + 64 * index : 192 + 64 * index, lanes] = low
                buffer[256 + 64 * index : 320 + 64 * index, lanes] = high
        y = jnp.dot(last[...], buffer[...], preferred_element_type=F32)
        dest[:, channel] = y.reshape(SHARDS, TIMES, COLS)

    def share(part_ref, dest, c):
        return [part_ref[dest, c, rows, lanes] for rows, lanes in lines_of]

    lines_of = [
        (pl.ds(16 * r, 16), pl.ds(128 * n, 128)) for r in range(TIMES // 16) for n in range(4)
    ]

    def read(ref, q, slot):
        return decode([ref[q, slot, b] for b in range(8)], ref[q, slot, 8])

    def write(ref, q, slot, values):
        def put(index, code):
            ref[q, slot, index] = code

        def put_top(top):
            ref[q, slot, 8] = top

        encode(values, put, put_top)

    def add(left, right):
        return [a + b for a, b in zip(left, right)]

    def reduce_copy(q, k, long):
        slot = k if long else 4 + k
        way = LONG_WAY[q] if long else -LONG_WAY[q]
        return pltpu.make_async_remote_copy(
            src_ref=sent.at[q, slot], dst_ref=recv.at[q, slot],
            send_sem=rs_send.at[q, slot], recv_sem=rs_recv.at[q, slot],
            device_id={"seq": ring(way)}, device_id_type=MESH,
        )

    def reduce_hop(q, k, long):
        hops = 4 if long else 3
        way = LONG_WAY[q] if long else -LONG_WAY[q]
        base = 0 if long else 4
        if k >= 0:
            reduce_copy(q, k, long).wait_recv()
        if k == hops - 1:
            return
        values = share(part, ring(way * (hops - 1 - k)), q)
        if k >= 0:
            values = add(values, read(recv, q, base + k))
        write(sent, q, base + k + 1, values)
        reduce_copy(q, k + 1, long).start()

    def gather_sent(q):
        for k in range(7):
            gather_copy(q, k % 4, k < 4).wait_send()

    def reduce_end(q):
        for k in range(7):
            reduce_copy(q, k % 4, k < 4).wait_send()
        values = add(share(part, me, q), add(read(recv, q, 3), read(recv, q, 6)))
        for (rows, lanes), value in zip(lines_of, values):
            xf[lanes.start // 128, q * TIMES + rows.start : q * TIMES + rows.start + 16, :] = value

    def pair_copy(h, slot):
        way = 1 if h else -1
        return pltpu.make_async_remote_copy(
            src_ref=sent_f.at[h, slot], dst_ref=recv_f.at[h, slot],
            send_sem=f_send.at[h, slot], recv_sem=f_recv.at[h, slot],
            device_id={"seq": ring(way * (1, 1, -1, -1, 3, 1, -2)[slot])}, device_id_type=MESH,
        )

    def pair_send(h, slot, offset, arrived=None):
        values = share(part_f, ring(offset * (1 if h else -1)), h)
        if arrived is not None:
            pair_copy(h, arrived).wait_recv()
            values = add(values, read(recv_f, h, arrived))
        write(sent_f, h, slot, values)
        pair_copy(h, slot).start()

    def chain_copy(h, k, long):
        slot = k if long else 4 + k
        return pltpu.make_async_remote_copy(
            src_ref=sent_f.at[h, slot], dst_ref=recv_f.at[h, slot],
            send_sem=f_send.at[h, slot], recv_sem=f_recv.at[h, slot],
            device_id={"seq": ring(CHAIN_WAY if long else -CHAIN_WAY)}, device_id_type=MESH,
        )

    def chain_hop(h, k, long):
        hops = 4 if long else 3
        base = 0 if long else 4
        if k >= 0:
            chain_copy(h, k, long).wait_recv()
        if k == hops - 1:
            return
        way = CHAIN_WAY if long else -CHAIN_WAY
        values = share(part_f, ring(way * (hops - 1 - k)), h)
        if k >= 0:
            values = add(values, read(recv_f, h, base + k))
        write(sent_f, h, base + k + 1, values)
        chain_copy(h, k + 1, long).start()

    def pair_start(h):
        for slot, offset in ((0, 4), (1, 2), (2, -3), (3, -1)):
            pair_send(h, slot, offset)

    def pair_end(h):
        values = share(part_f, me, h)
        for slot in (3, 6) if h == 0 else (3, 4, 5, 6):
            if h:
                pair_copy(h, slot).wait_recv()
            values = add(values, read(recv_f, h, slot))
        for (rows, lanes), value in zip(lines_of, values):
            part_f[me, h, rows, lanes] = value
        for o in (1, 2, 3):
            back_copy(h, o).start()
        for o in (1, 2, 3):
            batch_copy(h, o).wait_send()
        for slot in range(7):
            if h:
                pair_copy(h, slot).wait_send()
            else:
                chain_copy(h, slot % 4, slot < 4).wait_send()
        here = pl.multiple_of(batch * 8, 8)
        back[pl.ds(pl.multiple_of((HALF * h + batch) * 8, 8), 8), :] = part_f[
            me, h, pl.ds(here, 8), :
        ]

    def batch_copy(h, o):
        return pltpu.make_async_remote_copy(
            src_ref=dh_sent.at[h, o - 1], dst_ref=dh_recv.at[h, o - 1],
            send_sem=y_send.at[h, o - 1], recv_sem=y_recv.at[h, o - 1],
            device_id={"dp": peer(o)}, device_id_type=MESH,
        )

    tiles = [(pl.ds(16 * r, 16), pl.ds(128 * n, 128)) for r in range(ROWS // 16) for n in range(4)]

    def batch_send(h):
        for o in (1, 2, 3):

            def body(index, carry):
                def put(b, code):
                    dh_sent[h, o - 1, index, b] = code

                def put_top(top):
                    dh_sent[h, o - 1, index, 16] = top

                other = peer(o)
                encode([dh[h, other, index, rows, lanes] for rows, lanes in tiles], put, put_top)
                return carry

            lax.fori_loop(0, 2, body, 0)
            batch_copy(h, o).start()

    def batch_sum(h):
        for o in (1, 2, 3):
            batch_copy(h, o).wait_recv()

        def body(index, carry):
            for o in (1, 2, 3):
                codes = [dh_recv[h, o - 1, index, b] for b in range(16)]
                for (rows, lanes), value in zip(tiles, decode(codes, dh_recv[h, o - 1, index, 16])):
                    dh[h, batch, index, rows, lanes] += value
            return carry

        lax.fori_loop(0, 2, body, 0)
        values = [
            (
                dh[h, batch, 0, :, e * LANES : (e + 1) * LANES],
                dh[h, batch, 1, :, e * LANES : (e + 1) * LANES],
            )
            for e in range(4)
        ]
        for a, (real, imag) in enumerate(quarters(values, False)):
            put_split(zf, a, slice(0, ROWS), real, imag)

    def filter_part(h):
        batch_sum(h)
        columns(zf, yf, True)
        finish(yf, 0, u_f, part_f, h)

    def back_copy(h, o):
        there = pl.multiple_of(peer(o) * 8, 8)
        return pltpu.make_async_remote_copy(
            src_ref=part_f.at[me, h, pl.ds(there, 8), :],
            dst_ref=back.at[pl.ds(pl.multiple_of((HALF * h + batch) * 8, 8), 8), :],
            send_sem=b_send.at[h, o - 1], recv_sem=b_recv.at[h, o - 1],
            device_id={"dp": peer(o)}, device_id_type=MESH,
        )

    waited = set()

    def need(*indices):
        for index in indices:
            if index not in waited:
                waited.add(index)
                loads[index].wait()

    def run(kind, q, k=None):
        if kind == "gs":
            gather_start(q)
        elif kind in ("gl", "gr"):
            gather_hop(q, k, kind == "gl")
        elif kind == "A":
            need(0, 1)
            stage_a(q)
        elif kind == "B":
            need(2)
            columns(zb.at[q], yb.at[q], False)
        elif kind == "C":
            need(3, 4)
            products(q)
        elif kind == "Y":
            batch_send(q)
        elif kind == "D":
            columns(db.at[q], vb.at[q], True)
        elif kind == "UE":
            need(5)
            finish(vb.at[q // HALF], q % HALF, u.at[q % HALF], part, q)
            gather_sent(q)
        elif kind in ("Rl", "Rr"):
            reduce_hop(q, k, kind == "Rl")
        elif kind == "X":
            reduce_end(q)
        elif kind == "F":
            filter_part(q)
        elif kind == "Fs" and q == 0:
            chain_hop(q, -1, True)
            chain_hop(q, -1, False)
        elif kind in ("Fl", "Fr"):
            chain_hop(q, k, kind == "Fl")
        elif kind == "Fs":
            pair_start(q)
        elif kind == "Fa":
            pair_send(q, 4, 3, 0)
        elif kind == "Fb":
            pair_send(q, 5, 1, 1)
        elif kind == "Fc":
            pair_send(q, 6, -2, 2)
        elif kind == "Fend":
            pair_end(q)

    started = False
    for task in ORDER:
        if task[0] != "gs" and not started:
            for index in (0, 1, 2, 3, 4, 5, 8):
                loads[index].start()
            started = True
        run(*task)
    need(8)

    rows = jnp.concatenate([xf[n].astype(BF16) for n in range(4)], axis=1)
    rows = jnp.dot(rows, shuffle[1], preferred_element_type=F32)
    for n in range(4):
        xf[n] = rows[:, n * 128 : (n + 1) * 128]

    def collect(j, carry):
        for n in range(4):
            lanes = pl.ds(pl.multiple_of(j * COLS + n * 128, 128), 128)
            in_ref[0, :, lanes] = xf[n, pl.ds(j, CH, stride=TIMES), :].astype(BF16)
        return carry

    lax.fori_loop(0, TIMES, collect, 0, unroll=8)

    for h in range(2):
        for o in (1, 2, 3):
            back_copy(h, o).wait()
    high, low = split(back[...])
    rest = (back[...] - high.astype(F32) - low.astype(F32)).astype(BF16)
    lines = sum(
        jnp.dot(item, shuffle[1], preferred_element_type=F32) for item in (rest, low, high)
    )
    for n in range(4):
        xf[n, 0:64, :] = lines[:, n * 128 : (n + 1) * 128]
        for j in range(8):
            start = j * COLS + n * 128
            fl_ref[:, start : start + 128] = xf[n, pl.ds(j, CH, stride=8), :]


def hand_on(in_a, in_b, out_a, out_b, held_a, held_b, sems):
    arrays = ((in_a, held_a, out_a), (in_b, held_b, out_b))
    inward = [pltpu.make_async_copy(a, b, sems.at[i]) for i, (a, b, _) in enumerate(arrays)]
    outward = [pltpu.make_async_copy(b, c, sems.at[2 + i]) for i, (_, b, c) in enumerate(arrays)]
    for copy in inward:
        copy.start()
    for copy, after in zip(inward, outward):
        copy.wait()
        after.start()
    for copy in outward:
        copy.wait()


def on_device(grad_out, input_spectrum, filter_spectrum):
    wide, first, last, twist, shuffle = (jnp.asarray(t) for t in tables())
    vmem = pl.BlockSpec(memory_space=pltpu.VMEM)
    anywhere = pl.BlockSpec(memory_space=pl.ANY)
    dma = pltpu.SemaphoreType.DMA
    out_shape = (
        jax.ShapeDtypeStruct((1, CH, TIMES * COLS), BF16),
        jax.ShapeDtypeStruct((CH, TIMES * COLS // BATCHES), F32),
    )
    results = pl.pallas_call(
        kernel,
        out_shape=out_shape,
        in_specs=[anywhere] * 8,
        out_specs=(vmem, vmem),
        scratch_shapes=[
            pltpu.VMEM((1, CH, TIMES * COLS), BF16),
            pltpu.VMEM((8, 768, 256), BF16),
            pltpu.VMEM((256, 256), BF16),
            pltpu.VMEM((256, 384), BF16),
            pltpu.VMEM((2, ROWS, COLS), F32),
            pltpu.VMEM((2, COLS, COLS), BF16),
            pltpu.VMEM((2, CH, ROWS, COLS), F32),
            pltpu.VMEM((2, CH, ROWS, COLS), F32),
            pltpu.VMEM((4, CH * TIMES, 128), F32),
            pltpu.VMEM((CH, SHARDS * TIMES, COLS), BF16),
            pltpu.VMEM((2, 4, HALF * ROWS, 768), BF16),
            pltpu.VMEM((2, 4, HALF * ROWS, 256), F32),
            pltpu.VMEM((2, 4, HALF * ROWS, 768), BF16),
            pltpu.VMEM((2, 4, HALF * ROWS, 256), F32),
            pltpu.VMEM((HALF, 384, COLS), BF16),
            pltpu.VMEM((SHARDS, CH, TIMES, COLS), F32),
            pltpu.VMEM((CH, 7, 9, 16, 128), BF16),
            pltpu.VMEM((2, BATCHES, 2, ROWS, COLS), F32),
            pltpu.VMEM((2, 3, 2, 17, 16, 128), BF16),
            pltpu.VMEM((2, 3, 2, 17, 16, 128), BF16),
            pltpu.VMEM((4, ROWS, 768), BF16),
            pltpu.VMEM((4, ROWS, 256), F32),
            pltpu.VMEM((384, COLS), BF16),
            pltpu.VMEM((SHARDS, 2, TIMES, COLS), F32),
            pltpu.VMEM((2, 7, 9, 16, 128), BF16),
            pltpu.VMEM((CH * 8, COLS), F32),
            pltpu.VMEM((CH, 7, 9, 16, 128), BF16),
            pltpu.VMEM((2, 7, 9, 16, 128), BF16),
            dma((9,)),
            dma((CH, 7)), dma((CH, 7)),
            dma((CH, 7)), dma((CH, 7)),
            dma((2, 3)), dma((2, 3)),
            dma((2, 7)), dma((2, 7)),
            dma((2, 3)), dma((2, 3)),
        ],
        compiler_params=pltpu.CompilerParams(
            collective_id=0, has_side_effects=True, vmem_limit_bytes=56 * 1024 * 1024
        ),
    )(grad_out, input_spectrum, filter_spectrum, wide, first, last, twist, shuffle)
    return pl.pallas_call(
        hand_on,
        out_shape=out_shape,
        in_specs=[anywhere] * 2,
        out_specs=(anywhere,) * 2,
        scratch_shapes=[
            pltpu.VMEM((1, CH, TIMES * COLS), BF16),
            pltpu.VMEM((CH, TIMES * COLS // BATCHES), F32),
            dma((4,)),
        ],
        compiler_params=pltpu.CompilerParams(vmem_limit_bytes=56 * 1024 * 1024),
    )(*results)


def solution(mesh):
    in_specs = (
        P("dp", "chan", "seq"),
        P("dp", None, "chan", "seq", None),
        P(None, "chan", "seq", None),
    )
    out_specs = (P("dp", "chan", "seq"), P("chan", ("seq", "dp")))
    return jax.shard_map(
        on_device, mesh=mesh, in_specs=in_specs, out_specs=out_specs, check_vma=False
    )
```

```python
import functools

import jax
import jax.numpy as jnp
import numpy as np
from jax import lax
from jax.experimental import pallas as pl
from jax.experimental.pallas import tpu as pltpu
from jax.sharding import PartitionSpec as P

MESH = pl.DeviceIdType.MESH
F32 = jnp.float32
BF16 = jnp.bfloat16

SHARDS = 8
BATCHES = 4
CH = 8
HALF = 4
ROWS = 64
COLS = 512
BINS = 512
TIMES = 32
MODULUS = BINS * COLS
LANES = 128
NEAR = (1, -1, 2, -2, 3, -3)
CHAIN_WAY = -1
LONG_WAY = (1, 1, 1, -1, 1, -1, -1, -1)
ORDER = (
    ("gs", 0), ("gs", 1), ("gs", 2), ("gs", 3), ("gl", 0, 0), ("gr", 0, 0), ("gl", 1, 0),
    ("gr", 1, 0), ("gl", 2, 0), ("gr", 2, 0), ("gl", 3, 0), ("gs", 4), ("gr", 3, 0), ("gl", 0, 1),
    ("gr", 0, 1), ("gl", 1, 1), ("gr", 1, 1), ("gl", 2, 1), ("gr", 2, 1), ("gl", 4, 0),
    ("gl", 3, 1), ("gs", 7), ("gr", 4, 0), ("gr", 3, 1), ("gr", 0, 2), ("gl", 0, 2), ("gr", 1, 2),
    ("gl", 1, 2), ("gs", 6), ("gr", 2, 2), ("gl", 2, 2), ("gs", 5), ("gl", 4, 1), ("gl", 3, 2),
    ("gl", 7, 0), ("gr", 7, 0), ("gr", 4, 1), ("gr", 3, 2), ("gl", 6, 0), ("gl", 0, 3), ("A", 0),
    ("gl", 1, 3), ("gl", 5, 0), ("A", 1), ("gr", 6, 0), ("gl", 3, 3), ("A", 3), ("gl", 7, 1),
    ("gl", 2, 3), ("A", 2), ("B", 0), ("gr", 4, 2), ("gr", 5, 0), ("gl", 6, 1), ("gl", 4, 2),
    ("C", 0), ("gr", 7, 1), ("gl", 5, 1), ("Y", 0), ("D", 0), ("gr", 6, 1), ("gl", 7, 2),
    ("UE", 0), ("Rl", 0, -1), ("gr", 5, 1), ("gl", 6, 2), ("Rr", 0, -1), ("UE", 1), ("gl", 4, 3),
    ("Rl", 1, -1), ("gl", 5, 2), ("Rr", 1, -1), ("A", 4), ("UE", 2), ("gr", 7, 2), ("Rl", 2, -1),
    ("Rr", 2, -1), ("UE", 3), ("gr", 6, 2), ("gl", 7, 3), ("Rl", 3, -1), ("Rr", 3, -1), ("A", 7),
    ("Rl", 0, 0), ("gl", 6, 3), ("A", 6), ("gr", 5, 2), ("Rr", 0, 0), ("Rl", 1, 0), ("gl", 5, 3),
    ("A", 5), ("B", 1), ("Rr", 1, 0), ("Rl", 2, 0), ("C", 1), ("Rr", 3, 0), ("Rr", 2, 0),
    ("Rl", 0, 1), ("Rl", 3, 0), ("F", 0), ("Rr", 0, 1), ("Fs", 0), ("Rl", 1, 1), ("Rr", 1, 1),
    ("Rl", 2, 1), ("Y", 1), ("D", 1), ("Rr", 3, 1), ("Rr", 2, 1), ("Rl", 0, 2), ("Rl", 3, 1),
    ("UE", 4), ("Rl", 4, -1), ("Rr", 4, -1), ("UE", 5), ("Fr", 0, 0), ("Rl", 5, -1), ("Rr", 5, -1),
    ("Fl", 0, 0), ("Rl", 1, 2), ("UE", 6), ("Rl", 6, -1), ("Rr", 6, -1), ("Rl", 2, 2), ("UE", 7),
    ("Rl", 7, -1), ("Rr", 7, -1), ("Rr", 0, 2), ("Rr", 3, 2), ("Rr", 1, 2), ("Rr", 2, 2),
    ("Rl", 3, 2), ("Rl", 0, 3), ("X", 0), ("Rr", 4, 0), ("Rl", 4, 0), ("Rl", 5, 0), ("Fr", 0, 1),
    ("Fl", 0, 1), ("Rr", 5, 0), ("Rl", 6, 0), ("F", 1), ("Fs", 1), ("Rr", 6, 0), ("Rl", 7, 0),
    ("Rl", 3, 3), ("Rl", 1, 3), ("Rr", 4, 1), ("Rl", 2, 3), ("Rr", 7, 0), ("X", 1), ("X", 2),
    ("X", 3), ("Rl", 5, 1), ("Rl", 4, 1), ("Fl", 0, 2), ("Fr", 0, 2), ("Rl", 6, 1), ("Rr", 5, 1),
    ("Fc", 1), ("Fa", 1), ("Fb", 1), ("Rl", 7, 1), ("Rr", 6, 1), ("Rr", 4, 2), ("Rr", 7, 1),
    ("Rl", 5, 2), ("Rl", 4, 2), ("Fl", 0, 3), ("Fend", 0), ("Rr", 5, 2), ("Rl", 6, 2),
    ("Rl", 7, 2), ("Fend", 1), ("Rl", 5, 3), ("X", 5), ("Rr", 6, 2), ("Rl", 6, 3), ("X", 6),
    ("Rr", 7, 2), ("Rl", 4, 3), ("X", 4), ("Rl", 7, 3), ("X", 7),
)


def split_table(table):
    high = table.astype(np.float32).astype(jnp.bfloat16)
    low = (table - high.astype(np.float64)).astype(np.float32).astype(jnp.bfloat16)
    return high, low


@functools.cache
def tables():
    turn = 2.0 * np.pi
    fold = np.arange(LANES)
    forward, inverse = [], []
    for a in range(4):
        angle = turn * (np.outer(4 * fold + a, fold) % COLS) / COLS
        c, s = np.cos(angle), np.sin(angle)
        for group, block in (
            (forward, np.block([[c, -s], [s, c]])),
            (inverse, np.block([[c.T, s.T], [-s.T, c.T]])),
        ):
            high, low = split_table(block)
            group.append(np.concatenate([high, high, low], axis=0))
    wide = np.stack(forward + inverse)
    place = np.arange(COLS)
    order = 4 * (place % LANES) + place // LANES
    shuffle = np.zeros((COLS, COLS), np.float32)
    shuffle[order, place] = 1.0
    shuffle = np.stack([shuffle, shuffle.T]).astype(jnp.bfloat16)
    half = BINS // 2
    time_angle = turn * (np.outer(np.arange(BINS), np.arange(half)) % BINS) / BINS
    cos_t = np.cos(time_angle).reshape(SHARDS, ROWS, half)
    sin_t = np.sin(time_angle).reshape(SHARDS, ROWS, half)
    first = np.concatenate([cos_t, -sin_t], axis=1)
    first_high, first_low = split_table(first)
    first_table = np.concatenate([first_high, first_low], axis=1)
    last = np.concatenate([cos_t, -sin_t], axis=1).transpose(0, 2, 1) / MODULUS
    last_high, last_low = split_table(last)
    last_table = np.concatenate([last_high, last_high, last_low], axis=2)
    twist = turn * np.outer(np.arange(BINS), np.arange(COLS)) / MODULUS
    twist_table = np.stack(
        [np.cos(twist).reshape(SHARDS, ROWS, COLS), np.sin(twist).reshape(SHARDS, ROWS, COLS)],
        axis=1,
    ).astype(np.float32)[..., order]
    return wide, first_table, last_table, twist_table, shuffle


SPAN = 124.0
GAIN = 2.0 ** (2.0 * SPAN / 32.0) - 1.0
FLOOR = 2.0 ** (-SPAN / 32.0)


def encode(values, put, put_top):
    top = jnp.abs(values[0])
    for value in values[1:]:
        top = jnp.maximum(top, jnp.abs(value))
    top = (jnp.maximum(top, 1e-30) * 1.01).astype(BF16)
    put_top(top)
    slope = (GAIN * FLOOR) / top.astype(F32)
    for index, value in enumerate(values):
        level = jnp.abs(value) * slope + FLOOR
        for _ in range(5):
            level = level * level
        put(index, jnp.where(value < 0.0, -level, level).astype(BF16))


def decode(codes, top):
    unit = top.astype(F32) * (1.0 / GAIN)
    slope = unit * (1.0 / FLOOR)
    values = []
    for code in codes:
        wide_code = code.astype(F32)
        level = jnp.exp2(jnp.log2(jnp.abs(wide_code)) * (1.0 / 32.0))
        value = level * slope - unit
        values.append(jnp.where(wide_code < 0.0, -value, value))
    return values


def split(value):
    high = value.astype(BF16)
    low = (value - high.astype(F32)).astype(BF16)
    return high, low


def kernel(
    x_hbm, xs_hbm, hs_hbm, wide_hbm, first_hbm, last_hbm, twist_hbm, shuffle_hbm,
    in_ref, fl_ref,
    x_ref, wide, first, last, twist, shuffle, xs, hs, xf, xg, zb, yb, db, vb, u, part, recv, dh, dh_sent, dh_recv,
    zf, yf, u_f, part_f, recv_f, back, sent, sent_f, load_sem, ag_send, ag_recv, rs_send, rs_recv, y_send, y_recv,
    f_send, f_recv, b_send, b_recv,
):
    me = lax.axis_index("seq")
    batch = lax.axis_index("dp")

    def ring(offset):
        return lax.rem(me + (offset + SHARDS), SHARDS)

    def peer(offset):
        return lax.rem(batch + offset, BATCHES)

    barrier = pltpu.get_barrier_semaphore()
    for offset in NEAR:
        pl.semaphore_signal(barrier, inc=1, device_id={"seq": ring(offset)}, device_id_type=MESH)
    for offset in (1, 2, 3):
        pl.semaphore_signal(barrier, inc=1, device_id={"dp": peer(offset)}, device_id_type=MESH)

    loads = [
        pltpu.make_async_copy(first_hbm.at[me], first, load_sem.at[0]),
        pltpu.make_async_copy(twist_hbm.at[me], twist, load_sem.at[1]),
        pltpu.make_async_copy(wide_hbm, wide, load_sem.at[2]),
        pltpu.make_async_copy(hs_hbm, hs, load_sem.at[3]),
        pltpu.make_async_copy(xs_hbm.at[0], xs, load_sem.at[4]),
        pltpu.make_async_copy(last_hbm.at[me], last, load_sem.at[5]),
        pltpu.make_async_copy(shuffle_hbm.at[0], shuffle.at[0], load_sem.at[6]),
        pltpu.make_async_copy(x_hbm, x_ref, load_sem.at[7]),
        pltpu.make_async_copy(shuffle_hbm.at[1], shuffle.at[1], load_sem.at[8]),
    ]
    loads[7].start()
    loads[6].start()
    loads[7].wait()

    def spread(j, carry):
        for n in range(4):
            lanes = pl.ds(pl.multiple_of(j * COLS + n * 128, 128), 128)
            xf[n, pl.ds(j, CH, stride=TIMES), :] = x_ref[0, :, lanes].astype(F32)
        return carry

    lax.fori_loop(0, TIMES, spread, 0, unroll=8)
    mine = pl.multiple_of(me * TIMES, TIMES)
    loads[6].wait()
    rows = jnp.concatenate([xf[n, 0 : CH * TIMES, :].astype(BF16) for n in range(4)], axis=1)
    rows = jnp.dot(rows, shuffle[0], preferred_element_type=F32).astype(BF16)
    for c in range(CH):
        xg[c, pl.ds(mine, TIMES), :] = rows[c * TIMES : (c + 1) * TIMES, :]

    pl.semaphore_wait(barrier, len(NEAR) + 3)

    def gather_copy(q, k, long):
        way = LONG_WAY[q] if long else -LONG_WAY[q]
        source = pl.multiple_of(ring(-way * k) * TIMES, TIMES)
        block = xg.at[q, pl.ds(source, TIMES), :]
        slot = k if long else 4 + k
        return pltpu.make_async_remote_copy(
            src_ref=block, dst_ref=block, send_sem=ag_send.at[q, slot], recv_sem=ag_recv.at[q, slot],
            device_id={"seq": ring(way)}, device_id_type=MESH,
        )

    def gather_start(q):
        gather_copy(q, 0, True).start()
        gather_copy(q, 0, False).start()

    def gather_hop(q, k, long):
        gather_copy(q, k, long).wait_recv()
        if k < (3 if long else 2):
            gather_copy(q, k + 1, long).start()

    def put_split(dest, a, rows, real, imag):
        for index, value in enumerate((real, imag)):
            high, low = split(value)
            for place, item in ((0, high), (2, low), (4, high)):
                lane = (place + index) * LANES
                dest[a, rows, lane : lane + LANES] = item

    def stage_a(q):
        h, c = divmod(q, HALF)
        t = jnp.dot(first[...], xg[q], preferred_element_type=F32)
        real = t[0:64] + t[128:192]
        imag = t[64:128] + t[192:256]
        rows = slice(c * ROWS, (c + 1) * ROWS)
        for a in range(4):
            lanes = slice(a * LANES, (a + 1) * LANES)
            tc, ts = twist[0, :, lanes], twist[1, :, lanes]
            ar, ai = real[:, lanes], imag[:, lanes]
            put_split(zb.at[h], a, rows, ar * tc + ai * ts, ai * tc - ar * ts)

    def columns(source, dest, inverse):
        for a in range(4):
            weight = wide[a + 4] if inverse else wide[a]
            dest[a] = jnp.dot(source[a], weight, preferred_element_type=F32)

    def quarters(values, forward):
        (r0, i0), (r1, i1), (r2, i2), (r3, i3) = values
        sr, si, dr, di = r0 + r2, i0 + i2, r0 - r2, i0 - i2
        tr, ti, er, ei = r1 + r3, i1 + i3, r1 - r3, i1 - i3
        left = (dr + ei, di - er)
        right = (dr - ei, di + er)
        if not forward:
            left, right = right, left
        return [(sr + tr, si + ti), left, (sr - tr, si - ti), right]

    def products(h):
        def body(c, carry):
            rows = pl.ds(pl.multiple_of(c * ROWS, ROWS), ROWS)
            bins = quarters(
                [(yb[h, a, rows, 0:LANES], yb[h, a, rows, LANES : 2 * LANES]) for a in range(4)],
                True,
            )
            channel = HALF * h + c
            inner = []
            for e, (gr, gi) in enumerate(bins):
                lanes = slice(e * LANES, (e + 1) * LANES)
                hr, hi_ = hs[0, channel, :, lanes], hs[1, channel, :, lanes]
                inner.append((gr * hr + gi * hi_, gi * hr - gr * hi_))
                xr, xi = xs[0, channel, :, lanes], xs[1, channel, :, lanes]
                dh[h, c, 0, :, lanes] = gr * xr + gi * xi
                dh[h, c, 1, :, lanes] = gi * xr - gr * xi
            for a, (real, imag) in enumerate(quarters(inner, False)):
                put_split(db.at[h], a, rows, real, imag)
            return carry

        lax.fori_loop(0, HALF, body, 0)

    def finish(source, c, buffer, dest, channel):
        rows = slice(c * ROWS, (c + 1) * ROWS)
        for a in range(4):
            lanes = slice(a * LANES, (a + 1) * LANES)
            vr, vi = source[a, rows, 0:LANES], source[a, rows, LANES : 2 * LANES]
            tc, ts = twist[0, :, lanes], twist[1, :, lanes]
            for index, value in enumerate((vr * tc - vi * ts, vi * tc + vr * ts)):
                high, low = split(value)
                buffer[64 * index : 64 * index + 64, lanes] = high
                buffer[128 + 64 * index : 192 + 64 * index, lanes] = low
                buffer[256 + 64 * index : 320 + 64 * index, lanes] = high
        y = jnp.dot(last[...], buffer[...], preferred_element_type=F32)
        dest[:, channel] = y.reshape(SHARDS, TIMES, COLS)

    def share(part_ref, dest, c):
        return [part_ref[dest, c, rows, lanes] for rows, lanes in lines_of]

    lines_of = [
        (pl.ds(16 * r, 16), pl.ds(128 * n, 128)) for r in range(TIMES // 16) for n in range(4)
    ]

    def read(ref, q, slot):
        return decode([ref[q, slot, b] for b in range(8)], ref[q, slot, 8])

    def write(ref, q, slot, values):
        def put(index, code):
            ref[q, slot, index] = code

        def put_top(top):
            ref[q, slot, 8] = top

        encode(values, put, put_top)

    def add(left, right):
        return [a + b for a, b in zip(left, right)]

    def reduce_copy(q, k, long):
        slot = k if long else 4 + k
        way = LONG_WAY[q] if long else -LONG_WAY[q]
        return pltpu.make_async_remote_copy(
            src_ref=sent.at[q, slot], dst_ref=recv.at[q, slot],
            send_sem=rs_send.at[q, slot], recv_sem=rs_recv.at[q, slot],
            device_id={"seq": ring(way)}, device_id_type=MESH,
        )

    def reduce_hop(q, k, long):
        hops = 4 if long else 3
        way = LONG_WAY[q] if long else -LONG_WAY[q]
        base = 0 if long else 4
        if k >= 0:
            reduce_copy(q, k, long).wait_recv()
        if k == hops - 1:
            return
        values = share(part, ring(way * (hops - 1 - k)), q)
        if k >= 0:
            values = add(values, read(recv, q, base + k))
        write(sent, q, base + k + 1, values)
        reduce_copy(q, k + 1, long).start()

    def gather_sent(q):
        for k in range(7):
            gather_copy(q, k % 4, k < 4).wait_send()

    def reduce_end(q):
        for k in range(7):
            reduce_copy(q, k % 4, k < 4).wait_send()
        values = add(share(part, me, q), add(read(recv, q, 3), read(recv, q, 6)))
        for (rows, lanes), value in zip(lines_of, values):
            xf[lanes.start // 128, q * TIMES + rows.start : q * TIMES + rows.start + 16, :] = value

    def pair_copy(h, slot):
        way = 1 if h else -1
        return pltpu.make_async_remote_copy(
            src_ref=sent_f.at[h, slot], dst_ref=recv_f.at[h, slot],
            send_sem=f_send.at[h, slot], recv_sem=f_recv.at[h, slot],
            device_id={"seq": ring(way * (1, 1, -1, -1, 3, 1, -2)[slot])}, device_id_type=MESH,
        )

    def pair_send(h, slot, offset, arrived=None):
        values = share(part_f, ring(offset * (1 if h else -1)), h)
        if arrived is not None:
            pair_copy(h, arrived).wait_recv()
            values = add(values, read(recv_f, h, arrived))
        write(sent_f, h, slot, values)
        pair_copy(h, slot).start()

    def chain_copy(h, k, long):
        slot = k if long else 4 + k
        return pltpu.make_async_remote_copy(
            src_ref=sent_f.at[h, slot], dst_ref=recv_f.at[h, slot],
            send_sem=f_send.at[h, slot], recv_sem=f_recv.at[h, slot],
            device_id={"seq": ring(CHAIN_WAY if long else -CHAIN_WAY)}, device_id_type=MESH,
        )

    def chain_hop(h, k, long):
        hops = 4 if long else 3
        base = 0 if long else 4
        if k >= 0:
            chain_copy(h, k, long).wait_recv()
        if k == hops - 1:
            return
        way = CHAIN_WAY if long else -CHAIN_WAY
        values = share(part_f, ring(way * (hops - 1 - k)), h)
        if k >= 0:
            values = add(values, read(recv_f, h, base + k))
        write(sent_f, h, base + k + 1, values)
        chain_copy(h, k + 1, long).start()

    def pair_start(h):
        for slot, offset in ((0, 4), (1, 2), (2, -3), (3, -1)):
            pair_send(h, slot, offset)

    def pair_end(h):
        values = share(part_f, me, h)
        for slot in (3, 6) if h == 0 else (3, 4, 5, 6):
            if h:
                pair_copy(h, slot).wait_recv()
            values = add(values, read(recv_f, h, slot))
        for (rows, lanes), value in zip(lines_of, values):
            part_f[me, h, rows, lanes] = value
        for o in (1, 2, 3):
            back_copy(h, o).start()
        for o in (1, 2, 3):
            batch_copy(h, o).wait_send()
        for slot in range(7):
            if h:
                pair_copy(h, slot).wait_send()
            else:
                chain_copy(h, slot % 4, slot < 4).wait_send()
        here = pl.multiple_of(batch * 8, 8)
        back[pl.ds(pl.multiple_of((HALF * h + batch) * 8, 8), 8), :] = part_f[
            me, h, pl.ds(here, 8), :
        ]

    def batch_copy(h, o):
        return pltpu.make_async_remote_copy(
            src_ref=dh_sent.at[h, o - 1], dst_ref=dh_recv.at[h, o - 1],
            send_sem=y_send.at[h, o - 1], recv_sem=y_recv.at[h, o - 1],
            device_id={"dp": peer(o)}, device_id_type=MESH,
        )

    tiles = [(pl.ds(16 * r, 16), pl.ds(128 * n, 128)) for r in range(ROWS // 16) for n in range(4)]

    def batch_send(h):
        for o in (1, 2, 3):

            def body(index, carry):
                def put(b, code):
                    dh_sent[h, o - 1, index, b] = code

                def put_top(top):
                    dh_sent[h, o - 1, index, 16] = top

                other = peer(o)
                encode([dh[h, other, index, rows, lanes] for rows, lanes in tiles], put, put_top)
                return carry

            lax.fori_loop(0, 2, body, 0)
            batch_copy(h, o).start()

    def batch_sum(h):
        for o in (1, 2, 3):
            batch_copy(h, o).wait_recv()

        def body(index, carry):
            for o in (1, 2, 3):
                codes = [dh_recv[h, o - 1, index, b] for b in range(16)]
                for (rows, lanes), value in zip(tiles, decode(codes, dh_recv[h, o - 1, index, 16])):
                    dh[h, batch, index, rows, lanes] += value
            return carry

        lax.fori_loop(0, 2, body, 0)
        values = [
            (
                dh[h, batch, 0, :, e * LANES : (e + 1) * LANES],
                dh[h, batch, 1, :, e * LANES : (e + 1) * LANES],
            )
            for e in range(4)
        ]
        for a, (real, imag) in enumerate(quarters(values, False)):
            put_split(zf, a, slice(0, ROWS), real, imag)

    def filter_part(h):
        batch_sum(h)
        columns(zf, yf, True)
        finish(yf, 0, u_f, part_f, h)

    def back_copy(h, o):
        there = pl.multiple_of(peer(o) * 8, 8)
        return pltpu.make_async_remote_copy(
            src_ref=part_f.at[me, h, pl.ds(there, 8), :],
            dst_ref=back.at[pl.ds(pl.multiple_of((HALF * h + batch) * 8, 8), 8), :],
            send_sem=b_send.at[h, o - 1], recv_sem=b_recv.at[h, o - 1],
            device_id={"dp": peer(o)}, device_id_type=MESH,
        )

    waited = set()

    def need(*indices):
        for index in indices:
            if index not in waited:
                waited.add(index)
                loads[index].wait()

    def run(kind, q, k=None):
        if kind == "gs":
            gather_start(q)
        elif kind in ("gl", "gr"):
            gather_hop(q, k, kind == "gl")
        elif kind == "A":
            need(0, 1)
            stage_a(q)
        elif kind == "B":
            need(2)
            columns(zb.at[q], yb.at[q], False)
        elif kind == "C":
            need(3, 4)
            products(q)
        elif kind == "Y":
            batch_send(q)
        elif kind == "D":
            columns(db.at[q], vb.at[q], True)
        elif kind == "UE":
            need(5)
            finish(vb.at[q // HALF], q % HALF, u.at[q % HALF], part, q)
            gather_sent(q)
        elif kind in ("Rl", "Rr"):
            reduce_hop(q, k, kind == "Rl")
        elif kind == "X":
            reduce_end(q)
        elif kind == "F":
            filter_part(q)
        elif kind == "Fs" and q == 0:
            chain_hop(q, -1, True)
            chain_hop(q, -1, False)
        elif kind in ("Fl", "Fr"):
            chain_hop(q, k, kind == "Fl")
        elif kind == "Fs":
            pair_start(q)
        elif kind == "Fa":
            pair_send(q, 4, 3, 0)
        elif kind == "Fb":
            pair_send(q, 5, 1, 1)
        elif kind == "Fc":
            pair_send(q, 6, -2, 2)
        elif kind == "Fend":
            pair_end(q)

    started = False
    for task in ORDER:
        if task[0] != "gs" and not started:
            for index in (0, 1, 2, 3, 4, 5, 8):
                loads[index].start()
            started = True
        run(*task)
    need(8)

    rows = jnp.concatenate([xf[n, 0 : CH * TIMES, :].astype(BF16) for n in range(4)], axis=1)
    rows = jnp.dot(rows, shuffle[1], preferred_element_type=F32)
    for n in range(4):
        xf[n, 0 : CH * TIMES, :] = rows[:, n * 128 : (n + 1) * 128]

    def collect(j, carry):
        for n in range(4):
            lanes = pl.ds(pl.multiple_of(j * COLS + n * 128, 128), 128)
            in_ref[0, :, lanes] = xf[n, pl.ds(j, CH, stride=TIMES), :].astype(BF16)
        return carry

    lax.fori_loop(0, TIMES, collect, 0, unroll=8)

    for h in range(2):
        for o in (1, 2, 3):
            back_copy(h, o).wait()
    high, low = split(back[...])
    rest = (back[...] - high.astype(F32) - low.astype(F32)).astype(BF16)
    lines = sum(
        jnp.dot(item, shuffle[1], preferred_element_type=F32) for item in (rest, low, high)
    )
    for n in range(4):
        xf[n, 0:64, :] = lines[:, n * 128 : (n + 1) * 128]
        for j in range(8):
            start = j * COLS + n * 128
            fl_ref[:, start : start + 128] = xf[n, pl.ds(j, CH, stride=8), :]


def hand_on(in_a, in_b, out_a, out_b, held_a, held_b, sems):
    arrays = ((in_a, held_a, out_a), (in_b, held_b, out_b))
    inward = [pltpu.make_async_copy(a, b, sems.at[i]) for i, (a, b, _) in enumerate(arrays)]
    outward = [pltpu.make_async_copy(b, c, sems.at[2 + i]) for i, (_, b, c) in enumerate(arrays)]
    for copy in inward:
        copy.start()
    for copy, after in zip(inward, outward):
        copy.wait()
        after.start()
    for copy in outward:
        copy.wait()


def on_device(grad_out, input_spectrum, filter_spectrum):
    wide, first, last, twist, shuffle = (jnp.asarray(t) for t in tables())
    vmem = pl.BlockSpec(memory_space=pltpu.VMEM)
    anywhere = pl.BlockSpec(memory_space=pl.ANY)
    dma = pltpu.SemaphoreType.DMA
    out_shape = (
        jax.ShapeDtypeStruct((1, CH, TIMES * COLS), BF16),
        jax.ShapeDtypeStruct((CH, TIMES * COLS // BATCHES), F32),
    )
    results = pl.pallas_call(
        kernel,
        out_shape=out_shape,
        in_specs=[anywhere] * 8,
        out_specs=(vmem, vmem),
        scratch_shapes=[
            pltpu.VMEM((1, CH, TIMES * COLS), BF16),
            pltpu.VMEM((8, 768, 256), BF16),
            pltpu.VMEM((256, 256), BF16),
            pltpu.VMEM((256, 384), BF16),
            pltpu.VMEM((2, ROWS, COLS), F32),
            pltpu.VMEM((2, COLS, COLS), BF16),
            pltpu.VMEM((2, CH, ROWS, COLS), F32),
            pltpu.VMEM((2, CH, ROWS, COLS), F32),
            pltpu.VMEM((4, (CH + 1) * TIMES, 128), F32),
            pltpu.VMEM((CH, SHARDS * TIMES, COLS), BF16),
            pltpu.VMEM((2, 4, HALF * ROWS, 768), BF16),
            pltpu.VMEM((2, 4, HALF * ROWS, 256), F32),
            pltpu.VMEM((2, 4, HALF * ROWS, 768), BF16),
            pltpu.VMEM((2, 4, HALF * ROWS, 256), F32),
            pltpu.VMEM((HALF, 384, COLS), BF16),
            pltpu.VMEM((SHARDS, CH, TIMES, COLS), F32),
            pltpu.VMEM((CH, 7, 9, 16, 128), BF16),
            pltpu.VMEM((2, BATCHES, 2, ROWS, COLS), F32),
            pltpu.VMEM((2, 3, 2, 17, 16, 128), BF16),
            pltpu.VMEM((2, 3, 2, 17, 16, 128), BF16),
            pltpu.VMEM((4, ROWS, 768), BF16),
            pltpu.VMEM((4, ROWS, 256), F32),
            pltpu.VMEM((384, COLS), BF16),
            pltpu.VMEM((SHARDS, 2, TIMES, COLS), F32),
            pltpu.VMEM((2, 7, 9, 16, 128), BF16),
            pltpu.VMEM((CH * 8, COLS), F32),
            pltpu.VMEM((CH, 7, 9, 16, 128), BF16),
            pltpu.VMEM((2, 7, 9, 16, 128), BF16),
            dma((9,)),
            dma((CH, 7)), dma((CH, 7)),
            dma((CH, 7)), dma((CH, 7)),
            dma((2, 3)), dma((2, 3)),
            dma((2, 7)), dma((2, 7)),
            dma((2, 3)), dma((2, 3)),
        ],
        compiler_params=pltpu.CompilerParams(
            collective_id=0, has_side_effects=True, vmem_limit_bytes=56 * 1024 * 1024
        ),
    )(grad_out, input_spectrum, filter_spectrum, wide, first, last, twist, shuffle)
    return pl.pallas_call(
        hand_on,
        out_shape=out_shape,
        in_specs=[anywhere] * 2,
        out_specs=(anywhere,) * 2,
        scratch_shapes=[
            pltpu.VMEM((1, CH, TIMES * COLS), BF16),
            pltpu.VMEM((CH, TIMES * COLS // BATCHES), F32),
            dma((4,)),
        ],
        compiler_params=pltpu.CompilerParams(vmem_limit_bytes=56 * 1024 * 1024),
    )(*results)


def solution(mesh):
    in_specs = (
        P("dp", "chan", "seq"),
        P("dp", None, "chan", "seq", None),
        P(None, "chan", "seq", None),
    )
    out_specs = (P("dp", "chan", "seq"), P("chan", ("seq", "dp")))
    return jax.shard_map(
        on_device, mesh=mesh, in_specs=in_specs, out_specs=out_specs, check_vma=False
    )
```
